32 devices in a mesh: gx: 4 (over z), gy: 2 (over y), gz: 4 (over x, core).
Axes of the slice: x: 2, y: 2, z: 4, core: 2. Of those that a mesh axis runs over, the one named last changes fastest.
Arguments:
- stress_trial: float32 [6, 786432], P(None, ('gx', 'gy', 'gz')), may hold values from -6 to 6
- mean_stress: float32 [786432], P(('gx', 'gy', 'gz')), may hold values from 0.3 to 2
- consolidation: float32 [786432], P(('gx', 'gy', 'gz')), may hold values from 2.5 to 4
- point_velocity: float32 [3, 786432], P(None, ('gx', 'gy', 'gz')), may hold values from -6 to 6
- point_weight: float32 [786432], P(('gx', 'gy', 'gz')), may hold values from 0.5 to 1
- point_cell: int32 [786432], P(('gx', 'gy', 'gz')), may hold values from 0 to 16383
- yield_flag: int32 [786432], P(('gx', 'gy', 'gz')), may hold values 0 or 1
- point_count: int32 [4, 2, 4], P('gx', 'gy', 'gz'), may hold values from 12288 to 24576, as said below
- porosity: float32 [64, 32, 256], P('gz', 'gx', 'gy'), may hold values from 0.2 to 0.5
- permeability: float32 [64, 32, 256], P('gz', 'gx', 'gy'), may hold values from 1 to 10
Outputs:
- velocity: float32 [3, 64, 32, 256], P(None, 'gz', 'gx', 'gy')
- pressure: float32 [64, 32, 256], P('gz', 'gx', 'gy')
The draws below stay inside these ranges and needn't reach their ends.
Inputs may be any that keep to these rules, and one draw needn't show every extreme that they name: `point_cell`: a cell index within the brick, levels slowest, then rows, then columns. `point_count`: slots below the count hold live points, the rest are empty; some brick is full.
All inputs are finite; a program needn't handle non-finite values. No bound on the sum of `yield_flag` on one device may be relied on, other than what follows from the above.
Results may differ from the reference program's by a relative error of at most 0.0003.
Values sent between devices are 32-bit elements; how exact they have to be, the bound alone decides.
No kernel may reach another device: no remote copies, remote signals or barrier semaphores. Data moves between devices by JAX's collectives and lax.ppermute only.
A program may use at most 128 MiB of HBM per device.

```python
import math
import jax
import jax.numpy as jnp

CX = 8
CY = 128
CZ = 16
NP_DEV = 24576
NX = 32
NY = 256
NZ = 64
NP = 786432
N_GX = 4
N_GY = 2
N_GZ = 4


def draw_point_count(key, part):
    bricks = N_GX * N_GY * N_GZ
    key_counts = jax.random.fold_in(key, 11)
    key_full = jax.random.fold_in(key, 23)
    counts = jax.random.randint(key_counts, (bricks,), NP_DEV // 2, NP_DEV + 1)
    chosen = jax.random.randint(key_full, (), 0, bricks)
    counts = jnp.where(jnp.arange(bricks) == chosen, NP_DEV, counts)
    return counts.reshape(N_GX, N_GY, N_GZ).astype(jnp.int32)


def place_ends(values, stream_key, low, top_value):
    longest = values.shape.index(max(values.shape))
    spots = []
    for shift in (0, 1):
        where = [jax.random.randint(jax.random.fold_in(stream_key, axis), (), 0, length) for axis, length in enumerate(values.shape)]
        where[longest] = (where[longest] + shift) % values.shape[longest]
        spots.append(tuple(where))
    return values.at[spots[0]].set(low).at[spots[1]].set(top_value)


def steps_of(own_key, extent, split, smallest, largest):
    gain, own = 1.0, jax.random.fold_in(own_key, 6)
    for position, parts in split:
        draws = jnp.exp(jax.random.uniform(jax.random.fold_in(own, position), (parts,), jnp.float32, smallest / len(split), largest / len(split)))
        gain = gain * jnp.repeat(draws, extent[position] // parts).reshape([-1 if axis == position else 1 for axis in range(len(extent))])
    return gain


def noise(stream_key, dims, scale, reach, split=(), kind=jnp.bfloat16):
    values = jax.random.normal(stream_key, dims, jnp.float32) * scale
    if len(split) > 0:
        values = steps_of(stream_key, dims, split, -0.22, 0.18) * values
    return jnp.clip(values, min=-reach, max=reach).astype(kind)


def setup_inputs(seed: int = 0) -> dict:
    key_list = jax.random.split(jax.random.key(seed), 11)
    return {
        "stress_trial": noise(key_list[0], (6, NP), 1.0, 6.0, ((1, 32),), jnp.float32),
        "mean_stress": jnp.clip(jnp.exp(math.log(2.0) - 1.89712 * jax.random.uniform(key_list[1], (NP,), jnp.float32) ** steps_of(key_list[1], (NP,), ((0, 32),), -0.2, 0.2)), 0.3, 2.0),
        "consolidation": jnp.clip(2.5 + 1.5 * jax.random.uniform(key_list[2], (NP,), jnp.float32) ** steps_of(key_list[2], (NP,), ((0, 32),), -0.2, 0.2), 2.5, 4.0),
        "point_velocity": noise(key_list[3], (3, NP), 1.0, 6.0, ((1, 32),), jnp.float32),
        "point_weight": jnp.clip(0.5 + 0.5 * jax.random.uniform(key_list[4], (NP,), jnp.float32) ** steps_of(key_list[4], (NP,), ((0, 32),), -0.2, 0.2), 0.5, 1.0),
        "point_cell": place_ends(jax.random.randint(key_list[5], (NP,), 0, CZ * CX * CY), jax.random.fold_in(key_list[5], 1), 0, (CZ * CX * CY) - 1).astype(jnp.int32),
        "yield_flag": place_ends((jax.random.randint(key_list[6], (NP,), 0, 2) < 1).astype(jnp.int32), jax.random.fold_in(key_list[6], 1), 0, 1),
        "point_count": draw_point_count(jax.random.fold_in(key_list[10], 71), 0),
        "porosity": jnp.clip(0.2 + 0.3 * jax.random.uniform(key_list[8], (NZ, NX, NY), jnp.float32) ** steps_of(key_list[8], (NZ, NX, NY), ((0, 4), (1, 4), (2, 2)), -0.2, 0.2), 0.2, 0.5),
        "permeability": jnp.clip(jnp.exp(math.log(10.0) - 2.3025851 * jax.random.uniform(key_list[9], (NZ, NX, NY), jnp.float32) ** steps_of(key_list[9], (NZ, NX, NY), ((0, 4), (1, 4), (2, 2)), -0.2, 0.2)), 1.0, 10.0),
    }


time_step = 0.25
storage_rate = 0.002
source_rate = 0.003
critical_slope = 1.2
mass_floor = 0.5
shear_floor = 1.0

def along_x(padded):
    return (padded[..., 1:-1, 2:, 1:-1] - padded[..., 1:-1, :-2, 1:-1]) * 0.5

def along_y(padded):
    return (padded[..., 1:-1, 1:-1, 2:] - padded[..., 1:-1, 1:-1, :-2]) * 0.5

def along_z(padded):
    return (padded[..., 2:, 1:-1, 1:-1] - padded[..., :-2, 1:-1, 1:-1]) * 0.5

def harmonic(former, latter):
    return 2.0 * former * latter / (former + latter)

def returned_stress(stress_trial, mean_stress, consolidation, yield_flag):
    sq_normal = stress_trial[0] * stress_trial[0] + stress_trial[1] * stress_trial[1] + stress_trial[2] * stress_trial[2]
    sq_shear = stress_trial[3] * stress_trial[3] + stress_trial[4] * stress_trial[4] + stress_trial[5] * stress_trial[5]
    shear_size = jnp.sqrt(1.5 * (sq_normal + 2.0 * sq_shear))
    yield_size = critical_slope * jnp.sqrt(mean_stress * (consolidation - mean_stress))
    factor = jnp.where(yield_flag == 1, yield_size / jnp.maximum(shear_size, shear_floor), 1.0)
    isotropic = jnp.array([1.0, 1.0, 1.0, 0.0, 0.0, 0.0], dtype=jnp.float32)[:, None]
    return stress_trial * factor - isotropic * mean_stress

def point_sums(stress, point_velocity, weight, cell_index, segments):
    stacked = jnp.concatenate([stress * weight, point_velocity * weight, weight[None]], axis=0)
    return jax.vmap(lambda component: jax.ops.segment_sum(component, cell_index, num_segments=segments))(stacked)

def brick_velocity(cell_sums, padded):
    floored = jnp.maximum(cell_sums[9], mass_floor)
    force_x = along_x(padded[0]) + along_y(padded[3]) + along_z(padded[5])
    force_y = along_x(padded[3]) + along_y(padded[1]) + along_z(padded[4])
    force_z = along_x(padded[5]) + along_y(padded[4]) + along_z(padded[2])
    return jnp.stack([(cell_sums[6] + time_step * force_x) / floored, (cell_sums[7] + time_step * force_y) / floored, (cell_sums[8] + time_step * force_z) / floored])

def divergence(padded_velocity):
    return along_x(padded_velocity[0]) + along_y(padded_velocity[1]) + along_z(padded_velocity[2])

def band_terms(porosity, permeability, level_below, level_above, at_top, dilation):
    up_face = harmonic(permeability, level_above)
    down_face = harmonic(level_below, permeability)
    top_face = jnp.where(at_top, permeability, up_face)
    lower_band = -time_step * down_face
    upper_band = -time_step * up_face
    main_band = storage_rate * porosity + time_step * (down_face + top_face)
    right_side = -source_rate * (1.0 - porosity) * dilation
    return (lower_band, main_band, upper_band, right_side)

def earlier(values, stride, filler):
    head = jnp.full((stride,) + values.shape[1:], filler, values.dtype)
    return jnp.concatenate([head, values[:-stride]], axis=0)

def later(values, stride, filler):
    tail = jnp.full((stride,) + values.shape[1:], filler, values.dtype)
    return jnp.concatenate([values[stride:], tail], axis=0)

def cyclic_solve(lower_band, main_band, upper_band, right_side):
    length = main_band.shape[0]
    for bit in range((length - 1).bit_length()):
        stride = 1 << bit
        back_weight = -lower_band / earlier(main_band, stride, 1.0)
        ahead_weight = -upper_band / later(main_band, stride, 1.0)
        new_lower = back_weight * earlier(lower_band, stride, 0.0)
        new_upper = ahead_weight * later(upper_band, stride, 0.0)
        new_main = main_band + back_weight * earlier(upper_band, stride, 0.0) + ahead_weight * later(lower_band, stride, 0.0)
        new_right = right_side + back_weight * earlier(right_side, stride, 0.0) + ahead_weight * later(right_side, stride, 0.0)
        lower_band, main_band, upper_band, right_side = (new_lower, new_main, new_upper, new_right)
    return right_side / main_band

def reference(stress_trial, mean_stress, consolidation, point_velocity, point_weight, point_cell, yield_flag, point_count, porosity, permeability):
    point_total = mean_stress.shape[0]
    slot_index = jnp.arange(point_total, dtype=jnp.int32)
    device = slot_index // NP_DEV
    is_live = slot_index % NP_DEV < point_count.reshape(-1)[device]
    row_index = device // (N_GY * N_GZ)
    column_index = device // N_GZ % N_GY
    layer_index = device % N_GZ
    local_z = point_cell // (CX * CY)
    local_x = point_cell // CY % CX
    local_y = point_cell % CY
    cell_index = ((layer_index * CZ + local_z) * NX + row_index * CX + local_x) * NY + column_index * CY + local_y
    weight = jnp.where(is_live, point_weight, 0.0)
    stress = returned_stress(stress_trial, mean_stress, consolidation, yield_flag)
    cell_sums = point_sums(stress, point_velocity, weight, cell_index, NZ * NX * NY).reshape(10, NZ, NX, NY)
    padded = jnp.pad(cell_sums[:6], ((0, 0), (1, 1), (1, 1), (1, 1)))
    velocity = brick_velocity(cell_sums, padded)
    dilation = divergence(jnp.pad(velocity, ((0, 0), (1, 1), (1, 1), (1, 1))))
    zero_level = jnp.zeros((1, NX, NY), permeability.dtype)
    level_above = jnp.concatenate([permeability[1:], zero_level], axis=0)
    level_below = jnp.concatenate([zero_level, permeability[:-1]], axis=0)
    at_top = (jnp.arange(NZ, dtype=jnp.int32) == NZ - 1)[:, None, None]
    band_set = band_terms(porosity, permeability, level_below, level_above, at_top, dilation)
    solved = cyclic_solve(band_set[0].reshape(NZ, NX * NY), band_set[1].reshape(NZ, NX * NY), band_set[2].reshape(NZ, NX * NY), band_set[3].reshape(NZ, NX * NY))
    pressure = solved.reshape(NZ, NX, NY)
    padded_pressure = jnp.pad(pressure, 1)
    gradient = jnp.stack([along_x(padded_pressure), along_y(padded_pressure), along_z(padded_pressure)])
    return (velocity - time_step * gradient, pressure)
```

```python
import functools

import jax
import jax.numpy as jnp
from jax import lax
from jax.experimental import pallas as pl
from jax.experimental.pallas import tpu as pltpu
from jax.sharding import PartitionSpec as P

bf = jnp.bfloat16
f32 = jnp.float32

time_step = 0.25
storage_rate = 0.002
source_rate = 0.003
critical_slope = 1.2
mass_floor = 0.5
shear_floor = 1.0


def padded_2(cells, sides, width):
    for axis, dim in sides:
        count = lax.axis_size(axis)
        ends = count - 1
        head = lax.slice_in_dim(cells, 0, width, axis=dim)
        tail = lax.slice_in_dim(cells, cells.shape[dim] - width, cells.shape[dim], axis=dim)
        cells = jnp.concatenate(
            [
                lax.ppermute(tail, axis, [(i, (i + 1) % count) for i in range(ends)]),
                cells,
                lax.ppermute(head, axis, [((i + 1) % count, i) for i in range(ends)]),
            ],
            axis=dim,
        )
    return cells


def along_x(padded):
    return (padded[..., 1:-1, 2:, 1:-1] - padded[..., 1:-1, :-2, 1:-1]) * 0.5


def along_y(padded):
    return (padded[..., 1:-1, 1:-1, 2:] - padded[..., 1:-1, 1:-1, :-2]) * 0.5


def along_z(padded):
    return (padded[..., 2:, 1:-1, 1:-1] - padded[..., :-2, 1:-1, 1:-1]) * 0.5


def harmonic(former, latter):
    return 2.0 * former * latter / (former + latter)


def row_stress(st, mean, cons, flag):
    r = lax.broadcasted_iota(jnp.int32, st.shape, 0)
    w = jnp.where(r < 3, 1.5, 3.0)
    size = jnp.sqrt(jnp.sum(st*st*w, axis=0, keepdims=True))
    ysz = 1.2*jnp.sqrt(mean*(cons-mean))
    factor = jnp.where(flag == 1, ysz/jnp.maximum(size,1.0), 1.0)
    return st*factor - jnp.where(r<3, mean, 0.0)

def scatter_kernel(kc, count, st, mean, cons, vel, wt, cell, flag, out, acc):
    step = pl.program_id(0)
    slot = step*kc + lax.broadcasted_iota(jnp.int32,(1,kc),1)
    w = jnp.where(slot < count[0], wt[...], 0.0)
    stress = row_stress(st[...], mean[...], cons[...], flag[...]) * w
    mom = vel[...]*w
    c = cell[...]
    hi = (c >> 7) & 63
    lo = ((c >> 13) << 7) | (c & 127)

    f8 = jnp.float8_e4m3fn
    def tile(row, n, t):
        return jnp.broadcast_to(row, (n,kc)).astype(t)
    hi16 = tile(hi.astype(f32),16,bf); lo16 = tile(lo.astype(f32),16,bf)
    one, zero = jnp.array(1,bf), jnp.array(0,bf)
    base = lax.broadcasted_iota(jnp.int32,(16,kc),0)
    def eqs(idx16, n):
        return [(base + b*16).astype(f32).astype(bf) == idx16 for b in range(n//16)]
    hm = eqs(hi16, 64)
    lt = jnp.concatenate([jnp.where(m,one,zero) for m in eqs(lo16, 256)], axis=0)
    lt8 = lt.astype(f8)
    rows=[stress[i:i+1] for i in range(6)]+[mom[i:i+1] for i in range(3)]+[w]
    b32 = lax.broadcasted_iota(jnp.int32,(32,kc),0)
    hmask = [b32 + 32*b == jnp.broadcast_to(hi,(32,kc)) for b in range(2)]
    pieces=[]; p8=[]
    for r in rows:
        top = r.astype(bf).astype(f32)
        t = tile(top,16,bf)
        pieces += [jnp.where(m,t,zero) for m in hm]
        t = tile((r-top)*256.0,32,f8)
        z = jnp.zeros((32,kc), f8)
        p8 += [jnp.where(m, t, z) for m in hmask]
    a = jnp.concatenate(pieces, axis=0)
    a8 = jnp.concatenate(p8, axis=0)
    prod = lax.dot_general(a, lt, (((1,),(1,)),((),())), preferred_element_type=f32)
    prod8 = lax.dot_general(a8, lt8, (((1,),(1,)),((),())), preferred_element_type=f32)
    prod = prod + prod8*(1/256.)
    @pl.when(step == 0)
    def _(): acc[...] = prod
    @pl.when(step > 0)
    def _(): acc[...] += prod
    @pl.when(step == pl.num_programs(0)-1)
    def _():
        for i in range(10):
            s = acc[i*64:i*64+64,:]
            out[i,0:64,:] = s[:,:128]
            out[i,64:128,:] = s[:,128:]

def scatter(st, mean, cons, vel, wt, cell, flag, count):
    kc = 8192 if mean.shape[0] % 8192 == 0 else mean.shape[0]
    n = mean.shape[0]
    row = lambda v: v.reshape(1,n)
    spec = lambda r: pl.BlockSpec((r,kc), lambda i: (0,i))
    return pl.pallas_call(functools.partial(scatter_kernel, kc),
        grid=(n//kc,),
        in_specs=[pl.BlockSpec(memory_space=pltpu.SMEM), spec(6), spec(1), spec(1), spec(3), spec(1), spec(1), spec(1)],
        out_specs=pl.BlockSpec((10,128,128), lambda i: (0,0,0)),
        out_shape=jax.ShapeDtypeStruct((10,128,128), f32),
        scratch_shapes=[pltpu.VMEM((640,256), f32)],
        compiler_params=pltpu.CompilerParams(vmem_limit_bytes=60<<20),
        cost_estimate=pl.CostEstimate(flops=2*1280*256*n, bytes_accessed=64*n, transcendentals=0),
    )(count.reshape(1), st, row(mean), row(cons), vel, row(wt), row(cell), row(flag))


def brick_velocity(cell_sums, padded):
    floored = jnp.maximum(cell_sums[9], mass_floor)
    force_x = along_x(padded[0]) + along_y(padded[3]) + along_z(padded[5])
    force_y = along_x(padded[3]) + along_y(padded[1]) + along_z(padded[4])
    force_z = along_x(padded[5]) + along_y(padded[4]) + along_z(padded[2])
    return jnp.stack(
        [
            (cell_sums[6] + time_step * force_x) / floored,
            (cell_sums[7] + time_step * force_y) / floored,
            (cell_sums[8] + time_step * force_z) / floored,
        ]
    )


def divergence(padded_velocity):
    return along_x(padded_velocity[0]) + along_y(padded_velocity[1]) + along_z(padded_velocity[2])


def band_terms(porosity, permeability, level_below, level_above, at_top, dilation):
    up_face = harmonic(permeability, level_above)
    down_face = harmonic(level_below, permeability)
    top_face = jnp.where(at_top, permeability, up_face)
    lower_band = -time_step * down_face
    upper_band = -time_step * up_face
    main_band = storage_rate * porosity + time_step * (down_face + top_face)
    right_side = -source_rate * (1.0 - porosity) * dilation
    return (lower_band, main_band, upper_band, right_side)


def earlier(values, stride, filler):
    head = jnp.full((stride,) + values.shape[1:], filler, values.dtype)
    return jnp.concatenate([head, values[:-stride]], axis=0)


def later(values, stride, filler):
    tail = jnp.full((stride,) + values.shape[1:], filler, values.dtype)
    return jnp.concatenate([values[stride:], tail], axis=0)


def cyclic_solve(lower_band, main_band, upper_band, right_side):
    length = main_band.shape[0]
    for bit in range((length - 1).bit_length()):
        stride = 1 << bit
        back_weight = -lower_band / earlier(main_band, stride, 1.0)
        ahead_weight = -upper_band / later(main_band, stride, 1.0)
        new_lower = back_weight * earlier(lower_band, stride, 0.0)
        new_upper = ahead_weight * later(upper_band, stride, 0.0)
        new_main = (
            main_band
            + back_weight * earlier(upper_band, stride, 0.0)
            + ahead_weight * later(lower_band, stride, 0.0)
        )
        new_right = (
            right_side
            + back_weight * earlier(right_side, stride, 0.0)
            + ahead_weight * later(right_side, stride, 0.0)
        )
        lower_band, main_band, upper_band, right_side = (new_lower, new_main, new_upper, new_right)
    return right_side / main_band


def brick_bands(porosity, permeability, padded, dilation, levels, layer_count):
    level_index = lax.axis_index("gz") * levels + jnp.arange(levels, dtype=jnp.int32)
    at_top = (level_index == levels * layer_count - 1)[:, None, None]
    return band_terms(
        porosity,
        permeability,
        padded[6, :-2, 1:-1, 1:-1],
        padded[6, 2:, 1:-1, 1:-1],
        at_top,
        dilation,
    )


def partitioned_solve(band_set, levels, extent, breadth):
    lower, main, upper, right = [band.reshape(levels, -1) for band in band_set]
    columns = main.shape[1]
    zero_row = jnp.zeros((1, columns), jnp.float32)
    inner_lower = jnp.concatenate([zero_row, lower[2:-1]], axis=0)
    inner_upper = jnp.concatenate([upper[1:-2], zero_row], axis=0)
    inner_zeros = jnp.zeros((levels - 3, columns), jnp.float32)
    side_first = jnp.concatenate([-lower[1:2], inner_zeros], axis=0)
    side_last = jnp.concatenate([inner_zeros, -upper[levels - 2 : levels - 1]], axis=0)

    def tripled(values):
        return jnp.concatenate([values, values, values], axis=1)

    inner = cyclic_solve(
        tripled(inner_lower),
        tripled(main[1:-1]),
        tripled(inner_upper),
        jnp.concatenate([right[1:-1], side_first, side_last], axis=1),
    )
    base = inner[:, :columns]
    from_first = inner[:, columns : 2 * columns]
    from_last = inner[:, 2 * columns :]
    first_row = jnp.stack(
        [
            lower[0],
            main[0] + upper[0] * from_first[0],
            upper[0] * from_last[0],
            right[0] - upper[0] * base[0],
        ]
    )
    last_row = jnp.stack(
        [
            lower[-1] * from_first[-1],
            main[-1] + lower[-1] * from_last[-1],
            upper[-1],
            right[-1] - lower[-1] * base[-1],
        ]
    )
    reduced = jnp.stack([first_row, last_row])
    gathered = lax.all_gather(reduced, "gz", axis=0, tiled=True)
    coupled = cyclic_solve(gathered[:, 0], gathered[:, 1], gathered[:, 2], gathered[:, 3])
    own_pair = lax.dynamic_slice_in_dim(coupled, 2 * lax.axis_index("gz"), 2, 0)
    interior = base + from_first * own_pair[0][None] + from_last * own_pair[1][None]
    whole = jnp.concatenate([own_pair[0:1], interior, own_pair[1:2]], axis=0)
    return whole.reshape(levels, extent, breadth)


def shards(
    stress_trial,
    mean_stress,
    consolidation,
    point_velocity,
    point_weight,
    point_cell,
    yield_flag,
    point_count,
    porosity,
    permeability,
):
    levels, extent, breadth = porosity.shape
    cell_sums = scatter(
        stress_trial,
        mean_stress,
        consolidation,
        point_velocity,
        point_weight,
        point_cell,
        yield_flag,
        point_count,
    ).reshape(10, levels, extent, breadth)
    outgoing = jnp.concatenate([cell_sums[:6], permeability[None]], axis=0)
    padded = padded_2(outgoing, (("gx", 2), ("gy", 3), ("gz", 1)), 1)
    velocity = brick_velocity(cell_sums, padded)
    padded_velocity = padded_2(velocity, (("gx", 2), ("gy", 3), ("gz", 1)), 1)
    dilation = divergence(padded_velocity)
    layer_count = lax.axis_size("gz")
    band_set = brick_bands(porosity, permeability, padded, dilation, levels, layer_count)
    pressure = partitioned_solve(band_set, levels, extent, breadth)
    padded_pressure = padded_2(pressure, (("gx", 1), ("gy", 2), ("gz", 0)), 1)
    gradient = jnp.stack(
        [along_x(padded_pressure), along_y(padded_pressure), along_z(padded_pressure)]
    )
    return (velocity - time_step * gradient, pressure)


def solution(mesh):
    placed = (
        P(None, ("gx", "gy", "gz")),
        P(("gx", "gy", "gz")),
        P(("gx", "gy", "gz")),
        P(None, ("gx", "gy", "gz")),
        P(("gx", "gy", "gz")),
        P(("gx", "gy", "gz")),
        P(("gx", "gy", "gz")),
        P("gx", "gy", "gz"),
        P("gz", "gx", "gy"),
        P("gz", "gx", "gy"),
    )
    return jax.shard_map(
        shards,
        mesh=mesh,
        in_specs=placed,
        out_specs=(P(None, "gz", "gx", "gy"), P("gz", "gx", "gy")),
        check_vma=False,
    )
```

```python
import functools

import jax
import jax.numpy as jnp
from jax import lax
from jax.experimental import pallas as pl
from jax.experimental.pallas import tpu as pltpu
from jax.sharding import PartitionSpec as P

bf = jnp.bfloat16
f8 = jnp.float8_e4m3fn
f32 = jnp.float32
i32 = jnp.int32

LEVELS, ROWS, COLS = 16, 8, 128
CELLS = LEVELS * ROWS

ZX, YZ, ZZ, XX, YY, XY, MX, MY, MZ, MASS, POR, PERM = range(12)
FIELDS = 12
STRESS_ORDER = (5, 4, 2, 0, 1, 3)

X_ROWS = (
    (ZX, 0), (ZX, 1), (YZ, 0), (ZZ, 0), (PERM, 0),
    (XX, 0), (XX, 1), (XX, 2), (XY, 0), (XY, 1), (YY, 0),
    (MX, 0), (MX, 1), (MY, 0), (MZ, 0), (MASS, 0), (MASS, 1), (POR, 0),
)
X_LEVEL = 5
Y_DEPTH = {ZX: 1, YZ: 2, ZZ: 1, XX: 1, YY: 3, XY: 2, MX: 1, MY: 2, MZ: 1, MASS: 2, POR: 1, PERM: 1}
Y_PLACE = {}
_at = 0
for _f in range(FIELDS):
    Y_PLACE[_f] = _at + Y_DEPTH[_f]
    _at += 2 * Y_DEPTH[_f]
HALF = 64
Z_FIELDS = (ZX, YZ, ZZ, PERM)
Z_X = 8 * len(Z_FIELDS)
Z_Y = Z_X + 16
Z_ROWS = Z_Y + 8
REDUCED = 10
RED_X = 8 * REDUCED
RED_Y = RED_X + 24
RED_ROWS = RED_Y + 8


def tile_iota(dim):
    return lax.broadcasted_iota(i32, (ROWS, COLS), dim)


def turn(tile, shift, axis):
    shift %= tile.shape[axis]
    return tile if shift == 0 else pltpu.roll(tile, shift, axis)


def row_stress(trial, mean, cons, flag):
    part = lax.broadcasted_iota(i32, trial.shape, 0)
    size = jnp.sqrt(
        jnp.sum(trial * trial * jnp.where(part < 3, 1.5, 3.0), axis=0, keepdims=True)
    )
    yield_size = 1.2 * jnp.sqrt(mean * (cons - mean))
    factor = jnp.where(flag == 1, yield_size / jnp.maximum(size, 1.0), 1.0)
    return trial * factor - jnp.where(part < 3, mean, 0.0)


def scatter_kernel(
    chunk, count, trial, mean, cons, vel, wt, cell, flag, por, perm, out, low, high, acc
):
    step = pl.program_id(0)
    slot = step * chunk + lax.broadcasted_iota(i32, (1, chunk), 1)
    weight = jnp.where(slot < count[0], wt[...], 0.0)
    stress = row_stress(trial[...], mean[...], cons[...], flag[...]) * weight
    momentum = vel[...] * weight
    place = cell[...]
    hi = (place >> 7) & 63
    lo = ((place >> 13) << 7) | (place & 127)

    def spread(row, count, kind):
        return jnp.broadcast_to(row, (count, chunk)).astype(kind)

    one, zero = jnp.array(1, bf), jnp.array(0, bf)
    base = lax.broadcasted_iota(i32, (16, chunk), 0)

    def equal(index, count):
        index = spread(index.astype(f32), 16, bf)
        return [(base + b * 16).astype(f32).astype(bf) == index for b in range(count // 16)]

    hi_mask = equal(hi, 64)
    right = jnp.concatenate([jnp.where(m, one, zero) for m in equal(lo, 256)], axis=0)
    base32 = lax.broadcasted_iota(i32, (32, chunk), 0)
    hi_mask8 = [base32 + 32 * b == jnp.broadcast_to(hi, (32, chunk)) for b in range(2)]
    zero8 = jnp.zeros((32, chunk), f8)
    rows = [stress[i : i + 1] for i in STRESS_ORDER]
    rows += [momentum[i : i + 1] for i in range(3)] + [weight]
    left, left8 = [], []
    for row in rows:
        top = row.astype(bf).astype(f32)
        part = spread(top, 16, bf)
        left += [jnp.where(m, part, zero) for m in hi_mask]
        part = spread((row - top) * 256.0, 32, f8)
        left8 += [jnp.where(m, part, zero8) for m in hi_mask8]
    left = jnp.concatenate(left, axis=0)
    left8 = jnp.concatenate(left8, axis=0)
    dims = (((1,), (1,)), ((), ()))
    prod = lax.dot_general(left, right, dims, preferred_element_type=f32)
    prod8 = lax.dot_general(left8, right.astype(f8), dims, preferred_element_type=f32)
    prod = prod + prod8 * (1 / 256.0)

    @pl.when(step == 0)
    def _():
        acc[...] = prod

    @pl.when(step > 0)
    def _():
        acc[...] += prod

    @pl.when(step == pl.num_programs(0) - 1)
    def _():
        for i in range(10):
            out[i, 0:64, :] = acc[i * 64 : i * 64 + 64, :COLS]
            out[i, 64:128, :] = acc[i * 64 : i * 64 + 64, COLS:]
        for q, (field, depth) in enumerate(X_ROWS):
            for face, row in ((low, depth), (high, ROWS - 1 - depth)):
                rows = pl.ds(row, LEVELS, stride=ROWS)
                if field < 10:
                    face[q] = out[field, rows, :]
                else:
                    face[q] = (por if field == POR else perm)[rows, :]


def scatter(trial, mean, cons, vel, wt, cell, flag, count, por, perm):
    points = mean.shape[0]
    chunk = 8192 if points % 8192 == 0 else points
    row = lambda v: v.reshape(1, points)
    spec = lambda r: pl.BlockSpec((r, chunk), lambda i: (0, i))
    fixed = lambda *shape: pl.BlockSpec(shape, lambda i: (0,) * len(shape))
    faces = (len(X_ROWS), LEVELS, COLS)
    return pl.pallas_call(
        functools.partial(scatter_kernel, chunk),
        grid=(points // chunk,),
        in_specs=[pl.BlockSpec(memory_space=pltpu.SMEM)]
        + [spec(r) for r in (6, 1, 1, 3, 1, 1, 1)]
        + [fixed(CELLS, COLS)] * 2,
        out_specs=[fixed(10, CELLS, COLS), fixed(*faces), fixed(*faces)],
        out_shape=[
            jax.ShapeDtypeStruct((10, CELLS, COLS), f32),
            jax.ShapeDtypeStruct(faces, f32),
            jax.ShapeDtypeStruct(faces, f32),
        ],
        scratch_shapes=[pltpu.VMEM((640, 256), f32)],
        compiler_params=pltpu.CompilerParams(vmem_limit_bytes=60 << 20),
        cost_estimate=pl.CostEstimate(
            flops=2 * 960 * 256 * points, bytes_accessed=64 * points, transcendentals=0
        ),
        name="point_sums",
    )(count.reshape(1), trial, row(mean), row(cons), vel, row(wt), row(cell), row(flag), por, perm)


def y_pack_kernel(sums, por, perm, below, above, out):
    lane = lax.broadcasted_iota(i32, (CELLS, COLS), 1)
    lane16 = lax.broadcasted_iota(i32, (LEVELS, COLS), 1)
    packed = jnp.zeros((CELLS, COLS), f32)
    for field in range(FIELDS):
        at, depth = Y_PLACE[field], Y_DEPTH[field]
        own = sums[field] if field < 10 else (por if field == POR else perm)[...]
        packed = jnp.where((lane >= at - depth) & (lane < at + depth), turn(own, at, 1), packed)
    slots = [jnp.zeros((LEVELS, COLS), f32)] * ROWS
    for q, (field, deep) in enumerate(X_ROWS):
        at, depth = Y_PLACE[field] + HALF, Y_DEPTH[field]
        mask = (lane16 >= at - depth) & (lane16 < at + depth)
        for source, slot in ((above, deep), (below, ROWS - 1 - deep)):
            slots[slot] = jnp.where(mask, turn(source[q], at, 1), slots[slot])
    out[...] = jnp.where(lane < HALF, packed, jnp.concatenate(slots, axis=0))


def y_pack(sums, por, perm, below, above):
    return pl.pallas_call(
        y_pack_kernel,
        out_shape=jax.ShapeDtypeStruct((CELLS, COLS), f32),
        name="y_pack",
    )(sums, por, perm, below, above)


def y_from_above(shape):
    lane = lax.broadcasted_iota(i32, shape, 1) & (HALF - 1)
    mask = lane < 0
    for field in range(FIELDS):
        at = Y_PLACE[field]
        mask |= (lane >= at) & (lane < at + Y_DEPTH[field])
    return mask


Y_LOW, Y_HIGH, Z_LOW, Z_HIGH, X_HAS_LOW, X_HAS_HIGH, Y_HAS_LOW, Y_HAS_HIGH, Z_HAS_LOW, Z_HAS_HIGH, LAYER = range(11)


def met(where, packs, from_above, rows):
    low = packs[where[Y_LOW], rows, :] * where[Y_HAS_LOW].astype(f32)
    high = packs[where[Y_HIGH], rows, :] * where[Y_HAS_HIGH].astype(f32)
    return jnp.where(from_above, high, low)


def z_pack_kernel(where, first, last, perm_first, perm_last, below, above, packs, out):
    from_above = y_from_above((ROWS, COLS))
    lane = tile_iota(1)
    for side, (tiles, perm, level) in enumerate(
        ((first, perm_first, 0), (last, perm_last, LEVELS - 1))
    ):
        at = side * Z_ROWS
        for n in range(3):
            out[at + 8 * n : at + 8 * n + 8, :] = tiles[n]
        out[at + 24 : at + 32, :] = perm[...]
        for n, source in enumerate((below, above)):
            rows = [source[q, level : level + 1, :] for q in range(X_LEVEL)]
            rows.append(jnp.zeros((8 - X_LEVEL, COLS), f32))
            out[at + Z_X + 8 * n : at + Z_X + 8 * n + 8, :] = jnp.concatenate(rows, axis=0)
        own = met(where, packs, from_above, pl.ds(level * ROWS, ROWS))
        rim = met(where, packs, from_above, pl.ds(level, ROWS, stride=LEVELS))
        out[at + Z_Y : at + Z_Y + 8, :] = jnp.where(lane < HALF, own, rim)


def z_pack(where, sums, perm, below, above, packs):
    whole = lambda v: pl.BlockSpec(v.shape, lambda i: (0,) * v.ndim)
    block = lambda n: pl.BlockSpec((ROWS, COLS), lambda i: (n, 0))
    tiles = lambda n: pl.BlockSpec((3, ROWS, COLS), lambda i: (0, n, 0))
    rim = pl.BlockSpec((8, LEVELS, COLS), lambda i: (0, 0, 0))
    return pl.pallas_call(
        z_pack_kernel,
        grid=(1,),
        in_specs=[
            pl.BlockSpec(memory_space=pltpu.SMEM),
            tiles(0), tiles(LEVELS - 1), block(0), block(LEVELS - 1), rim, rim, whole(packs),
        ],
        out_specs=pl.BlockSpec((2 * Z_ROWS, COLS), lambda i: (0, 0)),
        out_shape=jax.ShapeDtypeStruct((2 * Z_ROWS, COLS), f32),
        name="z_pack",
    )(where, sums, sums, perm, perm, below, above, packs)


def diff_x(own, rim):
    row = tile_iota(0)
    own_up, rim_up = turn(own, -1, 0), turn(rim, -1, 0)
    own_down, rim_down = turn(own, 1, 0), turn(rim, 1, 0)
    top, bottom = row == ROWS - 1, row == 0
    return (
        jnp.where(top, rim_up, own_up) - jnp.where(bottom, rim_down, own_down),
        jnp.where(top, own_up, rim_up) - jnp.where(bottom, own_down, rim_down),
    )


def diff_y(own, rim):
    lane = tile_iota(1)
    own_up, rim_up = turn(own, -1, 1), turn(rim, -1, 1)
    own_down, rim_down = turn(own, 1, 1), turn(rim, 1, 1)
    top, bottom = lane == COLS - 1, lane == 0
    return (
        jnp.where(top, rim_up, own_up) - jnp.where(bottom, rim_down, own_down),
        jnp.where(top, own_up, rim_up) - jnp.where(bottom, own_down, rim_down),
    )


def ext_x(t):
    a0, a1 = diff_x(t[0], t[1])
    b0, b1 = diff_x(t[2], t[3])
    return [a0, a1, b0, b1]


def ext_y(t):
    a0, a2 = diff_y(t[0], t[2])
    b1, b3 = diff_y(t[1], t[3])
    return [a0, b1, a2, b3]


def rim_masks(where):
    row, lane = tile_iota(0), tile_iota(1)
    has = lambda low, high, test: jnp.where(test, where[high], where[low]) == 1
    in_x = has(X_HAS_LOW, X_HAS_HIGH, row < 4)
    in_y = has(Y_HAS_LOW, Y_HAS_HIGH, lane < HALF)
    return in_x, in_y, in_x & in_y


def local_kernel(
    where, sums, por, perm, below, above, packs, levels, vel, inner, out, rim, corner
):
    rim[...] = jnp.zeros_like(rim)
    for q, (field, deep) in enumerate(X_ROWS):
        rim[field, pl.ds(deep, LEVELS, stride=ROWS), :] = above[q]
        rim[field, pl.ds(ROWS - 1 - deep, LEVELS, stride=ROWS), :] = below[q]
    from_above = y_from_above((LEVELS, COLS))
    for slot in range(ROWS):
        rows = pl.ds(slot * LEVELS, LEVELS)
        corner[pl.ds(slot, LEVELS, stride=ROWS), :] = met(where, packs, from_above, rows)
    from_above = y_from_above((ROWS, COLS))
    in_x, in_y, in_xy = rim_masks(where)

    y_tiles = [met(where, packs, from_above, pl.ds(l * ROWS, ROWS)) for l in range(LEVELS)]

    def field_at(field, level):
        rows = pl.ds(level * ROWS, ROWS)
        at = Y_PLACE[field]
        own = sums[field, rows, :] if field < 10 else (por if field == POR else perm)[rows, :]
        return [
            own,
            rim[field, rows, :],
            turn(y_tiles[level], -at, 1),
            turn(corner[rows, :], -at - HALF, 1),
        ]

    def far_level(place, has, side):
        at = side * Z_ROWS
        has = where[has].astype(f32)
        read = lambda first, count: levels[where[place], pl.ds(at + first, count), :] * has
        lanes = read(Z_Y, 8)
        low, high = read(Z_X, 8), read(Z_X + 8, 8)
        row = tile_iota(0)
        found = {}
        for n, field in enumerate(Z_FIELDS):
            tile = jnp.zeros((ROWS, COLS), f32)
            for q, (other, deep) in enumerate(X_ROWS[:X_LEVEL]):
                if other == field:
                    tile = jnp.where(row == deep, turn(high, deep - q, 0), tile)
                    tile = jnp.where(
                        row == ROWS - 1 - deep, turn(low, ROWS - 1 - deep - q, 0), tile
                    )
            found[field] = [
                read(8 * n, 8),
                tile,
                turn(lanes, -Y_PLACE[field], 1),
                turn(lanes, -Y_PLACE[field] - HALF, 1),
            ]
        return found

    far_low = far_level(Z_LOW, Z_HAS_LOW, 1)
    far_high = far_level(Z_HIGH, Z_HAS_HIGH, 0)
    memo = {}

    def get(field, level):
        if level < 0:
            return far_low[field]
        if level >= LEVELS:
            return far_high[field]
        if (field, level) not in memo:
            memo[field, level] = field_at(field, level)
        return memo[field, level]

    def star(level):
        mass = get(MASS, level)
        inverse = [1.0 / jnp.maximum(m, 0.5) for m in mass]
        dz = lambda f: [u - d for u, d in zip(get(f, level + 1), get(f, level - 1))]
        forces = (
            (ext_x(get(XX, level)), ext_y(get(XY, level)), dz(ZX)),
            (ext_x(get(XY, level)), ext_y(get(YY, level)), dz(YZ)),
            (ext_x(get(ZX, level)), ext_y(get(YZ, level)), dz(ZZ)),
        )
        found = []
        for field, (fx, fy, fz) in zip((MX, MY, MZ), forces):
            parts = []
            for n, m in enumerate(get(field, level)):
                value = (m + 0.125 * (fx[n] + fy[n] + fz[n])) * inverse[n]
                if n > 0:
                    value = jnp.where((in_x, in_y, in_xy)[n - 1], value, 0.0)
                parts.append(value)
            found.append(parts)
        return found

    def level_perm(level):
        tiles = get(PERM, level)[:3]
        if 0 <= level < LEVELS:
            tiles = [tiles[0]] + [jnp.where(t > 0.0, t, 1.0) for t in tiles[1:]]
        return tiles

    def faces(level):
        pairs = zip(level_perm(level), level_perm(level + 1))
        return [0.5 * a * b / (a + b) for a, b in pairs]

    zero3 = [jnp.zeros((ROWS, COLS), f32)] * 3
    stars = {0: star(0)}
    first_star = stars[0][2]
    down = faces(-1)
    state = None
    kept = []
    first_terms = last_terms = None
    for level in range(LEVELS):
        if level + 1 < LEVELS:
            stars[level + 1] = star(level + 1)
        vx, vy, vz = stars[level]
        for n, part in enumerate((vx, vy, vz)):
            vel[n, pl.ds(level * ROWS, ROWS), :] = part[0]
        z_up = stars[level + 1][2] if level + 1 < LEVELS else zero3
        z_down = stars[level - 1][2] if level > 0 else zero3
        stars.pop(level - 2, None)
        for key in [k for k in memo if k[1] < level - 1]:
            del memo[key]
        dx, dy = ext_x(vx), ext_y(vy)
        porosity = get(POR, level)[:3]
        up = faces(level)
        open_top = where[Z_HAS_HIGH] == 0
        k_own = level_perm(level)
        now = []
        for n in range(3):
            source = -0.0015 * (1.0 - porosity[n])
            right = source * (dx[n] + dy[n] + (z_up[n] - z_down[n]))
            top = up[n]
            if level == LEVELS - 1:
                top = jnp.where(open_top, 0.25 * k_own[n], top)
            main = 0.002 * porosity[n] + (down[n] + top)
            now.append((-down[n], main, -up[n], right, source))
        down = up
        if level == 0:
            first_terms = now
        elif level == LEVELS - 1:
            last_terms = now
        elif level == 1:
            kept.append([(lo, 1.0 / mid, hi, r) for lo, mid, hi, r, _ in now])
        else:
            rows = []
            for (lo, mid, hi, r, _), (f, inv, u, pr) in zip(now, kept[-1]):
                w = lo * inv
                rows.append((-w * f, 1.0 / (mid - w * u), hi, r - w * pr))
            kept.append(rows)
    after = None
    for n_row in range(len(kept) - 1, -1, -1):
        rows = []
        for t in range(3):
            f, inv, u, r = kept[n_row][t]
            if after is None:
                rows.append((r * inv, -f * inv, -u * inv))
            else:
                b2, f2, g2 = after[t]
                rows.append(((r - u * b2) * inv, -(f + u * f2) * inv, -u * g2 * inv))
            for m in range(3):
                inner[t, m, n_row] = rows[t][m]
        if after is None:
            last_inner = rows
        after = rows
    first_inner = after
    values = []
    for t in range(3):
        lo, mid, hi, r, source = first_terms[t]
        b, f, g = first_inner[t]
        inv = 1.0 / (mid + hi * f)
        mine = [lo * inv, hi * g * inv, (r - hi * b) * inv, -source * inv]
        lo, mid, hi, r, source = last_terms[t]
        b, f, g = last_inner[t]
        inv = 1.0 / (mid + lo * g)
        mine += [lo * f * inv, hi * inv, (r - lo * b) * inv, source * inv]
        mine += [first_star[t], stars[LEVELS - 1][2][t]]
        values.append(mine)
    row, lane = tile_iota(0), tile_iota(1)
    x_parts = [jnp.zeros((ROWS, COLS), f32)] * 3
    y_part = jnp.zeros((ROWS, COLS), f32)
    for q in range(REDUCED):
        out[8 * q : 8 * q + 8, :] = values[0][q]
        at = 2 * q % 8
        x_parts[q // 4] = jnp.where(
            (row == at) | (row == at + 1), turn(values[1][q], at + 1, 0), x_parts[q // 4]
        )
        y_part = jnp.where(
            (lane == 2 * q) | (lane == 2 * q + 1), turn(values[2][q], 2 * q + 1, 1), y_part
        )
    for n in range(3):
        out[RED_X + 8 * n : RED_X + 8 * n + 8, :] = x_parts[n]
    out[RED_Y : RED_Y + 8, :] = y_part


def local_solve(where, sums, por, perm, below, above, packs, levels):
    smem = pl.BlockSpec(memory_space=pltpu.SMEM)
    vmem = pl.BlockSpec(memory_space=pltpu.VMEM)
    return pl.pallas_call(
        local_kernel,
        in_specs=[smem] + [vmem] * 7,
        out_shape=[
            jax.ShapeDtypeStruct((3, CELLS, COLS), f32),
            jax.ShapeDtypeStruct((3, 3, LEVELS - 2, ROWS, COLS), f32),
            jax.ShapeDtypeStruct((RED_ROWS, COLS), f32),
        ],
        scratch_shapes=[pltpu.VMEM((FIELDS, CELLS, COLS), f32), pltpu.VMEM((CELLS, COLS), f32)],
        compiler_params=pltpu.CompilerParams(vmem_limit_bytes=32 << 20),
        name="local_solve",
    )(where, sums, por, perm, below, above, packs, levels)


def final_kernel(layers, where, vel, inner, reduced, out, pressure):
    me = where[LAYER]

    def value(k, q):
        own = reduced[k, 8 * q : 8 * q + 8, :]
        at = RED_X + 8 * (q // 4)
        x = turn(reduced[k, at : at + 8, :], -(2 * q % 8 + 1), 0)
        y = turn(reduced[k, RED_Y : RED_Y + 8, :], -(2 * q + 1), 1)
        return [own, x, y]

    rows = []
    for k in range(layers):
        a = [value(k, q) for q in range(REDUCED)]
        rf, rl = a[2], a[6]
        if k > 0:
            below = value(k - 1, 9)
            rf = [r + c * v for r, c, v in zip(rf, a[3], below)]
        if k + 1 < layers:
            above = value(k + 1, 8)
            rl = [r + c * v for r, c, v in zip(rl, a[7], above)]
        rows.append((a[0], a[1], rf))
        rows.append((a[4], a[5], rl))
    done = []
    for n, (lo, hi, r) in enumerate(rows):
        if n == 0:
            done.append((hi, r))
            continue
        hs, rs = done[-1]
        inv = [1.0 / (1.0 - l * h) for l, h in zip(lo, hs)]
        done.append(
            (
                [h * i for h, i in zip(hi, inv)],
                [(a - l * b) * i for a, l, b, i in zip(r, lo, rs, inv)],
            )
        )
    ends = [None] * len(rows)
    ends[-1] = done[-1][1]
    for n in range(len(rows) - 2, -1, -1):
        hs, rs = done[n]
        ends[n] = [r - h * e for r, h, e in zip(rs, hs, ends[n + 1])]

    def pick(offset):
        chosen = [jnp.zeros((ROWS, COLS), f32)] * 3
        for k in range(layers):
            n = 2 * k + offset
            if 0 <= n < len(rows):
                chosen = [jnp.where(me == k, e, c) for e, c in zip(ends[n], chosen)]
        return chosen

    first, last = pick(0), pick(1)
    under, over = pick(-1)[0], pick(2)[0]
    in_x, in_y, _ = rim_masks(where)

    def press(level):
        if level < 0:
            return [under]
        if level >= LEVELS:
            return [over]
        if level == 0:
            parts = first
        elif level == LEVELS - 1:
            parts = last
        else:
            parts = [
                inner[t, 0, level - 1]
                + inner[t, 1, level - 1] * first[t]
                + inner[t, 2, level - 1] * last[t]
                for t in range(3)
            ]
        return [parts[0], jnp.where(in_x, parts[1], 0.0), jnp.where(in_y, parts[2], 0.0)]

    before, now = press(-1), press(0)
    for level in range(LEVELS):
        after = press(level + 1)
        rows_at = pl.ds(level * ROWS, ROWS)
        pressure[rows_at, :] = now[0]
        grads = (
            diff_x(now[0], now[1])[0],
            diff_y(now[0], now[2])[0],
            after[0] - before[0],
        )
        for n in range(3):
            out[n, rows_at, :] = vel[n, rows_at, :] - 0.125 * grads[n]
        before, now = now, after


def final(where, vel, inner, reduced):
    smem = pl.BlockSpec(memory_space=pltpu.SMEM)
    vmem = pl.BlockSpec(memory_space=pltpu.VMEM)
    return pl.pallas_call(
        functools.partial(final_kernel, reduced.shape[0]),
        in_specs=[smem] + [vmem] * 3,
        out_shape=[
            jax.ShapeDtypeStruct((3, CELLS, COLS), f32),
            jax.ShapeDtypeStruct((CELLS, COLS), f32),
        ],
        compiler_params=pltpu.CompilerParams(vmem_limit_bytes=32 << 20),
        name="final",
    )(where, vel, inner, reduced)


def shift_up(block, axis):
    count = lax.axis_size(axis)
    return lax.ppermute(block, axis, [(i, i + 1) for i in range(count - 1)])


def shift_down(block, axis):
    count = lax.axis_size(axis)
    return lax.ppermute(block, axis, [(i + 1, i) for i in range(count - 1)])


def neighbours(block, axis):
    count, me = lax.axis_size(axis), lax.axis_index(axis)
    if count > 4:
        return jnp.stack([shift_up(block, axis), shift_down(block, axis)]), 0, 1
    stacked = lax.all_gather(block, axis, axis=0)
    return stacked, jnp.maximum(me - 1, 0), jnp.minimum(me + 1, count - 1)


def shards(trial, mean, cons, vel, wt, cell, flag, count, por, perm):
    por = por.reshape(CELLS, COLS)
    perm = perm.reshape(CELLS, COLS)
    sums, low, high = scatter(trial, mean, cons, vel, wt, cell, flag, count, por, perm)
    above = shift_down(low, "gx")
    below = shift_up(high, "gx")

    def ends(axis):
        me = lax.axis_index(axis)
        return [(me > 0).astype(i32), (me < lax.axis_size(axis) - 1).astype(i32)]

    has = ends("gx") + ends("gy") + ends("gz")
    packs, y_low, y_high = neighbours(y_pack(sums, por, perm, below, above), "gy")
    gz = lax.axis_index("gz")
    places = [y_low, y_high, jnp.maximum(gz - 1, 0), jnp.minimum(gz + 1, lax.axis_size("gz") - 1)]
    where = jnp.stack([jnp.asarray(v, i32) for v in places + has + [gz]])
    levels = lax.all_gather(z_pack(where, sums, perm, below, above, packs), "gz", axis=0)
    star, inner, reduced = local_solve(where, sums, por, perm, below, above, packs, levels)
    velocity, pressure = final(where, star, inner, lax.all_gather(reduced, "gz", axis=0))
    return (
        velocity.reshape(3, LEVELS, ROWS, COLS),
        pressure.reshape(LEVELS, ROWS, COLS),
    )


def solution(mesh):
    points = ("gx", "gy", "gz")
    cells = P("gz", "gx", "gy")
    placed = (
        P(None, points), P(points), P(points), P(None, points), P(points), P(points), P(points),
        P(*points), cells, cells,
    )
    return jax.shard_map(
        shards,
        mesh=mesh,
        in_specs=placed,
        out_specs=(P(None, *cells), cells),
        check_vma=False,
    )
```

```python
import functools

import jax
import jax.numpy as jnp
from jax import lax
from jax.experimental import pallas as pl
from jax.experimental.pallas import tpu as pltpu
from jax.sharding import PartitionSpec as P

bf = jnp.bfloat16
f8 = jnp.float8_e4m3fn
f32 = jnp.float32
i32 = jnp.int32

LEVELS, ROWS, COLS = 16, 8, 128
CELLS = LEVELS * ROWS

ZX, YZ, ZZ, XX, YY, XY, MX, MY, MZ, MASS, POR, PERM = range(12)
FIELDS = 12
STRESS_ORDER = (5, 4, 2, 0, 1, 3)

X_ROWS = (
    (ZX, 0), (ZX, 1), (YZ, 0), (ZZ, 0), (PERM, 0), (POR, 0),
    (XX, 0), (XX, 1), (XX, 2), (XY, 0), (XY, 1), (YY, 0),
    (MX, 0), (MX, 1), (MY, 0), (MZ, 0), (MASS, 0), (MASS, 1),
)
Y_DEPTH = {ZX: 1, YZ: 2, ZZ: 1, XX: 1, YY: 3, XY: 2, MX: 1, MY: 2, MZ: 1, MASS: 2, POR: 1, PERM: 1}
Y_PLACE = {}
_at = 0
for _f in range(FIELDS):
    Y_PLACE[_f] = _at + Y_DEPTH[_f]
    _at += 2 * Y_DEPTH[_f]
HALF = 64
FACE, MAIN, NEAR, FAR, RIGHT, SOURCE, ECHO, VELZ, STRESSZ = range(9)
WEIGHT, SHEARX, SHEARY = range(3)
NARROW, WIDE = 18, 6
MSG_X = 8 * (NARROW + WIDE)
MSG_X_WIDE = MSG_X + 8 * -(-NARROW // 4)
MSG_Y = MSG_X_WIDE + 8 * -(-WIDE // 2)
MSG_ROWS = MSG_Y + 8
LANE_WIDE = 2 * NARROW
LANE_CORNER = LANE_WIDE + 4 * WIDE


def tile_iota(dim):
    return lax.broadcasted_iota(i32, (ROWS, COLS), dim)


def turn(tile, shift, axis):
    shift %= tile.shape[axis]
    return tile if shift == 0 else pltpu.roll(tile, shift, axis)


def row_stress(trial, mean, cons, flag):
    part = lax.broadcasted_iota(i32, trial.shape, 0)
    size = jnp.sqrt(
        jnp.sum(trial * trial * jnp.where(part < 3, 1.5, 3.0), axis=0, keepdims=True)
    )
    yield_size = 1.2 * jnp.sqrt(mean * (cons - mean))
    factor = jnp.where(flag == 1, yield_size / jnp.maximum(size, 1.0), 1.0)
    return trial * factor - jnp.where(part < 3, mean, 0.0)


def scatter_kernel(
    chunk, count, trial, mean, cons, vel, wt, cell, flag, por, perm, out, low, high, acc
):
    step = pl.program_id(0)
    slot = step * chunk + lax.broadcasted_iota(i32, (1, chunk), 1)
    weight = jnp.where(slot < count[0], wt[...], 0.0)
    stress = row_stress(trial[...], mean[...], cons[...], flag[...]) * weight
    momentum = vel[...] * weight
    place = cell[...]
    hi = (place >> 7) & 63
    lo = ((place >> 13) << 7) | (place & 127)

    def spread(row, count, kind):
        return jnp.broadcast_to(row, (count, chunk)).astype(kind)

    one, zero = jnp.array(1, bf), jnp.array(0, bf)
    base = lax.broadcasted_iota(i32, (16, chunk), 0)

    def equal(index, count):
        index = spread(index.astype(f32), 16, bf)
        return [(base + b * 16).astype(f32).astype(bf) == index for b in range(count // 16)]

    hi_mask = equal(hi, 64)
    right = jnp.concatenate([jnp.where(m, one, zero) for m in equal(lo, 256)], axis=0)
    base32 = lax.broadcasted_iota(i32, (32, chunk), 0)
    hi_mask8 = [base32 + 32 * b == jnp.broadcast_to(hi, (32, chunk)) for b in range(2)]
    zero8 = jnp.zeros((32, chunk), f8)
    rows = [stress[i : i + 1] for i in STRESS_ORDER]
    rows += [momentum[i : i + 1] for i in range(3)] + [weight]
    left, left8 = [], []
    for row in rows:
        top = row.astype(bf).astype(f32)
        part = spread(top, 16, bf)
        left += [jnp.where(m, part, zero) for m in hi_mask]
        part = spread((row - top) * 256.0, 32, f8)
        left8 += [jnp.where(m, part, zero8) for m in hi_mask8]
    left = jnp.concatenate(left, axis=0)
    left8 = jnp.concatenate(left8, axis=0)
    dims = (((1,), (1,)), ((), ()))
    prod = lax.dot_general(left, right, dims, preferred_element_type=f32)
    prod8 = lax.dot_general(left8, right.astype(f8), dims, preferred_element_type=f32)
    prod = prod + prod8 * (1 / 256.0)

    @pl.when(step == 0)
    def _():
        acc[...] = prod

    @pl.when(step > 0)
    def _():
        acc[...] += prod

    @pl.when(step == pl.num_programs(0) - 1)
    def _():
        for i in range(10):
            out[i, 0:64, :] = acc[i * 64 : i * 64 + 64, :COLS]
            out[i, 64:128, :] = acc[i * 64 : i * 64 + 64, COLS:]
        for q, (field, depth) in enumerate(X_ROWS):
            for face, row in ((low, depth), (high, ROWS - 1 - depth)):
                rows = pl.ds(row, LEVELS, stride=ROWS)
                if field < 10:
                    face[q] = out[field, rows, :]
                else:
                    face[q] = (por if field == POR else perm)[rows, :]


def scatter(trial, mean, cons, vel, wt, cell, flag, count, por, perm):
    points = mean.shape[0]
    chunk = 8192 if points % 8192 == 0 else points
    row = lambda v: v.reshape(1, points)
    spec = lambda r: pl.BlockSpec((r, chunk), lambda i: (0, i))
    fixed = lambda *shape: pl.BlockSpec(shape, lambda i: (0,) * len(shape))
    faces = (len(X_ROWS), LEVELS, COLS)
    return pl.pallas_call(
        functools.partial(scatter_kernel, chunk),
        grid=(points // chunk,),
        in_specs=[pl.BlockSpec(memory_space=pltpu.SMEM)]
        + [spec(r) for r in (6, 1, 1, 3, 1, 1, 1)]
        + [fixed(CELLS, COLS)] * 2,
        out_specs=[fixed(10, CELLS, COLS), fixed(*faces), fixed(*faces)],
        out_shape=[
            jax.ShapeDtypeStruct((10, CELLS, COLS), f32),
            jax.ShapeDtypeStruct(faces, f32),
            jax.ShapeDtypeStruct(faces, f32),
        ],
        scratch_shapes=[pltpu.VMEM((640, 256), f32)],
        compiler_params=pltpu.CompilerParams(vmem_limit_bytes=60 << 20),
        cost_estimate=pl.CostEstimate(
            flops=2 * 960 * 256 * points, bytes_accessed=64 * points, transcendentals=0
        ),
        name="point_sums",
    )(count.reshape(1), trial, row(mean), row(cons), vel, row(wt), row(cell), row(flag), por, perm)


def y_own_kernel(sums, por, perm, out):
    lane = lax.broadcasted_iota(i32, (CELLS, COLS), 1)
    packed = jnp.zeros((CELLS, COLS), f32)
    for field in range(FIELDS):
        at, depth = Y_PLACE[field], Y_DEPTH[field]
        own = sums[field] if field < 10 else (por if field == POR else perm)[...]
        packed = jnp.where((lane >= at - depth) & (lane < at + depth), turn(own, at, 1), packed)
    out[...] = packed


def y_own(sums, por, perm):
    return pl.pallas_call(
        y_own_kernel,
        out_shape=jax.ShapeDtypeStruct((CELLS, COLS), f32),
        cost_estimate=pl.CostEstimate(flops=4000000, bytes_accessed=900000, transcendentals=0),
        name="y_own",
    )(sums, por, perm)


def y_pack_kernel(own, below, above, out):
    lane = lax.broadcasted_iota(i32, (CELLS, COLS), 1)
    lane16 = lax.broadcasted_iota(i32, (LEVELS, COLS), 1)
    slots = [jnp.zeros((LEVELS, COLS), f32)] * ROWS
    for q, (field, deep) in enumerate(X_ROWS):
        at, depth = Y_PLACE[field] + HALF, Y_DEPTH[field]
        mask = (lane16 >= at - depth) & (lane16 < at + depth)
        for source, slot in ((above, deep), (below, ROWS - 1 - deep)):
            slots[slot] = jnp.where(mask, turn(source[q], at, 1), slots[slot])
    out[...] = jnp.where(lane < HALF, own[...], jnp.concatenate(slots, axis=0))


def y_pack(own, below, above):
    return pl.pallas_call(
        y_pack_kernel,
        out_shape=jax.ShapeDtypeStruct((CELLS, COLS), f32),
        name="y_pack",
    )(own, below, above)


def y_from_above(shape):
    lane = lax.broadcasted_iota(i32, shape, 1) & (HALF - 1)
    mask = lane < 0
    for field in range(FIELDS):
        at = Y_PLACE[field]
        mask |= (lane >= at) & (lane < at + Y_DEPTH[field])
    return mask


Y_LOW, Y_HIGH, X_HAS_LOW, X_HAS_HIGH, Y_HAS_LOW, Y_HAS_HIGH, LAYER = range(7)


def met(where, packs, from_above, rows):
    low = packs[where[Y_LOW], rows, :] * where[Y_HAS_LOW].astype(f32)
    high = packs[where[Y_HIGH], rows, :] * where[Y_HAS_HIGH].astype(f32)
    return jnp.where(from_above, high, low)


def diff_x(own, rim):
    row = tile_iota(0)
    own_up, rim_up = turn(own, -1, 0), turn(rim, -1, 0)
    own_down, rim_down = turn(own, 1, 0), turn(rim, 1, 0)
    top, bottom = row == ROWS - 1, row == 0
    return (
        jnp.where(top, rim_up, own_up) - jnp.where(bottom, rim_down, own_down),
        jnp.where(top, own_up, rim_up) - jnp.where(bottom, own_down, rim_down),
    )


def diff_y(own, rim):
    lane = tile_iota(1)
    own_up, rim_up = turn(own, -1, 1), turn(rim, -1, 1)
    own_down, rim_down = turn(own, 1, 1), turn(rim, 1, 1)
    top, bottom = lane == COLS - 1, lane == 0
    return (
        jnp.where(top, rim_up, own_up) - jnp.where(bottom, rim_down, own_down),
        jnp.where(top, own_up, rim_up) - jnp.where(bottom, own_down, rim_down),
    )


def ext_x(t):
    a0, a1 = diff_x(t[0], t[1])
    b0, b1 = diff_x(t[2], t[3])
    return [a0, a1, b0, b1]


def ext_y(t):
    a0, a2 = diff_y(t[0], t[2])
    b1, b3 = diff_y(t[1], t[3])
    return [a0, b1, a2, b3]


def rim_masks(where):
    row, lane = tile_iota(0), tile_iota(1)
    has = lambda low, high, test: jnp.where(test, where[high], where[low]) == 1
    in_x = has(X_HAS_LOW, X_HAS_HIGH, row < 4)
    in_y = has(Y_HAS_LOW, Y_HAS_HIGH, lane < HALF)
    return in_x, in_y, in_x & in_y


def local_kernel(where, sums, por, perm, below, above, packs, vel, inner, out, rim, corner):
    rim[...] = jnp.zeros_like(rim)
    for q, (field, deep) in enumerate(X_ROWS):
        rim[field, pl.ds(deep, LEVELS, stride=ROWS), :] = above[q]
        rim[field, pl.ds(ROWS - 1 - deep, LEVELS, stride=ROWS), :] = below[q]
    from_above = y_from_above((LEVELS, COLS))
    for slot in range(ROWS):
        rows = pl.ds(slot * LEVELS, LEVELS)
        corner[pl.ds(slot, LEVELS, stride=ROWS), :] = met(where, packs, from_above, rows)
    from_above = y_from_above((ROWS, COLS))
    in_x, in_y, in_xy = rim_masks(where)
    in_rims = (in_x, in_y, in_xy)
    inside = lambda t: t[:1] + [jnp.where(m, v, 0.0) for m, v in zip(in_rims, t[1:])]
    zero = jnp.zeros((ROWS, COLS), f32)

    def field_at(field, level):
        rows = pl.ds(level * ROWS, ROWS)
        at = Y_PLACE[field]
        own = sums[field, rows, :] if field < 10 else (por if field == POR else perm)[rows, :]
        lanes = met(where, packs, from_above, rows)
        return [
            own,
            rim[field, rows, :],
            turn(lanes, -at, 1),
            turn(corner[rows, :], -at - HALF, 1),
        ]

    memo = {}

    def get(field, level):
        if not 0 <= level < LEVELS:
            return [zero] * 4
        if (field, level) not in memo:
            memo[field, level] = field_at(field, level)
        return memo[field, level]

    def star(level):
        weight = inside([0.125 / jnp.maximum(m, 0.5) for m in get(MASS, level)])
        dz = lambda f: [u - d for u, d in zip(get(f, level + 1), get(f, level - 1))]
        forces = (
            (ext_x(get(XX, level)), ext_y(get(XY, level)), dz(ZX)),
            (ext_x(get(XY, level)), ext_y(get(YY, level)), dz(YZ)),
            (ext_x(get(ZX, level)), ext_y(get(YZ, level)), dz(ZZ)),
        )
        found = []
        for field, (fx, fy, fz) in zip((MX, MY, MZ), forces):
            found.append(
                [
                    (8.0 * m + (fx[n] + fy[n] + fz[n])) * weight[n]
                    for n, m in enumerate(get(field, level))
                ]
            )
        return found, weight

    def level_perm(level):
        own, x, y, _ = get(PERM, level)
        return [own] + [jnp.where(t > 0.0, t, 1.0) for t in (x, y)]

    def faces(level):
        pairs = zip(level_perm(level), level_perm(level + 1))
        return [0.5 * a * b / (a + b) for a, b in pairs]

    zero3 = [zero] * 3
    stars, weights = {}, {}
    stars[0], weights[0] = star(0)
    first_star = stars[0][2]
    wide = {0: [weights[0], get(ZX, 0), get(YZ, 0)]}
    stress = {0: get(ZZ, 0)}
    down = zero3
    kept, terms, sources, links = [], {}, {}, {}
    for level in range(LEVELS):
        if level + 1 < LEVELS:
            stars[level + 1], weights[level + 1] = star(level + 1)
        vx, vy, vz = stars[level]
        for n, part in enumerate((vx, vy, vz)):
            vel[n, pl.ds(level * ROWS, ROWS), :] = part[0]
        z_up = stars[level + 1][2] if level + 1 < LEVELS else zero3
        z_down = stars[level - 1][2] if level > 0 else zero3
        if level == LEVELS - 1:
            wide[1] = [weights[level], get(ZX, level), get(YZ, level)]
            stress[1] = get(ZZ, level)
        dx, dy = ext_x(vx), ext_y(vy)
        porosity = get(POR, level)[:3]
        up = faces(level) if level + 1 < LEVELS else zero3
        now = []
        for n in range(3):
            source = -0.0015 * (1.0 - porosity[n])
            right = source * (dx[n] + dy[n] + (z_up[n] - z_down[n]))
            main = 0.002 * porosity[n] + (down[n] + up[n])
            now.append((-down[n], main, -up[n], right, source))
        sources[level], links[level] = [t[4] for t in now], up
        down = up
        if level in (0, LEVELS - 1):
            terms[level] = now
        elif level == 1:
            kept.append([(lo, 1.0 / mid, hi, r) for lo, mid, hi, r, _ in now])
        else:
            rows = []
            for (lo, mid, hi, r, _), (f, inv, u, pr) in zip(now, kept[-1]):
                w = lo * inv
                rows.append((-w * f, 1.0 / (mid - w * u), hi, r - w * pr))
            kept.append(rows)
        for key in [k for k in memo if k[1] < level]:
            del memo[key]
    after = last_inner = None
    for n_row in range(len(kept) - 1, -1, -1):
        rows = []
        for t in range(3):
            f, inv, u, r = kept[n_row][t]
            if after is None:
                rows.append((r * inv, -f * inv, -u * inv))
            else:
                b2, f2, g2 = after[t]
                rows.append(((r - u * b2) * inv, -(f + u * f2) * inv, -u * g2 * inv))
            for m in range(3):
                inner[t, m, n_row] = rows[t][m]
        last_inner = last_inner or rows
        after = rows
    first_inner = after
    top = LEVELS - 1
    narrow = []
    for t in range(3):
        _, mid, hi, r, source = terms[0][t]
        b, f, g = first_inner[t]
        echo = sources[1][t] * weights[0][t] / links[0][t]
        face = level_perm(0)[t]
        mine = [face, mid + hi * f, hi * f, hi * g, r - hi * b, source, echo, first_star[t], stress[0][t]]
        lo, mid, _, r, source = terms[top][t]
        b, f, g = last_inner[t]
        echo = sources[top - 1][t] * weights[top][t] / links[top - 1][t]
        face = level_perm(top)[t]
        mine += [face, mid + lo * g, lo * g, lo * f, r - lo * b, source, echo, stars[top][2][t], stress[1][t]]
        narrow.append(mine)
    row, lane = tile_iota(0), tile_iota(1)
    x_parts = [zero] * -(-NARROW // 4)
    x_wide = [zero] * -(-WIDE // 2)
    y_part = zero

    def between(index, at, count):
        return (index >= at) & (index < at + count)

    for q in range(NARROW):
        own, x, y = (narrow[t][q] for t in range(3))
        out[8 * q : 8 * q + 8, :] = own
        at = 2 * q % 8
        x_parts[q // 4] = jnp.where(between(row, at, 2), turn(x, at + 1, 0), x_parts[q // 4])
        y_part = jnp.where(between(lane, 2 * q, 2), turn(y, 2 * q + 1, 1), y_part)
    for m, (own, x, y, xy) in enumerate(wide[0] + wide[1]):
        at = 8 * (NARROW + m)
        out[at : at + 8, :] = own
        at = 4 * (m % 2)
        x_wide[m // 2] = jnp.where(between(row, at, 4), turn(x, at + 2, 0), x_wide[m // 2])
        at = LANE_WIDE + 4 * m
        y_part = jnp.where(between(lane, at, 4), turn(y, at + 2, 1), y_part)
        at = LANE_CORNER + 2 * m
        y_part = jnp.where(between(lane, at, 2), turn(xy, at + 1, 1), y_part)
    for n, part in enumerate(x_parts):
        out[MSG_X + 8 * n : MSG_X + 8 * n + 8, :] = part
    for n, part in enumerate(x_wide):
        out[MSG_X_WIDE + 8 * n : MSG_X_WIDE + 8 * n + 8, :] = part
    out[MSG_Y : MSG_Y + 8, :] = y_part


def local_solve(where, sums, por, perm, below, above, packs):
    smem = pl.BlockSpec(memory_space=pltpu.SMEM)
    vmem = pl.BlockSpec(memory_space=pltpu.VMEM)
    return pl.pallas_call(
        local_kernel,
        in_specs=[smem] + [vmem] * 6,
        out_shape=[
            jax.ShapeDtypeStruct((3, CELLS, COLS), f32),
            jax.ShapeDtypeStruct((3, 3, LEVELS - 2, ROWS, COLS), f32),
            jax.ShapeDtypeStruct((MSG_ROWS, COLS), f32),
        ],
        scratch_shapes=[pltpu.VMEM((FIELDS, CELLS, COLS), f32), pltpu.VMEM((CELLS, COLS), f32)],
        compiler_params=pltpu.CompilerParams(vmem_limit_bytes=32 << 20),
        name="local_solve",
    )(where, sums, por, perm, below, above, packs)


def final_kernel(layers, where, vel, inner, told, out, pressure):
    me = where[LAYER]
    zero = jnp.zeros((ROWS, COLS), f32)

    def narrow(k, side, what):
        q = 9 * side + what
        at = MSG_X + 8 * (q // 4)
        return [
            told[k, 8 * q : 8 * q + 8, :],
            turn(told[k, at : at + 8, :], -(2 * q % 8 + 1), 0),
            turn(told[k, MSG_Y : MSG_Y + 8, :], -(2 * q + 1), 1),
        ]

    def wide(k, side, what):
        m = 3 * side + what
        own = 8 * (NARROW + m)
        at = MSG_X_WIDE + 8 * (m // 2)
        lanes = told[k, MSG_Y : MSG_Y + 8, :]
        return [
            told[k, own : own + 8, :],
            turn(told[k, at : at + 8, :], -(4 * (m % 2) + 2), 0),
            turn(lanes, -(LANE_WIDE + 4 * m + 2), 1),
            turn(lanes, -(LANE_CORNER + 2 * m + 1), 1),
        ]

    def times(*factors):
        product = factors[0]
        for factor in factors[1:]:
            product = [a * b for a, b in zip(product, factor)]
        return product

    def plus(*terms):
        total = terms[0]
        for term in terms[1:]:
            total = [a + b for a, b in zip(total, term)]
        return total

    def minus(a, b):
        return [x - y for x, y in zip(a, b)]

    def half_face(a, b):
        return [0.5 * x * y / (x + y) for x, y in zip(a, b)]

    rows, gains, echoes = [], [], []
    for k in range(layers):
        gain, echo = [], []
        sides = []
        for side, other in ((0, k - 1), (1, k + 1)):
            right = narrow(k, side, RIGHT)
            main = narrow(k, side, MAIN)
            if 0 <= other < layers:
                weight = wide(k, side, WEIGHT)
                sign = -1.0 if side == 0 else 1.0
                weight = [sign * w for w in weight]
                stress = narrow(other, 1 - side, STRESSZ)
                vx = times(weight, wide(other, 1 - side, SHEARX))
                vy = times(weight, wide(other, 1 - side, SHEARY))
                vz = times(weight, stress)
                change = times(wide(other, 1 - side, WEIGHT), narrow(k, side, STRESSZ))
                beyond = minus(narrow(other, 1 - side, VELZ), [sign * c for c in change])
                spread = plus(ext_x(vx)[:3], ext_y(vy)[:3], [sign * v for v in beyond])
                right = plus(right, times(narrow(k, side, SOURCE), spread))
                link = half_face(narrow(k, side, FACE), narrow(other, 1 - side, FACE))
                main = plus(main, link)
                echo.append(times(narrow(k, side, ECHO), stress))
                gain.append((vx[0], vy[0], vz[0]))
            else:
                link = [zero] * 3
                if side == 1:
                    main = plus(main, [0.25 * v for v in narrow(k, side, FACE)])
                echo.append([zero] * 3)
                gain.append((zero, zero, zero))
            sides.append((link, main, right))
        for side, (link, main, right) in enumerate(sides):
            near, far = narrow(k, side, NEAR), narrow(k, side, FAR)
            right = minus(right, plus(times(near, echo[side]), times(far, echo[1 - side])))
            inv = [1.0 / m for m in main]
            link = [-v * i for v, i in zip(link, inv)]
            far, right = times(far, inv), times(right, inv)
            rows.append((link, far, right) if side == 0 else (far, link, right))
        gains.append(gain)
        echoes.append(echo)
    done = []
    for n, (lo, hi, r) in enumerate(rows):
        if n == 0:
            done.append((hi, r))
            continue
        hs, rs = done[-1]
        inv = [1.0 / (1.0 - l * h) for l, h in zip(lo, hs)]
        done.append((times(hi, inv), times(minus(r, times(lo, rs)), inv)))
    ends = [None] * len(rows)
    ends[-1] = done[-1][1]
    for n in range(len(rows) - 2, -1, -1):
        hs, rs = done[n]
        ends[n] = minus(rs, times(hs, ends[n + 1]))

    def mine(values):
        chosen = values[0]
        for k in range(1, layers):
            chosen = [jnp.where(me == k, v, c) for v, c in zip(values[k], chosen)]
        return chosen

    first, last = mine(ends[0::2]), mine(ends[1::2])
    under = mine([[zero]] + [e[:1] for e in ends[1:-1:2]])[0]
    over = mine([e[:1] for e in ends[2::2]] + [[zero]])[0]
    first_seen = plus(first, mine([e[0] for e in echoes]))
    last_seen = plus(last, mine([e[1] for e in echoes]))
    gain = {0: mine([g[0] for g in gains]), LEVELS - 1: mine([g[1] for g in gains])}
    in_x, in_y, _ = rim_masks(where)

    def press(level):
        if level < 0:
            return [under]
        if level >= LEVELS:
            return [over]
        if level == 0:
            parts = first
        elif level == LEVELS - 1:
            parts = last
        else:
            parts = [
                inner[t, 0, level - 1]
                + inner[t, 1, level - 1] * first_seen[t]
                + inner[t, 2, level - 1] * last_seen[t]
                for t in range(3)
            ]
        return [parts[0], jnp.where(in_x, parts[1], 0.0), jnp.where(in_y, parts[2], 0.0)]

    before, now = press(-1), press(0)
    for level in range(LEVELS):
        after = press(level + 1)
        rows_at = pl.ds(level * ROWS, ROWS)
        pressure[rows_at, :] = now[0]
        grads = (
            diff_x(now[0], now[1])[0],
            diff_y(now[0], now[2])[0],
            after[0] - before[0],
        )
        for n in range(3):
            value = vel[n, rows_at, :] - 0.125 * grads[n]
            out[n, rows_at, :] = value + gain[level][n] if level in gain else value
        before, now = now, after


def final(where, vel, inner, told):
    smem = pl.BlockSpec(memory_space=pltpu.SMEM)
    vmem = pl.BlockSpec(memory_space=pltpu.VMEM)
    return pl.pallas_call(
        functools.partial(final_kernel, told.shape[0]),
        in_specs=[smem] + [vmem] * 3,
        out_shape=[
            jax.ShapeDtypeStruct((3, CELLS, COLS), f32),
            jax.ShapeDtypeStruct((CELLS, COLS), f32),
        ],
        compiler_params=pltpu.CompilerParams(vmem_limit_bytes=32 << 20),
        name="final",
    )(where, vel, inner, told)


def shift_up(block, axis):
    count = lax.axis_size(axis)
    return lax.ppermute(block, axis, [(i, i + 1) for i in range(count - 1)])


def shift_down(block, axis):
    count = lax.axis_size(axis)
    return lax.ppermute(block, axis, [(i + 1, i) for i in range(count - 1)])


def neighbours(block, axis):
    count, me = lax.axis_size(axis), lax.axis_index(axis)
    if count > 4:
        return jnp.stack([shift_up(block, axis), shift_down(block, axis)]), 0, 1
    stacked = lax.all_gather(block, axis, axis=0)
    return stacked, jnp.maximum(me - 1, 0), jnp.minimum(me + 1, count - 1)


def shards(trial, mean, cons, vel, wt, cell, flag, count, por, perm):
    por = por.reshape(CELLS, COLS)
    perm = perm.reshape(CELLS, COLS)
    sums, low, high = scatter(trial, mean, cons, vel, wt, cell, flag, count, por, perm)
    above = shift_down(low, "gx")
    below = shift_up(high, "gx")

    def ends(axis):
        me = lax.axis_index(axis)
        return [(me > 0).astype(i32), (me < lax.axis_size(axis) - 1).astype(i32)]

    has = ends("gx") + ends("gy")
    own = y_own(sums, por, perm)
    packs, y_low, y_high = neighbours(y_pack(own, below, above), "gy")
    where = jnp.stack(
        [jnp.asarray(v, i32) for v in [y_low, y_high] + has + [lax.axis_index("gz")]]
    )
    star, inner, told = local_solve(where, sums, por, perm, below, above, packs)
    velocity, pressure = final(where, star, inner, lax.all_gather(told, "gz", axis=0))
    return (
        velocity.reshape(3, LEVELS, ROWS, COLS),
        pressure.reshape(LEVELS, ROWS, COLS),
    )


def solution(mesh):
    points = ("gx", "gy", "gz")
    cells = P("gz", "gx", "gy")
    placed = (
        P(None, points), P(points), P(points), P(None, points), P(points), P(points), P(points),
        P(*points), cells, cells,
    )
    return jax.shard_map(
        shards,
        mesh=mesh,
        in_specs=placed,
        out_specs=(P(None, *cells), cells),
        check_vma=False,
    )
```

```python
import functools

import jax
import jax.numpy as jnp
from jax import lax
from jax.experimental import pallas as pl
from jax.experimental.pallas import tpu as pltpu
from jax.sharding import PartitionSpec as P

bf = jnp.bfloat16
f8 = jnp.float8_e4m3fn
f32 = jnp.float32
i32 = jnp.int32

LEVELS, ROWS, COLS = 16, 8, 128
CELLS = LEVELS * ROWS

ZX, YZ, ZZ, XX, YY, XY, MX, MY, MZ, MASS, POR, PERM = range(12)
FIELDS = 12
STRESS_ORDER = (5, 4, 2, 0, 1, 3)

X_ROWS = (
    (ZX, 0), (ZX, 1), (YZ, 0), (ZZ, 0), (PERM, 0), (POR, 0),
    (XX, 0), (XX, 1), (XX, 2), (XY, 0), (XY, 1), (YY, 0),
    (MX, 0), (MX, 1), (MY, 0), (MZ, 0), (MASS, 0), (MASS, 1),
)
X_DEEP = 3
X_SENT = len(X_ROWS) + X_DEEP
Y_DEPTH = {ZX: 1, YZ: 2, ZZ: 1, XX: 1, YY: 3, XY: 2, MX: 1, MY: 2, MZ: 1, MASS: 2, POR: 1, PERM: 1}
Y_PLACE = {}
_at = 0
for _f in range(FIELDS):
    Y_PLACE[_f] = _at + Y_DEPTH[_f]
    _at += 2 * Y_DEPTH[_f]
HALF = 64
FACE, MAIN, NEAR, FAR, RIGHT, SOURCE, ECHO, VELZ, STRESSZ = range(9)
WEIGHT, SHEARX, SHEARY = range(3)
NARROW, WIDE = 18, 6
MSG_X = 8 * (NARROW + WIDE)
MSG_X_WIDE = MSG_X + 8 * -(-NARROW // 4)
MSG_Y = MSG_X_WIDE + 8 * -(-WIDE // 2)
MSG_ROWS = MSG_Y + 8
LANE_WIDE = 2 * NARROW
LANE_CORNER = LANE_WIDE + 4 * WIDE


def tile_iota(dim):
    return lax.broadcasted_iota(i32, (ROWS, COLS), dim)


def turn(tile, shift, axis):
    shift %= tile.shape[axis]
    return tile if shift == 0 else pltpu.roll(tile, shift, axis)


def row_stress(trial, mean, cons, flag):
    part = lax.broadcasted_iota(i32, trial.shape, 0)
    size = jnp.sqrt(
        jnp.sum(trial * trial * jnp.where(part < 3, 1.5, 3.0), axis=0, keepdims=True)
    )
    yield_size = 1.2 * jnp.sqrt(mean * (cons - mean))
    factor = jnp.where(flag == 1, yield_size / jnp.maximum(size, 1.0), 1.0)
    return trial * factor - jnp.where(part < 3, mean, 0.0)


def point_rows(trial, mean, cons, vel, wt, flag, live):
    weight = jnp.where(live, wt, 0.0)
    stress = row_stress(trial, mean, cons, flag) * weight
    momentum = vel * weight
    rows = [stress[i : i + 1] for i in STRESS_ORDER]
    return rows + [momentum[i : i + 1] for i in range(3)] + [weight]


def cell_products(rows, place):
    chunk = place.shape[1]
    hi = (place >> 7) & 63
    lo = ((place >> 13) << 7) | (place & 127)

    def spread(row, count, kind):
        return jnp.broadcast_to(row, (count, chunk)).astype(kind)

    one, zero = jnp.array(1, bf), jnp.array(0, bf)
    base = lax.broadcasted_iota(i32, (16, chunk), 0)

    def equal(index, count):
        index = spread(index.astype(f32), 16, bf)
        return [(base + b * 16).astype(f32).astype(bf) == index for b in range(count // 16)]

    hi_mask = equal(hi, 64)
    right = jnp.concatenate([jnp.where(m, one, zero) for m in equal(lo, 256)], axis=0)
    base32 = lax.broadcasted_iota(i32, (32, chunk), 0)
    hi_mask8 = [base32 + 32 * b == jnp.broadcast_to(hi, (32, chunk)) for b in range(2)]
    zero8 = jnp.zeros((32, chunk), f8)
    left, left8 = [], []
    for row in rows:
        top = row.astype(bf).astype(f32)
        part = spread(top, 16, bf)
        left += [jnp.where(m, part, zero) for m in hi_mask]
        part = spread((row - top) * 256.0, 32, f8)
        left8 += [jnp.where(m, part, zero8) for m in hi_mask8]
    left = jnp.concatenate(left, axis=0)
    left8 = jnp.concatenate(left8, axis=0)
    dims = (((1,), (1,)), ((), ()))
    prod = lax.dot_general(left, right, dims, preferred_element_type=f32)
    prod8 = lax.dot_general(left8, right.astype(f8), dims, preferred_element_type=f32)
    return prod + prod8 * (1 / 256.0)


def scatter_kernel(chunk, *refs):
    sources, (out, low, high), scratch = refs[:10], refs[10:13], refs[13:]
    trial, mean, cons, vel, wt, cell, flag, count, por, perm = scratch[:10]
    acc, sems = scratch[10:]
    chunks = cell.shape[1] // chunk

    def copy(n, c):
        if n < 7:
            at = pl.ds(pl.multiple_of(c * chunk, chunk), chunk)
            return pltpu.make_async_copy(sources[n].at[:, at], scratch[n].at[:, at], sems.at[n, c])
        return pltpu.make_async_copy(sources[n], scratch[n], sems.at[n, 0])

    copy(7, 0).start()
    for c in range(chunks):
        for n in range(7):
            copy(n, c).start()
    copy(8, 0).start()
    copy(9, 0).start()
    copy(7, 0).wait()

    def step(c, carry):
        for n in range(7):
            copy(n, c).wait()
        at = pl.ds(pl.multiple_of(c * chunk, chunk), chunk)
        slot = c * chunk + lax.broadcasted_iota(i32, (1, chunk), 1)
        live = slot < count[0]
        rows = point_rows(
            trial[:, at], mean[:, at], cons[:, at], vel[:, at], wt[:, at], flag[:, at], live
        )
        prod = cell_products(rows, cell[:, at])

        @pl.when(c == 0)
        def _():
            acc[...] = prod

        @pl.when(c > 0)
        def _():
            acc[...] += prod

        return carry

    lax.fori_loop(0, chunks, step, 0)
    copy(8, 0).wait()
    copy(9, 0).wait()
    for i in range(10):
        out[i, 0:64, :] = acc[i * 64 : i * 64 + 64, :COLS]
        out[i, 64:128, :] = acc[i * 64 : i * 64 + 64, COLS:]
    lane = lax.broadcasted_iota(i32, (LEVELS, COLS), 1)
    packed = [[jnp.zeros((LEVELS, COLS), f32)] * X_DEEP for _ in range(2)]
    for q, (field, deep) in enumerate(X_ROWS):
        at, depth = Y_PLACE[field] + HALF, Y_DEPTH[field]
        mask = (lane >= at - depth) & (lane < at + depth)
        for side, row in ((0, deep), (1, ROWS - 1 - deep)):
            rows = pl.ds(row, LEVELS, stride=ROWS)
            if field < 10:
                values = out[field, rows, :]
            else:
                values = (por if field == POR else perm)[rows, :]
            (low, high)[side][q] = values
            packed[side][deep] = jnp.where(mask, turn(values, at, 1), packed[side][deep])
    for deep in range(X_DEEP):
        low[len(X_ROWS) + deep] = packed[0][deep]
        high[len(X_ROWS) + X_DEEP - 1 - deep] = packed[1][deep]


def scatter(trial, mean, cons, vel, wt, cell, flag, count, por, perm):
    points = mean.shape[0]
    chunk = points // 2 if points % 256 == 0 else points
    row = lambda v: v.reshape(1, points)
    args = (trial, row(mean), row(cons), vel, row(wt), row(cell), row(flag), count, por, perm)
    faces = (X_SENT, LEVELS, COLS)
    return pl.pallas_call(
        functools.partial(scatter_kernel, chunk),
        in_specs=[pl.BlockSpec(memory_space=pltpu.HBM)] * len(args),
        out_shape=[
            jax.ShapeDtypeStruct((10, CELLS, COLS), f32),
            jax.ShapeDtypeStruct(faces, f32),
            jax.ShapeDtypeStruct(faces, f32),
        ],
        scratch_shapes=[pltpu.VMEM(v.shape, v.dtype) for v in args]
        + [pltpu.VMEM((640, 256), f32), pltpu.SemaphoreType.DMA((len(args), points // chunk))],
        compiler_params=pltpu.CompilerParams(vmem_limit_bytes=56 << 20),
        cost_estimate=pl.CostEstimate(
            flops=2 * 960 * 256 * points, bytes_accessed=64 * points, transcendentals=0
        ),
        name="point_sums",
    )(*args)


def y_own_kernel(sums, por, perm, out):
    lane = lax.broadcasted_iota(i32, (CELLS, COLS), 1)
    packed = jnp.zeros((CELLS, COLS), f32)
    for field in range(FIELDS):
        at, depth = Y_PLACE[field], Y_DEPTH[field]
        own = sums[field] if field < 10 else (por if field == POR else perm)[...]
        packed = jnp.where((lane >= at - depth) & (lane < at + depth), turn(own, at, 1), packed)
    out[...] = packed


def y_own(sums, por, perm):
    return pl.pallas_call(
        y_own_kernel,
        out_shape=jax.ShapeDtypeStruct((CELLS, COLS), f32),
        cost_estimate=pl.CostEstimate(flops=4000000, bytes_accessed=900000, transcendentals=0),
        compiler_params=pltpu.CompilerParams(vmem_limit_bytes=8 << 20),
        name="y_own",
    )(sums, por, perm)


def with_rims(own, below, above):
    rows = X_DEEP * LEVELS
    first = above[len(X_ROWS) :].reshape(rows, COLS)
    last = below[len(X_ROWS) :].reshape(rows, COLS)
    return own + jnp.concatenate([first, jnp.zeros((CELLS - 2 * rows, COLS), f32), last])


def y_from_above(shape):
    lane = lax.broadcasted_iota(i32, shape, 1) & (HALF - 1)
    mask = lane < 0
    for field in range(FIELDS):
        at = Y_PLACE[field]
        mask |= (lane >= at) & (lane < at + Y_DEPTH[field])
    return mask


Y_LOW, Y_HIGH, X_HAS_LOW, X_HAS_HIGH, Y_HAS_LOW, Y_HAS_HIGH, LAYER = range(7)


def met(where, packs, from_above, rows):
    low = packs[where[Y_LOW], rows, :] * where[Y_HAS_LOW].astype(f32)
    high = packs[where[Y_HIGH], rows, :] * where[Y_HAS_HIGH].astype(f32)
    return jnp.where(from_above, high, low)


def diff_x(own, rim):
    row = tile_iota(0)
    own_up, rim_up = turn(own, -1, 0), turn(rim, -1, 0)
    own_down, rim_down = turn(own, 1, 0), turn(rim, 1, 0)
    top, bottom = row == ROWS - 1, row == 0
    return (
        jnp.where(top, rim_up, own_up) - jnp.where(bottom, rim_down, own_down),
        jnp.where(top, own_up, rim_up) - jnp.where(bottom, own_down, rim_down),
    )


def diff_y(own, rim):
    lane = tile_iota(1)
    own_up, rim_up = turn(own, -1, 1), turn(rim, -1, 1)
    own_down, rim_down = turn(own, 1, 1), turn(rim, 1, 1)
    top, bottom = lane == COLS - 1, lane == 0
    return (
        jnp.where(top, rim_up, own_up) - jnp.where(bottom, rim_down, own_down),
        jnp.where(top, own_up, rim_up) - jnp.where(bottom, own_down, rim_down),
    )


def ext_x(t):
    a0, a1 = diff_x(t[0], t[1])
    b0, b1 = diff_x(t[2], t[3])
    return [a0, a1, b0, b1]


def ext_y(t):
    a0, a2 = diff_y(t[0], t[2])
    b1, b3 = diff_y(t[1], t[3])
    return [a0, b1, a2, b3]


def rim_masks(where):
    row, lane = tile_iota(0), tile_iota(1)
    has = lambda low, high, test: jnp.where(test, where[high], where[low]) == 1
    in_x = has(X_HAS_LOW, X_HAS_HIGH, row < 4)
    in_y = has(Y_HAS_LOW, Y_HAS_HIGH, lane < HALF)
    return in_x, in_y, in_x & in_y


def local_kernel(where, sums, por, perm, below, above, packs, vel, inner, out, rim, corner):
    rim[...] = jnp.zeros_like(rim)
    for q, (field, deep) in enumerate(X_ROWS):
        rim[field, pl.ds(deep, LEVELS, stride=ROWS), :] = above[q]
        rim[field, pl.ds(ROWS - 1 - deep, LEVELS, stride=ROWS), :] = below[q]
    from_above = y_from_above((LEVELS, COLS))
    for slot in range(ROWS):
        rows = pl.ds(slot * LEVELS, LEVELS)
        corner[pl.ds(slot, LEVELS, stride=ROWS), :] = met(where, packs, from_above, rows)
    from_above = y_from_above((ROWS, COLS))
    in_x, in_y, in_xy = rim_masks(where)
    in_rims = (in_x, in_y, in_xy)
    inside = lambda t: t[:1] + [jnp.where(m, v, 0.0) for m, v in zip(in_rims, t[1:])]
    zero = jnp.zeros((ROWS, COLS), f32)

    def field_at(field, level):
        rows = pl.ds(level * ROWS, ROWS)
        at = Y_PLACE[field]
        own = sums[field, rows, :] if field < 10 else (por if field == POR else perm)[rows, :]
        lanes = met(where, packs, from_above, rows)
        return [
            own,
            rim[field, rows, :],
            turn(lanes, -at, 1),
            turn(corner[rows, :], -at - HALF, 1),
        ]

    memo = {}

    def get(field, level):
        if not 0 <= level < LEVELS:
            return [zero] * 4
        if (field, level) not in memo:
            memo[field, level] = field_at(field, level)
        return memo[field, level]

    def star(level):
        weight = inside([0.125 / jnp.maximum(m, 0.5) for m in get(MASS, level)])
        dz = lambda f: [u - d for u, d in zip(get(f, level + 1), get(f, level - 1))]
        forces = (
            (ext_x(get(XX, level)), ext_y(get(XY, level)), dz(ZX)),
            (ext_x(get(XY, level)), ext_y(get(YY, level)), dz(YZ)),
            (ext_x(get(ZX, level)), ext_y(get(YZ, level)), dz(ZZ)),
        )
        found = []
        for field, (fx, fy, fz) in zip((MX, MY, MZ), forces):
            found.append(
                [
                    (8.0 * m + (fx[n] + fy[n] + fz[n])) * weight[n]
                    for n, m in enumerate(get(field, level))
                ]
            )
        return found, weight

    def level_perm(level):
        own, x, y, _ = get(PERM, level)
        return [own] + [jnp.where(t > 0.0, t, 1.0) for t in (x, y)]

    def faces(level):
        pairs = zip(level_perm(level), level_perm(level + 1))
        return [0.5 * a * b / (a + b) for a, b in pairs]

    zero3 = [zero] * 3
    stars, weights = {}, {}
    stars[0], weights[0] = star(0)
    first_star = stars[0][2]
    wide = {0: [weights[0], get(ZX, 0), get(YZ, 0)]}
    stress = {0: get(ZZ, 0)}
    down = zero3
    kept, terms, sources, links = [], {}, {}, {}
    for level in range(LEVELS):
        if level + 1 < LEVELS:
            stars[level + 1], weights[level + 1] = star(level + 1)
        vx, vy, vz = stars[level]
        for n, part in enumerate((vx, vy, vz)):
            vel[n, pl.ds(level * ROWS, ROWS), :] = part[0]
        z_up = stars[level + 1][2] if level + 1 < LEVELS else zero3
        z_down = stars[level - 1][2] if level > 0 else zero3
        if level == LEVELS - 1:
            wide[1] = [weights[level], get(ZX, level), get(YZ, level)]
            stress[1] = get(ZZ, level)
        dx, dy = ext_x(vx), ext_y(vy)
        porosity = get(POR, level)[:3]
        up = faces(level) if level + 1 < LEVELS else zero3
        now = []
        for n in range(3):
            source = -0.0015 * (1.0 - porosity[n])
            right = source * (dx[n] + dy[n] + (z_up[n] - z_down[n]))
            main = 0.002 * porosity[n] + (down[n] + up[n])
            now.append((-down[n], main, -up[n], right, source))
        sources[level], links[level] = [t[4] for t in now], up
        down = up
        if level in (0, LEVELS - 1):
            terms[level] = now
        elif level == 1:
            kept.append([(lo, 1.0 / mid, hi, r) for lo, mid, hi, r, _ in now])
        else:
            rows = []
            for (lo, mid, hi, r, _), (f, inv, u, pr) in zip(now, kept[-1]):
                w = lo * inv
                rows.append((-w * f, 1.0 / (mid - w * u), hi, r - w * pr))
            kept.append(rows)
        for key in [k for k in memo if k[1] < level]:
            del memo[key]
    after = last_inner = None
    for n_row in range(len(kept) - 1, -1, -1):
        rows = []
        for t in range(3):
            f, inv, u, r = kept[n_row][t]
            if after is None:
                rows.append((r * inv, -f * inv, -u * inv))
            else:
                b2, f2, g2 = after[t]
                rows.append(((r - u * b2) * inv, -(f + u * f2) * inv, -u * g2 * inv))
            for m in range(3):
                inner[t, m, n_row] = rows[t][m]
        last_inner = last_inner or rows
        after = rows
    first_inner = after
    top = LEVELS - 1
    narrow = []
    for t in range(3):
        _, mid, hi, r, source = terms[0][t]
        b, f, g = first_inner[t]
        echo = sources[1][t] * weights[0][t] / links[0][t]
        face = level_perm(0)[t]
        mine = [face, mid + hi * f, hi * f, hi * g, r - hi * b, source, echo, first_star[t], stress[0][t]]
        lo, mid, _, r, source = terms[top][t]
        b, f, g = last_inner[t]
        echo = sources[top - 1][t] * weights[top][t] / links[top - 1][t]
        face = level_perm(top)[t]
        mine += [face, mid + lo * g, lo * g, lo * f, r - lo * b, source, echo, stars[top][2][t], stress[1][t]]
        narrow.append(mine)
    row, lane = tile_iota(0), tile_iota(1)
    x_parts = [zero] * -(-NARROW // 4)
    x_wide = [zero] * -(-WIDE // 2)
    y_part = zero

    def between(index, at, count):
        return (index >= at) & (index < at + count)

    for q in range(NARROW):
        own, x, y = (narrow[t][q] for t in range(3))
        out[8 * q : 8 * q + 8, :] = own
        at = 2 * q % 8
        x_parts[q // 4] = jnp.where(between(row, at, 2), turn(x, at + 1, 0), x_parts[q // 4])
        y_part = jnp.where(between(lane, 2 * q, 2), turn(y, 2 * q + 1, 1), y_part)
    for m, (own, x, y, xy) in enumerate(wide[0] + wide[1]):
        at = 8 * (NARROW + m)
        out[at : at + 8, :] = own
        at = 4 * (m % 2)
        x_wide[m // 2] = jnp.where(between(row, at, 4), turn(x, at + 2, 0), x_wide[m // 2])
        at = LANE_WIDE + 4 * m
        y_part = jnp.where(between(lane, at, 4), turn(y, at + 2, 1), y_part)
        at = LANE_CORNER + 2 * m
        y_part = jnp.where(between(lane, at, 2), turn(xy, at + 1, 1), y_part)
    for n, part in enumerate(x_parts):
        out[MSG_X + 8 * n : MSG_X + 8 * n + 8, :] = part
    for n, part in enumerate(x_wide):
        out[MSG_X_WIDE + 8 * n : MSG_X_WIDE + 8 * n + 8, :] = part
    out[MSG_Y : MSG_Y + 8, :] = y_part


def local_solve(where, sums, por, perm, below, above, packs):
    smem = pl.BlockSpec(memory_space=pltpu.SMEM)
    vmem = pl.BlockSpec(memory_space=pltpu.VMEM)
    return pl.pallas_call(
        local_kernel,
        in_specs=[smem] + [vmem] * 6,
        out_shape=[
            jax.ShapeDtypeStruct((3, CELLS, COLS), f32),
            jax.ShapeDtypeStruct((3, 3, LEVELS - 2, ROWS, COLS), f32),
            jax.ShapeDtypeStruct((MSG_ROWS, COLS), f32),
        ],
        scratch_shapes=[pltpu.VMEM((FIELDS, CELLS, COLS), f32), pltpu.VMEM((CELLS, COLS), f32)],
        compiler_params=pltpu.CompilerParams(vmem_limit_bytes=16 << 20),
        name="local_solve",
    )(where, sums, por, perm, below, above, packs)


def final_kernel(layers, where, vel, inner, told, out, pressure):
    me = where[LAYER]
    zero = jnp.zeros((ROWS, COLS), f32)

    def narrow(k, side, what):
        q = 9 * side + what
        at = MSG_X + 8 * (q // 4)
        return [
            told[k, 8 * q : 8 * q + 8, :],
            turn(told[k, at : at + 8, :], -(2 * q % 8 + 1), 0),
            turn(told[k, MSG_Y : MSG_Y + 8, :], -(2 * q + 1), 1),
        ]

    def wide(k, side, what):
        m = 3 * side + what
        own = 8 * (NARROW + m)
        at = MSG_X_WIDE + 8 * (m // 2)
        lanes = told[k, MSG_Y : MSG_Y + 8, :]
        return [
            told[k, own : own + 8, :],
            turn(told[k, at : at + 8, :], -(4 * (m % 2) + 2), 0),
            turn(lanes, -(LANE_WIDE + 4 * m + 2), 1),
            turn(lanes, -(LANE_CORNER + 2 * m + 1), 1),
        ]

    def times(*factors):
        product = factors[0]
        for factor in factors[1:]:
            product = [a * b for a, b in zip(product, factor)]
        return product

    def plus(*terms):
        total = terms[0]
        for term in terms[1:]:
            total = [a + b for a, b in zip(total, term)]
        return total

    def minus(a, b):
        return [x - y for x, y in zip(a, b)]

    def half_face(a, b):
        return [0.5 * x * y / (x + y) for x, y in zip(a, b)]

    rows, gains, echoes = [], [], []
    for k in range(layers):
        gain, echo = [], []
        sides = []
        for side, other in ((0, k - 1), (1, k + 1)):
            right = narrow(k, side, RIGHT)
            main = narrow(k, side, MAIN)
            if 0 <= other < layers:
                weight = wide(k, side, WEIGHT)
                sign = -1.0 if side == 0 else 1.0
                weight = [sign * w for w in weight]
                stress = narrow(other, 1 - side, STRESSZ)
                vx = times(weight, wide(other, 1 - side, SHEARX))
                vy = times(weight, wide(other, 1 - side, SHEARY))
                vz = times(weight, stress)
                change = times(wide(other, 1 - side, WEIGHT), narrow(k, side, STRESSZ))
                beyond = minus(narrow(other, 1 - side, VELZ), [sign * c for c in change])
                spread = plus(ext_x(vx)[:3], ext_y(vy)[:3], [sign * v for v in beyond])
                right = plus(right, times(narrow(k, side, SOURCE), spread))
                link = half_face(narrow(k, side, FACE), narrow(other, 1 - side, FACE))
                main = plus(main, link)
                echo.append(times(narrow(k, side, ECHO), stress))
                gain.append((vx[0], vy[0], vz[0]))
            else:
                link = [zero] * 3
                if side == 1:
                    main = plus(main, [0.25 * v for v in narrow(k, side, FACE)])
                echo.append([zero] * 3)
                gain.append((zero, zero, zero))
            sides.append((link, main, right))
        for side, (link, main, right) in enumerate(sides):
            near, far = narrow(k, side, NEAR), narrow(k, side, FAR)
            right = minus(right, plus(times(near, echo[side]), times(far, echo[1 - side])))
            inv = [1.0 / m for m in main]
            link = [-v * i for v, i in zip(link, inv)]
            far, right = times(far, inv), times(right, inv)
            rows.append((link, far, right) if side == 0 else (far, link, right))
        gains.append(gain)
        echoes.append(echo)
    done = []
    for n, (lo, hi, r) in enumerate(rows):
        if n == 0:
            done.append((hi, r))
            continue
        hs, rs = done[-1]
        inv = [1.0 / (1.0 - l * h) for l, h in zip(lo, hs)]
        done.append((times(hi, inv), times(minus(r, times(lo, rs)), inv)))
    ends = [None] * len(rows)
    ends[-1] = done[-1][1]
    for n in range(len(rows) - 2, -1, -1):
        hs, rs = done[n]
        ends[n] = minus(rs, times(hs, ends[n + 1]))

    def mine(values):
        chosen = values[0]
        for k in range(1, layers):
            chosen = [jnp.where(me == k, v, c) for v, c in zip(values[k], chosen)]
        return chosen

    first, last = mine(ends[0::2]), mine(ends[1::2])
    under = mine([[zero]] + [e[:1] for e in ends[1:-1:2]])[0]
    over = mine([e[:1] for e in ends[2::2]] + [[zero]])[0]
    first_seen = plus(first, mine([e[0] for e in echoes]))
    last_seen = plus(last, mine([e[1] for e in echoes]))
    gain = {0: mine([g[0] for g in gains]), LEVELS - 1: mine([g[1] for g in gains])}
    in_x, in_y, _ = rim_masks(where)

    def press(level):
        if level < 0:
            return [under]
        if level >= LEVELS:
            return [over]
        if level == 0:
            parts = first
        elif level == LEVELS - 1:
            parts = last
        else:
            parts = [
                inner[t, 0, level - 1]
                + inner[t, 1, level - 1] * first_seen[t]
                + inner[t, 2, level - 1] * last_seen[t]
                for t in range(3)
            ]
        return [parts[0], jnp.where(in_x, parts[1], 0.0), jnp.where(in_y, parts[2], 0.0)]

    before, now = press(-1), press(0)
    for level in range(LEVELS):
        after = press(level + 1)
        rows_at = pl.ds(level * ROWS, ROWS)
        pressure[rows_at, :] = now[0]
        grads = (
            diff_x(now[0], now[1])[0],
            diff_y(now[0], now[2])[0],
            after[0] - before[0],
        )
        for n in range(3):
            value = vel[n, rows_at, :] - 0.125 * grads[n]
            out[n, rows_at, :] = value + gain[level][n] if level in gain else value
        before, now = now, after


def final(where, vel, inner, told):
    smem = pl.BlockSpec(memory_space=pltpu.SMEM)
    vmem = pl.BlockSpec(memory_space=pltpu.VMEM)
    return pl.pallas_call(
        functools.partial(final_kernel, told.shape[0]),
        in_specs=[smem] + [vmem] * 3,
        out_shape=[
            jax.ShapeDtypeStruct((3, CELLS, COLS), f32),
            jax.ShapeDtypeStruct((CELLS, COLS), f32),
        ],
        compiler_params=pltpu.CompilerParams(vmem_limit_bytes=16 << 20),
        name="final",
    )(where, vel, inner, told)


def shift_up(block, axis):
    count = lax.axis_size(axis)
    return lax.ppermute(block, axis, [(i, i + 1) for i in range(count - 1)])


def shift_down(block, axis):
    count = lax.axis_size(axis)
    return lax.ppermute(block, axis, [(i + 1, i) for i in range(count - 1)])


def neighbours(block, axis):
    count, me = lax.axis_size(axis), lax.axis_index(axis)
    if count > 4:
        return jnp.stack([shift_up(block, axis), shift_down(block, axis)]), 0, 1
    stacked = lax.all_gather(block, axis, axis=0)
    return stacked, jnp.maximum(me - 1, 0), jnp.minimum(me + 1, count - 1)


def shards(trial, mean, cons, vel, wt, cell, flag, count, por, perm):
    por = por.reshape(CELLS, COLS)
    perm = perm.reshape(CELLS, COLS)
    sums, low, high = scatter(trial, mean, cons, vel, wt, cell, flag, count, por, perm)
    above = shift_down(low, "gx")
    below = shift_up(high, "gx")

    def ends(axis):
        me = lax.axis_index(axis)
        return [(me > 0).astype(i32), (me < lax.axis_size(axis) - 1).astype(i32)]

    has = ends("gx") + ends("gy")
    own = y_own(sums, por, perm)
    packs, y_low, y_high = neighbours(with_rims(own, below, above), "gy")
    where = jnp.stack(
        [jnp.asarray(v, i32) for v in [y_low, y_high] + has + [lax.axis_index("gz")]]
    )
    star, inner, told = local_solve(where, sums, por, perm, below, above, packs)
    velocity, pressure = final(where, star, inner, lax.all_gather(told, "gz", axis=0))
    return (
        velocity.reshape(3, LEVELS, ROWS, COLS),
        pressure.reshape(LEVELS, ROWS, COLS),
    )


def solution(mesh):
    points = ("gx", "gy", "gz")
    cells = P("gz", "gx", "gy")
    placed = (
        P(None, points), P(points), P(points), P(None, points), P(points), P(points), P(points),
        P(*points), cells, cells,
    )
    return jax.shard_map(
        shards,
        mesh=mesh,
        in_specs=placed,
        out_specs=(P(None, *cells), cells),
        check_vma=False,
    )
```

```python
import functools

import jax
import jax.numpy as jnp
from jax import lax
from jax.experimental import pallas as pl
from jax.experimental.pallas import tpu as pltpu
from jax.sharding import PartitionSpec as P

bf = jnp.bfloat16
f8 = jnp.float8_e4m3fn
f32 = jnp.float32
i32 = jnp.int32

LEVELS, ROWS, COLS = 16, 8, 128
CELLS = LEVELS * ROWS

ZX, YZ, ZZ, XX, YY, XY, MX, MY, MZ, MASS, POR, PERM = range(12)
FIELDS = 12
STRESS_ORDER = (5, 4, 2, 0, 1, 3)

X_ROWS = (
    (ZX, 0), (ZX, 1), (YZ, 0), (ZZ, 0), (PERM, 0), (POR, 0),
    (XX, 0), (XX, 1), (XX, 2), (XY, 0), (XY, 1), (YY, 0),
    (MX, 0), (MX, 1), (MY, 0), (MZ, 0), (MASS, 0), (MASS, 1),
)
X_DEEP = 3
X_SENT = len(X_ROWS) + X_DEEP
Y_DEPTH = {ZX: 1, YZ: 2, ZZ: 1, XX: 1, YY: 3, XY: 2, MX: 1, MY: 2, MZ: 1, MASS: 2, POR: 1, PERM: 1}
Y_PLACE = {}
_at = 0
for _f in range(FIELDS):
    Y_PLACE[_f] = _at + Y_DEPTH[_f]
    _at += 2 * Y_DEPTH[_f]
HALF = 64
FACE, MAIN, NEAR, FAR, RIGHT, SOURCE, ECHO, VELZ, STRESSZ = range(9)
WEIGHT, SHEARX, SHEARY = range(3)
NARROW, WIDE = 18, 6
MSG_X = 8 * (NARROW + WIDE)
MSG_X_WIDE = MSG_X + 8 * -(-NARROW // 4)
MSG_Y = MSG_X_WIDE + 8 * -(-WIDE // 2)
MSG_ROWS = MSG_Y + 8
LANE_WIDE = 2 * NARROW
LANE_CORNER = LANE_WIDE + 4 * WIDE


def tile_iota(dim):
    return lax.broadcasted_iota(i32, (ROWS, COLS), dim)


def turn(tile, shift, axis):
    shift %= tile.shape[axis]
    return tile if shift == 0 else pltpu.roll(tile, shift, axis)


def row_stress(trial, mean, cons, flag):
    part = lax.broadcasted_iota(i32, trial.shape, 0)
    size = jnp.sqrt(
        jnp.sum(trial * trial * jnp.where(part < 3, 1.5, 3.0), axis=0, keepdims=True)
    )
    yield_size = 1.2 * jnp.sqrt(mean * (cons - mean))
    factor = jnp.where(flag == 1, yield_size / jnp.maximum(size, 1.0), 1.0)
    return trial * factor - jnp.where(part < 3, mean, 0.0)


def point_rows(trial, mean, cons, vel, wt, flag, live):
    weight = jnp.where(live, wt, 0.0)
    stress = row_stress(trial, mean, cons, flag) * weight
    momentum = vel * weight
    rows = [stress[i : i + 1] for i in STRESS_ORDER]
    return rows + [momentum[i : i + 1] for i in range(3)] + [weight]


def cell_products(rows, place, groups):
    chunk = place.shape[1]
    row = (place >> 7) & (ROWS - 1)
    deep = jnp.where(row < ROWS // 2, row, ROWS - 1 - row)
    hi = deep * 16 + (row >> 2) * 8 + ((place >> 10) & 7)
    lo = ((place >> 13) << 7) | (place & (COLS - 1))

    def spread(row):
        return jnp.broadcast_to(row, (16, chunk)).astype(bf)

    one, zero = jnp.array(1, bf), jnp.array(0, bf)
    base = lax.broadcasted_iota(i32, (16, chunk), 0)

    def equal(index, count):
        index = spread(index.astype(f32))
        return [(base + b * 16).astype(f32).astype(bf) == index for b in range(count // 16)]

    mask = equal(hi, 64)
    right = jnp.concatenate([jnp.where(m, one, zero) for m in equal(lo, 256)], axis=0)
    tops = [row.astype(bf).astype(f32) for row in rows]
    parts = [spread(top) for top in tops]
    rests = [spread((row - top) * 256.0) for row, top in zip(rows, tops)]
    left = jnp.concatenate([jnp.where(mask[d], parts[f], zero) for f, d in groups], axis=0)
    left8 = jnp.concatenate([jnp.where(mask[d], rests[f], zero) for f, d in groups], axis=0)
    dims = (((1,), (1,)), ((), ()))
    prod = lax.dot_general(left, right, dims, preferred_element_type=f32)
    prod8 = lax.dot_general(
        left8.astype(f8), right.astype(f8), dims, preferred_element_type=f32
    )
    return prod + prod8 * (1 / 256.0)


POINT_ARGS = 8


def group_sums(chunk, groups, args, acc, arrived=lambda c: None):
    trial, mean, cons, vel, wt, cell, flag, count = args[:POINT_ARGS]

    def step(c, carry):
        arrived(c)
        at = pl.ds(pl.multiple_of(c * chunk, chunk), chunk)
        slot = c * chunk + lax.broadcasted_iota(i32, (1, chunk), 1)
        live = slot < count[0]
        rows = point_rows(
            trial[:, at], mean[:, at], cons[:, at], vel[:, at], wt[:, at], flag[:, at], live
        )
        prod = cell_products(rows, cell[:, at], groups)

        @pl.when(c == 0)
        def _():
            acc[...] = prod

        @pl.when(c > 0)
        def _():
            acc[...] += prod

        return carry

    lax.fori_loop(0, cell.shape[1] // chunk, step, 0)


def copied_sums(chunk, groups, sources, scratch, acc, sems):
    chunks = sources[1].shape[1] // chunk
    points = range(POINT_ARGS - 1)

    def copy(n, c):
        if n in points:
            at = pl.ds(pl.multiple_of(c * chunk, chunk), chunk)
            return pltpu.make_async_copy(sources[n].at[:, at], scratch[n].at[:, at], sems.at[n, c])
        return pltpu.make_async_copy(sources[n], scratch[n], sems.at[n, 0])

    others = range(POINT_ARGS, len(sources))
    copy(7, 0).start()
    for c in range(chunks):
        for n in points:
            copy(n, c).start()
    for n in others:
        copy(n, 0).start()
    copy(7, 0).wait()

    def arrived(c):
        for n in points:
            copy(n, c).wait()

    group_sums(chunk, groups, scratch, acc, arrived)
    for n in others:
        copy(n, 0).wait()


NEAR_GROUPS = tuple(x for x in X_ROWS if x[0] < 10)
FAR_GROUPS = tuple(
    (f, d) for f in range(10) for d in range(ROWS // 2) if (f, d) not in NEAR_GROUPS
)
HALVES = ((0, 0), (1, COLS))


def near_kernel(chunk, *refs):
    sources, (acc, low, high), scratch, sems = refs[:10], refs[10:13], refs[13:23], refs[23]
    copied_sums(chunk, NEAR_GROUPS, sources, scratch, acc, sems)
    por, perm = scratch[POINT_ARGS:]
    lane = lax.broadcasted_iota(i32, (LEVELS, COLS), 1)
    packed = [[jnp.zeros((LEVELS, COLS), f32)] * X_DEEP for _ in range(2)]
    for q, (field, deep) in enumerate(X_ROWS):
        at, depth = Y_PLACE[field] + HALF, Y_DEPTH[field]
        mask = (lane >= at - depth) & (lane < at + depth)
        for side, row in ((0, deep), (1, ROWS - 1 - deep)):
            face = (low, high)[side]
            if field < 10:
                first = NEAR_GROUPS.index((field, deep)) * 16 + side * 8
                for half, col in HALVES:
                    face[q, 8 * half : 8 * half + 8, :] = acc[first : first + 8, col : col + COLS]
            else:
                face[q] = (por if field == POR else perm)[pl.ds(row, LEVELS, stride=ROWS), :]
            packed[side][deep] = jnp.where(mask, turn(face[q], at, 1), packed[side][deep])
    for deep in range(X_DEEP):
        low[len(X_ROWS) + deep] = packed[0][deep]
        high[len(X_ROWS) + X_DEEP - 1 - deep] = packed[1][deep]


def far_kernel(chunk, *refs):
    args, out, own, acc = refs[:11], *refs[11:]
    group_sums(chunk, FAR_GROUPS, args, acc)
    por, perm, near = args[POINT_ARGS:]
    for groups, values in ((NEAR_GROUPS, near), (FAR_GROUPS, acc)):
        for n, (field, deep) in enumerate(groups):
            for side, row in ((0, deep), (1, ROWS - 1 - deep)):
                first = n * 16 + side * 8
                for half, col in HALVES:
                    rows = pl.ds(half * (CELLS // 2) + row, LEVELS // 2, stride=ROWS)
                    out[field, rows, :] = values[first : first + 8, col : col + COLS]
    lane = lax.broadcasted_iota(i32, (CELLS, COLS), 1)
    packed = jnp.zeros((CELLS, COLS), f32)
    for field in range(FIELDS):
        at, depth = Y_PLACE[field], Y_DEPTH[field]
        values = out[field] if field < 10 else (por if field == POR else perm)[...]
        mask = (lane >= at - depth) & (lane < at + depth)
        packed = jnp.where(mask, turn(values, at, 1), packed)
    own[...] = packed


def group_call(kernel, groups, args, outs, copied, scratch, grant, name):
    points = args[1].shape[1]
    chunk = points // 2 if points % 256 == 0 else points
    if copied:
        scratch = [pltpu.VMEM(v.shape, v.dtype) for v in args] + scratch
        scratch = scratch + [pltpu.SemaphoreType.DMA((len(args), points // chunk))]
    space = pltpu.HBM if copied else pltpu.VMEM
    return pl.pallas_call(
        functools.partial(kernel, chunk),
        in_specs=[pl.BlockSpec(memory_space=space)] * len(args),
        out_shape=[jax.ShapeDtypeStruct(shape, f32) for shape in outs],
        scratch_shapes=scratch,
        compiler_params=pltpu.CompilerParams(vmem_limit_bytes=grant << 20),
        cost_estimate=pl.CostEstimate(
            flops=2 * 24 * len(groups) * 256 * points, bytes_accessed=64 * points, transcendentals=0
        ),
        name=name,
    )(*args)


def point_args(trial, mean, cons, vel, wt, cell, flag, count):
    row = lambda v: v.reshape(1, -1)
    return (trial, row(mean), row(cons), vel, row(wt), row(cell), row(flag), count)


def near_sums(points, por, perm):
    acc = (16 * len(NEAR_GROUPS), 2 * COLS)
    faces = (X_SENT, LEVELS, COLS)
    outs = [acc, faces, faces]
    args = (*points, por, perm)
    return group_call(near_kernel, NEAR_GROUPS, args, outs, True, [], 56, "near_sums")


def far_sums(points, por, perm, near):
    acc = pltpu.VMEM((16 * len(FAR_GROUPS), 2 * COLS), f32)
    outs = [(10, CELLS, COLS), (CELLS, COLS)]
    args = (*points, por, perm, near)
    return group_call(far_kernel, FAR_GROUPS, args, outs, False, [acc], 44, "far_sums")


def with_rims(own, below, above):
    rows = X_DEEP * LEVELS
    first = above[len(X_ROWS) :].reshape(rows, COLS)
    last = below[len(X_ROWS) :].reshape(rows, COLS)
    return own + jnp.concatenate([first, jnp.zeros((CELLS - 2 * rows, COLS), f32), last])


def y_from_above(shape):
    lane = lax.broadcasted_iota(i32, shape, 1) & (HALF - 1)
    mask = lane < 0
    for field in range(FIELDS):
        at = Y_PLACE[field]
        mask |= (lane >= at) & (lane < at + Y_DEPTH[field])
    return mask


Y_LOW, Y_HIGH, X_HAS_LOW, X_HAS_HIGH, Y_HAS_LOW, Y_HAS_HIGH, LAYER = range(7)


def met(where, packs, from_above, rows):
    low = packs[where[Y_LOW], rows, :] * where[Y_HAS_LOW].astype(f32)
    high = packs[where[Y_HIGH], rows, :] * where[Y_HAS_HIGH].astype(f32)
    return jnp.where(from_above, high, low)


def diff_x(own, rim):
    row = tile_iota(0)
    own_up, rim_up = turn(own, -1, 0), turn(rim, -1, 0)
    own_down, rim_down = turn(own, 1, 0), turn(rim, 1, 0)
    top, bottom = row == ROWS - 1, row == 0
    return (
        jnp.where(top, rim_up, own_up) - jnp.where(bottom, rim_down, own_down),
        jnp.where(top, own_up, rim_up) - jnp.where(bottom, own_down, rim_down),
    )


def diff_y(own, rim):
    lane = tile_iota(1)
    own_up, rim_up = turn(own, -1, 1), turn(rim, -1, 1)
    own_down, rim_down = turn(own, 1, 1), turn(rim, 1, 1)
    top, bottom = lane == COLS - 1, lane == 0
    return (
        jnp.where(top, rim_up, own_up) - jnp.where(bottom, rim_down, own_down),
        jnp.where(top, own_up, rim_up) - jnp.where(bottom, own_down, rim_down),
    )


def ext_x(t):
    a0, a1 = diff_x(t[0], t[1])
    b0, b1 = diff_x(t[2], t[3])
    return [a0, a1, b0, b1]


def ext_y(t):
    a0, a2 = diff_y(t[0], t[2])
    b1, b3 = diff_y(t[1], t[3])
    return [a0, b1, a2, b3]


def rim_masks(where):
    row, lane = tile_iota(0), tile_iota(1)
    has = lambda low, high, test: jnp.where(test, where[high], where[low]) == 1
    in_x = has(X_HAS_LOW, X_HAS_HIGH, row < 4)
    in_y = has(Y_HAS_LOW, Y_HAS_HIGH, lane < HALF)
    return in_x, in_y, in_x & in_y


def local_kernel(where, sums, por, perm, below, above, packs, vel, inner, out, rim, corner):
    rim[...] = jnp.zeros_like(rim)
    for q, (field, deep) in enumerate(X_ROWS):
        rim[field, pl.ds(deep, LEVELS, stride=ROWS), :] = above[q]
        rim[field, pl.ds(ROWS - 1 - deep, LEVELS, stride=ROWS), :] = below[q]
    from_above = y_from_above((LEVELS, COLS))
    for slot in range(ROWS):
        rows = pl.ds(slot * LEVELS, LEVELS)
        corner[pl.ds(slot, LEVELS, stride=ROWS), :] = met(where, packs, from_above, rows)
    from_above = y_from_above((ROWS, COLS))
    in_x, in_y, in_xy = rim_masks(where)
    in_rims = (in_x, in_y, in_xy)
    inside = lambda t: t[:1] + [jnp.where(m, v, 0.0) for m, v in zip(in_rims, t[1:])]
    zero = jnp.zeros((ROWS, COLS), f32)

    def field_at(field, level):
        rows = pl.ds(level * ROWS, ROWS)
        at = Y_PLACE[field]
        own = sums[field, rows, :] if field < 10 else (por if field == POR else perm)[rows, :]
        lanes = met(where, packs, from_above, rows)
        return [
            own,
            rim[field, rows, :],
            turn(lanes, -at, 1),
            turn(corner[rows, :], -at - HALF, 1),
        ]

    memo = {}

    def get(field, level):
        if not 0 <= level < LEVELS:
            return [zero] * 4
        if (field, level) not in memo:
            memo[field, level] = field_at(field, level)
        return memo[field, level]

    def star(level):
        weight = inside([0.125 / jnp.maximum(m, 0.5) for m in get(MASS, level)])
        dz = lambda f: [u - d for u, d in zip(get(f, level + 1), get(f, level - 1))]
        forces = (
            (ext_x(get(XX, level)), ext_y(get(XY, level)), dz(ZX)),
            (ext_x(get(XY, level)), ext_y(get(YY, level)), dz(YZ)),
            (ext_x(get(ZX, level)), ext_y(get(YZ, level)), dz(ZZ)),
        )
        found = []
        for field, (fx, fy, fz) in zip((MX, MY, MZ), forces):
            found.append(
                [
                    (8.0 * m + (fx[n] + fy[n] + fz[n])) * weight[n]
                    for n, m in enumerate(get(field, level))
                ]
            )
        return found, weight

    def level_perm(level):
        own, x, y, _ = get(PERM, level)
        return [own] + [jnp.where(t > 0.0, t, 1.0) for t in (x, y)]

    def faces(level):
        pairs = zip(level_perm(level), level_perm(level + 1))
        return [0.5 * a * b / (a + b) for a, b in pairs]

    zero3 = [zero] * 3
    stars, weights = {}, {}
    stars[0], weights[0] = star(0)
    first_star = stars[0][2]
    wide = {0: [weights[0], get(ZX, 0), get(YZ, 0)]}
    stress = {0: get(ZZ, 0)}
    down = zero3
    kept, terms, sources, links = [], {}, {}, {}
    for level in range(LEVELS):
        if level + 1 < LEVELS:
            stars[level + 1], weights[level + 1] = star(level + 1)
        vx, vy, vz = stars[level]
        for n, part in enumerate((vx, vy, vz)):
            vel[n, pl.ds(level * ROWS, ROWS), :] = part[0]
        z_up = stars[level + 1][2] if level + 1 < LEVELS else zero3
        z_down = stars[level - 1][2] if level > 0 else zero3
        if level == LEVELS - 1:
            wide[1] = [weights[level], get(ZX, level), get(YZ, level)]
            stress[1] = get(ZZ, level)
        dx, dy = ext_x(vx), ext_y(vy)
        porosity = get(POR, level)[:3]
        up = faces(level) if level + 1 < LEVELS else zero3
        now = []
        for n in range(3):
            source = -0.0015 * (1.0 - porosity[n])
            right = source * (dx[n] + dy[n] + (z_up[n] - z_down[n]))
            main = 0.002 * porosity[n] + (down[n] + up[n])
            now.append((-down[n], main, -up[n], right, source))
        sources[level], links[level] = [t[4] for t in now], up
        down = up
        if level in (0, LEVELS - 1):
            terms[level] = now
        elif level == 1:
            kept.append([(lo, 1.0 / mid, hi, r) for lo, mid, hi, r, _ in now])
        else:
            rows = []
            for (lo, mid, hi, r, _), (f, inv, u, pr) in zip(now, kept[-1]):
                w = lo * inv
                rows.append((-w * f, 1.0 / (mid - w * u), hi, r - w * pr))
            kept.append(rows)
        for key in [k for k in memo if k[1] < level]:
            del memo[key]
    after = last_inner = None
    for n_row in range(len(kept) - 1, -1, -1):
        rows = []
        for t in range(3):
            f, inv, u, r = kept[n_row][t]
            if after is None:
                rows.append((r * inv, -f * inv, -u * inv))
            else:
                b2, f2, g2 = after[t]
                rows.append(((r - u * b2) * inv, -(f + u * f2) * inv, -u * g2 * inv))
            for m in range(3):
                inner[t, m, n_row] = rows[t][m]
        last_inner = last_inner or rows
        after = rows
    first_inner = after
    top = LEVELS - 1
    narrow = []
    for t in range(3):
        _, mid, hi, r, source = terms[0][t]
        b, f, g = first_inner[t]
        echo = sources[1][t] * weights[0][t] / links[0][t]
        face = level_perm(0)[t]
        mine = [face, mid + hi * f, hi * f, hi * g, r - hi * b, source, echo, first_star[t], stress[0][t]]
        lo, mid, _, r, source = terms[top][t]
        b, f, g = last_inner[t]
        echo = sources[top - 1][t] * weights[top][t] / links[top - 1][t]
        face = level_perm(top)[t]
        mine += [face, mid + lo * g, lo * g, lo * f, r - lo * b, source, echo, stars[top][2][t], stress[1][t]]
        narrow.append(mine)
    row, lane = tile_iota(0), tile_iota(1)
    x_parts = [zero] * -(-NARROW // 4)
    x_wide = [zero] * -(-WIDE // 2)
    y_part = zero

    def between(index, at, count):
        return (index >= at) & (index < at + count)

    for q in range(NARROW):
        own, x, y = (narrow[t][q] for t in range(3))
        out[8 * q : 8 * q + 8, :] = own
        at = 2 * q % 8
        x_parts[q // 4] = jnp.where(between(row, at, 2), turn(x, at + 1, 0), x_parts[q // 4])
        y_part = jnp.where(between(lane, 2 * q, 2), turn(y, 2 * q + 1, 1), y_part)
    for m, (own, x, y, xy) in enumerate(wide[0] + wide[1]):
        at = 8 * (NARROW + m)
        out[at : at + 8, :] = own
        at = 4 * (m % 2)
        x_wide[m // 2] = jnp.where(between(row, at, 4), turn(x, at + 2, 0), x_wide[m // 2])
        at = LANE_WIDE + 4 * m
        y_part = jnp.where(between(lane, at, 4), turn(y, at + 2, 1), y_part)
        at = LANE_CORNER + 2 * m
        y_part = jnp.where(between(lane, at, 2), turn(xy, at + 1, 1), y_part)
    for n, part in enumerate(x_parts):
        out[MSG_X + 8 * n : MSG_X + 8 * n + 8, :] = part
    for n, part in enumerate(x_wide):
        out[MSG_X_WIDE + 8 * n : MSG_X_WIDE + 8 * n + 8, :] = part
    out[MSG_Y : MSG_Y + 8, :] = y_part


def local_solve(where, sums, por, perm, below, above, packs):
    smem = pl.BlockSpec(memory_space=pltpu.SMEM)
    vmem = pl.BlockSpec(memory_space=pltpu.VMEM)
    return pl.pallas_call(
        local_kernel,
        in_specs=[smem] + [vmem] * 6,
        out_shape=[
            jax.ShapeDtypeStruct((3, CELLS, COLS), f32),
            jax.ShapeDtypeStruct((3, 3, LEVELS - 2, ROWS, COLS), f32),
            jax.ShapeDtypeStruct((MSG_ROWS, COLS), f32),
        ],
        scratch_shapes=[pltpu.VMEM((FIELDS, CELLS, COLS), f32), pltpu.VMEM((CELLS, COLS), f32)],
        compiler_params=pltpu.CompilerParams(vmem_limit_bytes=16 << 20),
        name="local_solve",
    )(where, sums, por, perm, below, above, packs)


def final_kernel(layers, where, vel, inner, told, out, pressure):
    me = where[LAYER]
    zero = jnp.zeros((ROWS, COLS), f32)

    def narrow(k, side, what):
        q = 9 * side + what
        at = MSG_X + 8 * (q // 4)
        return [
            told[k, 8 * q : 8 * q + 8, :],
            turn(told[k, at : at + 8, :], -(2 * q % 8 + 1), 0),
            turn(told[k, MSG_Y : MSG_Y + 8, :], -(2 * q + 1), 1),
        ]

    def wide(k, side, what):
        m = 3 * side + what
        own = 8 * (NARROW + m)
        at = MSG_X_WIDE + 8 * (m // 2)
        lanes = told[k, MSG_Y : MSG_Y + 8, :]
        return [
            told[k, own : own + 8, :],
            turn(told[k, at : at + 8, :], -(4 * (m % 2) + 2), 0),
            turn(lanes, -(LANE_WIDE + 4 * m + 2), 1),
            turn(lanes, -(LANE_CORNER + 2 * m + 1), 1),
        ]

    def times(*factors):
        product = factors[0]
        for factor in factors[1:]:
            product = [a * b for a, b in zip(product, factor)]
        return product

    def plus(*terms):
        total = terms[0]
        for term in terms[1:]:
            total = [a + b for a, b in zip(total, term)]
        return total

    def minus(a, b):
        return [x - y for x, y in zip(a, b)]

    def half_face(a, b):
        return [0.5 * x * y / (x + y) for x, y in zip(a, b)]

    rows, gains, echoes = [], [], []
    for k in range(layers):
        gain, echo = [], []
        sides = []
        for side, other in ((0, k - 1), (1, k + 1)):
            right = narrow(k, side, RIGHT)
            main = narrow(k, side, MAIN)
            if 0 <= other < layers:
                weight = wide(k, side, WEIGHT)
                sign = -1.0 if side == 0 else 1.0
                weight = [sign * w for w in weight]
                stress = narrow(other, 1 - side, STRESSZ)
                vx = times(weight, wide(other, 1 - side, SHEARX))
                vy = times(weight, wide(other, 1 - side, SHEARY))
                vz = times(weight, stress)
                change = times(wide(other, 1 - side, WEIGHT), narrow(k, side, STRESSZ))
                beyond = minus(narrow(other, 1 - side, VELZ), [sign * c for c in change])
                spread = plus(ext_x(vx)[:3], ext_y(vy)[:3], [sign * v for v in beyond])
                right = plus(right, times(narrow(k, side, SOURCE), spread))
                link = half_face(narrow(k, side, FACE), narrow(other, 1 - side, FACE))
                main = plus(main, link)
                echo.append(times(narrow(k, side, ECHO), stress))
                gain.append((vx[0], vy[0], vz[0]))
            else:
                link = [zero] * 3
                if side == 1:
                    main = plus(main, [0.25 * v for v in narrow(k, side, FACE)])
                echo.append([zero] * 3)
                gain.append((zero, zero, zero))
            sides.append((link, main, right))
        for side, (link, main, right) in enumerate(sides):
            near, far = narrow(k, side, NEAR), narrow(k, side, FAR)
            right = minus(right, plus(times(near, echo[side]), times(far, echo[1 - side])))
            inv = [1.0 / m for m in main]
            link = [-v * i for v, i in zip(link, inv)]
            far, right = times(far, inv), times(right, inv)
            rows.append((link, far, right) if side == 0 else (far, link, right))
        gains.append(gain)
        echoes.append(echo)
    done = []
    for n, (lo, hi, r) in enumerate(rows):
        if n == 0:
            done.append((hi, r))
            continue
        hs, rs = done[-1]
        inv = [1.0 / (1.0 - l * h) for l, h in zip(lo, hs)]
        done.append((times(hi, inv), times(minus(r, times(lo, rs)), inv)))
    ends = [None] * len(rows)
    ends[-1] = done[-1][1]
    for n in range(len(rows) - 2, -1, -1):
        hs, rs = done[n]
        ends[n] = minus(rs, times(hs, ends[n + 1]))

    def mine(values):
        chosen = values[0]
        for k in range(1, layers):
            chosen = [jnp.where(me == k, v, c) for v, c in zip(values[k], chosen)]
        return chosen

    first, last = mine(ends[0::2]), mine(ends[1::2])
    under = mine([[zero]] + [e[:1] for e in ends[1:-1:2]])[0]
    over = mine([e[:1] for e in ends[2::2]] + [[zero]])[0]
    first_seen = plus(first, mine([e[0] for e in echoes]))
    last_seen = plus(last, mine([e[1] for e in echoes]))
    gain = {0: mine([g[0] for g in gains]), LEVELS - 1: mine([g[1] for g in gains])}
    in_x, in_y, _ = rim_masks(where)

    def press(level):
        if level < 0:
            return [under]
        if level >= LEVELS:
            return [over]
        if level == 0:
            parts = first
        elif level == LEVELS - 1:
            parts = last
        else:
            parts = [
                inner[t, 0, level - 1]
                + inner[t, 1, level - 1] * first_seen[t]
                + inner[t, 2, level - 1] * last_seen[t]
                for t in range(3)
            ]
        return [parts[0], jnp.where(in_x, parts[1], 0.0), jnp.where(in_y, parts[2], 0.0)]

    before, now = press(-1), press(0)
    for level in range(LEVELS):
        after = press(level + 1)
        rows_at = pl.ds(level * ROWS, ROWS)
        pressure[rows_at, :] = now[0]
        grads = (
            diff_x(now[0], now[1])[0],
            diff_y(now[0], now[2])[0],
            after[0] - before[0],
        )
        for n in range(3):
            value = vel[n, rows_at, :] - 0.125 * grads[n]
            out[n, rows_at, :] = value + gain[level][n] if level in gain else value
        before, now = now, after


def final(where, vel, inner, told):
    smem = pl.BlockSpec(memory_space=pltpu.SMEM)
    vmem = pl.BlockSpec(memory_space=pltpu.VMEM)
    return pl.pallas_call(
        functools.partial(final_kernel, told.shape[0]),
        in_specs=[smem] + [vmem] * 3,
        out_shape=[
            jax.ShapeDtypeStruct((3, CELLS, COLS), f32),
            jax.ShapeDtypeStruct((CELLS, COLS), f32),
        ],
        compiler_params=pltpu.CompilerParams(vmem_limit_bytes=16 << 20),
        name="final",
    )(where, vel, inner, told)


def shift_up(block, axis):
    count = lax.axis_size(axis)
    return lax.ppermute(block, axis, [(i, i + 1) for i in range(count - 1)])


def shift_down(block, axis):
    count = lax.axis_size(axis)
    return lax.ppermute(block, axis, [(i + 1, i) for i in range(count - 1)])


def neighbours(block, axis):
    count, me = lax.axis_size(axis), lax.axis_index(axis)
    if count > 4:
        return jnp.stack([shift_up(block, axis), shift_down(block, axis)]), 0, 1
    stacked = lax.all_gather(block, axis, axis=0)
    return stacked, jnp.maximum(me - 1, 0), jnp.minimum(me + 1, count - 1)


def shards(trial, mean, cons, vel, wt, cell, flag, count, por, perm):
    por = por.reshape(CELLS, COLS)
    perm = perm.reshape(CELLS, COLS)
    points = point_args(trial, mean, cons, vel, wt, cell, flag, count)
    near, low, high = near_sums(points, por, perm)
    above = shift_down(low, "gx")
    below = shift_up(high, "gx")

    def ends(axis):
        me = lax.axis_index(axis)
        return [(me > 0).astype(i32), (me < lax.axis_size(axis) - 1).astype(i32)]

    has = ends("gx") + ends("gy")
    sums, own = far_sums(points, por, perm, near)
    packs, y_low, y_high = neighbours(with_rims(own, below, above), "gy")
    where = jnp.stack(
        [jnp.asarray(v, i32) for v in [y_low, y_high] + has + [lax.axis_index("gz")]]
    )
    star, inner, told = local_solve(where, sums, por, perm, below, above, packs)
    velocity, pressure = final(where, star, inner, lax.all_gather(told, "gz", axis=0))
    return (
        velocity.reshape(3, LEVELS, ROWS, COLS),
        pressure.reshape(LEVELS, ROWS, COLS),
    )


def solution(mesh):
    points = ("gx", "gy", "gz")
    cells = P("gz", "gx", "gy")
    placed = (
        P(None, points), P(points), P(points), P(None, points), P(points), P(points), P(points),
        P(*points), cells, cells,
    )
    return jax.shard_map(
        shards,
        mesh=mesh,
        in_specs=placed,
        out_specs=(P(None, *cells), cells),
        check_vma=False,
    )
```

```python
import functools

import jax
import jax.numpy as jnp
from jax import lax
from jax.experimental import pallas as pl
from jax.experimental.pallas import tpu as pltpu
from jax.sharding import PartitionSpec as P

bf = jnp.bfloat16
f8 = jnp.float8_e4m3fn
f32 = jnp.float32
i32 = jnp.int32

LEVELS, ROWS, COLS = 16, 8, 128
CELLS = LEVELS * ROWS

ZX, YZ, ZZ, XX, YY, XY, MX, MY, MZ, MASS, POR, PERM = range(12)
FIELDS = 12
STRESS_ORDER = (5, 4, 2, 0, 1, 3)

X_ROWS = (
    (ZX, 0), (ZX, 1), (YZ, 0), (ZZ, 0), (PERM, 0), (POR, 0),
    (XX, 0), (XX, 1), (XX, 2), (XY, 0), (XY, 1), (YY, 0),
    (MX, 0), (MX, 1), (MY, 0), (MZ, 0), (MASS, 0), (MASS, 1),
)
X_DEEP = 3
X_SENT = len(X_ROWS) + X_DEEP
Y_DEPTH = {ZX: 1, YZ: 2, ZZ: 1, XX: 1, YY: 3, XY: 2, MX: 1, MY: 2, MZ: 1, MASS: 2, POR: 1, PERM: 1}
Y_PLACE = {}
_at = 0
for _f in range(FIELDS):
    Y_PLACE[_f] = _at + Y_DEPTH[_f]
    _at += 2 * Y_DEPTH[_f]
HALF = 64
FACE, MAIN, NEAR, FAR, RIGHT, SOURCE, ECHO, VELZ, STRESSZ = range(9)
WEIGHT, SHEARX, SHEARY = range(3)
NARROW, WIDE = 18, 6
MSG_X = 8 * (NARROW + WIDE)
MSG_X_WIDE = MSG_X + 8 * -(-NARROW // 4)
MSG_Y = MSG_X_WIDE + 8 * -(-WIDE // 2)
MSG_ROWS = MSG_Y + 8
LANE_WIDE = 2 * NARROW
LANE_CORNER = LANE_WIDE + 4 * WIDE


def tile_iota(dim):
    return lax.broadcasted_iota(i32, (ROWS, COLS), dim)


def turn(tile, shift, axis):
    shift %= tile.shape[axis]
    return tile if shift == 0 else pltpu.roll(tile, shift, axis)


def row_stress(trial, mean, cons, flag):
    part = lax.broadcasted_iota(i32, trial.shape, 0)
    size = jnp.sqrt(
        jnp.sum(trial * trial * jnp.where(part < 3, 1.5, 3.0), axis=0, keepdims=True)
    )
    yield_size = 1.2 * jnp.sqrt(mean * (cons - mean))
    factor = jnp.where(flag == 1, yield_size / jnp.maximum(size, 1.0), 1.0)
    return trial * factor - jnp.where(part < 3, mean, 0.0)


def point_rows(trial, mean, cons, vel, wt, flag, live):
    weight = jnp.where(live, wt, 0.0)
    stress = row_stress(trial, mean, cons, flag) * weight
    momentum = vel * weight
    rows = [stress[i : i + 1] for i in STRESS_ORDER]
    return rows + [momentum[i : i + 1] for i in range(3)] + [weight]


def cell_products(rows, place, groups):
    chunk = place.shape[1]
    row = (place >> 7) & (ROWS - 1)
    deep = jnp.where(row < ROWS // 2, row, ROWS - 1 - row)
    hi = deep * 16 + (row >> 2) * 8 + ((place >> 10) & 7)
    lo = ((place >> 13) << 7) | (place & (COLS - 1))

    def spread(row):
        return jnp.broadcast_to(row, (16, chunk)).astype(bf)

    one, zero = jnp.array(1, bf), jnp.array(0, bf)
    base = lax.broadcasted_iota(i32, (16, chunk), 0)

    def equal(index, count):
        index = spread(index.astype(f32))
        return [(base + b * 16).astype(f32).astype(bf) == index for b in range(count // 16)]

    mask = equal(hi, 64)
    right = jnp.concatenate([jnp.where(m, one, zero) for m in equal(lo, 256)], axis=0)
    tops = [row.astype(bf).astype(f32) for row in rows]
    parts = [spread(top) for top in tops]
    rests = [spread((row - top) * 256.0) for row, top in zip(rows, tops)]
    left = jnp.concatenate([jnp.where(mask[d], parts[f], zero) for f, d in groups], axis=0)
    left8 = jnp.concatenate([jnp.where(mask[d], rests[f], zero) for f, d in groups], axis=0)
    dims = (((1,), (1,)), ((), ()))
    prod = lax.dot_general(left, right, dims, preferred_element_type=f32)
    prod8 = lax.dot_general(
        left8.astype(f8), right.astype(f8), dims, preferred_element_type=f32
    )
    return prod + prod8 * (1 / 256.0)


POINT_ARGS = 8


def group_sums(chunk, groups, args, acc, arrived=lambda c: None):
    trial, mean, cons, vel, wt, cell, flag, count = args[:POINT_ARGS]

    def step(c, carry):
        arrived(c)
        at = pl.ds(pl.multiple_of(c * chunk, chunk), chunk)
        slot = c * chunk + lax.broadcasted_iota(i32, (1, chunk), 1)
        live = slot < count[0]
        rows = point_rows(
            trial[:, at], mean[:, at], cons[:, at], vel[:, at], wt[:, at], flag[:, at], live
        )
        prod = cell_products(rows, cell[:, at], groups)

        @pl.when(c == 0)
        def _():
            acc[...] = prod

        @pl.when(c > 0)
        def _():
            acc[...] += prod

        return carry

    lax.fori_loop(0, cell.shape[1] // chunk, step, 0)


def copied_sums(chunk, groups, sources, scratch, acc, sems):
    chunks = sources[1].shape[1] // chunk
    points = range(POINT_ARGS - 1)

    def copy(n, c):
        if n in points:
            at = pl.ds(pl.multiple_of(c * chunk, chunk), chunk)
            return pltpu.make_async_copy(sources[n].at[:, at], scratch[n].at[:, at], sems.at[n, c])
        return pltpu.make_async_copy(sources[n], scratch[n], sems.at[n, 0])

    others = range(POINT_ARGS, len(sources))
    copy(7, 0).start()
    for c in range(chunks):
        for n in points:
            copy(n, c).start()
    for n in others:
        copy(n, 0).start()
    copy(7, 0).wait()

    def arrived(c):
        for n in points:
            copy(n, c).wait()

    group_sums(chunk, groups, scratch, acc, arrived)
    for n in others:
        copy(n, 0).wait()


NEAR_GROUPS = tuple(x for x in X_ROWS if x[0] < 10)
FAR_GROUPS = tuple(
    (f, d) for f in range(10) for d in range(ROWS // 2) if (f, d) not in NEAR_GROUPS
)
HALVES = ((0, 0), (1, COLS))


def near_kernel(chunk, *refs):
    sources, (acc, low, high), scratch, sems = refs[:10], refs[10:13], refs[13:23], refs[23]
    copied_sums(chunk, NEAR_GROUPS, sources, scratch, acc, sems)
    por, perm = scratch[POINT_ARGS:]
    lane = lax.broadcasted_iota(i32, (LEVELS, COLS), 1)
    packed = [[jnp.zeros((LEVELS, COLS), f32)] * X_DEEP for _ in range(2)]
    for q, (field, deep) in enumerate(X_ROWS):
        at, depth = Y_PLACE[field] + HALF, Y_DEPTH[field]
        mask = (lane >= at - depth) & (lane < at + depth)
        for side, row in ((0, deep), (1, ROWS - 1 - deep)):
            face = (low, high)[side]
            if field < 10:
                first = NEAR_GROUPS.index((field, deep)) * 16 + side * 8
                for half, col in HALVES:
                    face[q, 8 * half : 8 * half + 8, :] = acc[first : first + 8, col : col + COLS]
            else:
                face[q] = (por if field == POR else perm)[pl.ds(row, LEVELS, stride=ROWS), :]
            packed[side][deep] = jnp.where(mask, turn(face[q], at, 1), packed[side][deep])
    for deep in range(X_DEEP):
        low[len(X_ROWS) + deep] = packed[0][deep]
        high[len(X_ROWS) + X_DEEP - 1 - deep] = packed[1][deep]


def far_kernel(chunk, *refs):
    args, acc = refs[:POINT_ARGS], refs[POINT_ARGS]
    group_sums(chunk, FAR_GROUPS, args, acc)


def assemble_kernel(near, far, por, perm, out, own):
    for groups, values in ((NEAR_GROUPS, near), (FAR_GROUPS, far)):
        for n, (field, deep) in enumerate(groups):
            for side, row in ((0, deep), (1, ROWS - 1 - deep)):
                first = n * 16 + side * 8
                for half, col in HALVES:
                    rows = pl.ds(half * (CELLS // 2) + row, LEVELS // 2, stride=ROWS)
                    out[field, rows, :] = values[first : first + 8, col : col + COLS]
    lane = lax.broadcasted_iota(i32, (CELLS, COLS), 1)
    packed = jnp.zeros((CELLS, COLS), f32)
    for field in range(FIELDS):
        at, depth = Y_PLACE[field], Y_DEPTH[field]
        values = out[field] if field < 10 else (por if field == POR else perm)[...]
        mask = (lane >= at - depth) & (lane < at + depth)
        packed = jnp.where(mask, turn(values, at, 1), packed)
    own[...] = packed


def assemble(near, far, por, perm):
    return pl.pallas_call(
        assemble_kernel,
        out_shape=[
            jax.ShapeDtypeStruct((10, CELLS, COLS), f32),
            jax.ShapeDtypeStruct((CELLS, COLS), f32),
        ],
        compiler_params=pltpu.CompilerParams(vmem_limit_bytes=8 << 20),
        cost_estimate=pl.CostEstimate(flops=4000000, bytes_accessed=1500000, transcendentals=0),
        name="assemble",
    )(near, far, por, perm)


def group_call(kernel, groups, args, outs, copied, scratch, grant, name):
    points = args[1].shape[1]
    chunk = points // 2 if points % 256 == 0 else points
    if copied:
        scratch = [pltpu.VMEM(v.shape, v.dtype) for v in args] + scratch
        scratch = scratch + [pltpu.SemaphoreType.DMA((len(args), points // chunk))]
    space = pltpu.HBM if copied else pltpu.VMEM
    return pl.pallas_call(
        functools.partial(kernel, chunk),
        in_specs=[pl.BlockSpec(memory_space=space)] * len(args),
        out_shape=[jax.ShapeDtypeStruct(shape, f32) for shape in outs],
        scratch_shapes=scratch,
        compiler_params=pltpu.CompilerParams(vmem_limit_bytes=grant << 20),
        cost_estimate=pl.CostEstimate(
            flops=2 * 24 * len(groups) * 256 * points, bytes_accessed=64 * points, transcendentals=0
        ),
        name=name,
    )(*args)


def point_args(trial, mean, cons, vel, wt, cell, flag, count):
    row = lambda v: v.reshape(1, -1)
    return (trial, row(mean), row(cons), vel, row(wt), row(cell), row(flag), count)


def near_sums(points, por, perm):
    acc = (16 * len(NEAR_GROUPS), 2 * COLS)
    faces = (X_SENT, LEVELS, COLS)
    outs = [acc, faces, faces]
    args = (*points, por, perm)
    return group_call(near_kernel, NEAR_GROUPS, args, outs, True, [], 56, "near_sums")


def far_sums(points):
    outs = [(16 * len(FAR_GROUPS), 2 * COLS)]
    return group_call(far_kernel, FAR_GROUPS, points, outs, False, [], 44, "far_sums")[0]


def with_rims(own, below, above):
    rows = X_DEEP * LEVELS
    first = above[len(X_ROWS) :].reshape(rows, COLS)
    last = below[len(X_ROWS) :].reshape(rows, COLS)
    return own + jnp.concatenate([first, jnp.zeros((CELLS - 2 * rows, COLS), f32), last])


def y_from_above(shape):
    lane = lax.broadcasted_iota(i32, shape, 1) & (HALF - 1)
    mask = lane < 0
    for field in range(FIELDS):
        at = Y_PLACE[field]
        mask |= (lane >= at) & (lane < at + Y_DEPTH[field])
    return mask


Y_LOW, Y_HIGH, X_HAS_LOW, X_HAS_HIGH, Y_HAS_LOW, Y_HAS_HIGH, LAYER = range(7)


def met(where, packs, from_above, rows):
    low = packs[where[Y_LOW], rows, :] * where[Y_HAS_LOW].astype(f32)
    high = packs[where[Y_HIGH], rows, :] * where[Y_HAS_HIGH].astype(f32)
    return jnp.where(from_above, high, low)


def diff_x(own, rim):
    row = tile_iota(0)
    own_up, rim_up = turn(own, -1, 0), turn(rim, -1, 0)
    own_down, rim_down = turn(own, 1, 0), turn(rim, 1, 0)
    top, bottom = row == ROWS - 1, row == 0
    return (
        jnp.where(top, rim_up, own_up) - jnp.where(bottom, rim_down, own_down),
        jnp.where(top, own_up, rim_up) - jnp.where(bottom, own_down, rim_down),
    )


def diff_y(own, rim):
    lane = tile_iota(1)
    own_up, rim_up = turn(own, -1, 1), turn(rim, -1, 1)
    own_down, rim_down = turn(own, 1, 1), turn(rim, 1, 1)
    top, bottom = lane == COLS - 1, lane == 0
    return (
        jnp.where(top, rim_up, own_up) - jnp.where(bottom, rim_down, own_down),
        jnp.where(top, own_up, rim_up) - jnp.where(bottom, own_down, rim_down),
    )


def ext_x(t):
    a0, a1 = diff_x(t[0], t[1])
    b0, b1 = diff_x(t[2], t[3])
    return [a0, a1, b0, b1]


def ext_y(t):
    a0, a2 = diff_y(t[0], t[2])
    b1, b3 = diff_y(t[1], t[3])
    return [a0, b1, a2, b3]


def rim_masks(where):
    row, lane = tile_iota(0), tile_iota(1)
    has = lambda low, high, test: jnp.where(test, where[high], where[low]) == 1
    in_x = has(X_HAS_LOW, X_HAS_HIGH, row < 4)
    in_y = has(Y_HAS_LOW, Y_HAS_HIGH, lane < HALF)
    return in_x, in_y, in_x & in_y


def local_kernel(where, sums, por, perm, below, above, packs, vel, inner, out, rim, corner):
    rim[...] = jnp.zeros_like(rim)
    for q, (field, deep) in enumerate(X_ROWS):
        rim[field, pl.ds(deep, LEVELS, stride=ROWS), :] = above[q]
        rim[field, pl.ds(ROWS - 1 - deep, LEVELS, stride=ROWS), :] = below[q]
    from_above = y_from_above((LEVELS, COLS))
    for slot in range(ROWS):
        rows = pl.ds(slot * LEVELS, LEVELS)
        corner[pl.ds(slot, LEVELS, stride=ROWS), :] = met(where, packs, from_above, rows)
    from_above = y_from_above((ROWS, COLS))
    in_x, in_y, in_xy = rim_masks(where)
    in_rims = (in_x, in_y, in_xy)
    inside = lambda t: t[:1] + [jnp.where(m, v, 0.0) for m, v in zip(in_rims, t[1:])]
    zero = jnp.zeros((ROWS, COLS), f32)

    def field_at(field, level):
        rows = pl.ds(level * ROWS, ROWS)
        at = Y_PLACE[field]
        own = sums[field, rows, :] if field < 10 else (por if field == POR else perm)[rows, :]
        if level not in merged:
            merged[level] = met(where, packs, from_above, rows)
        lanes = merged[level]
        return [
            own,
            rim[field, rows, :],
            turn(lanes, -at, 1),
            turn(corner[rows, :], -at - HALF, 1),
        ]

    memo, merged = {}, {}

    def get(field, level):
        if not 0 <= level < LEVELS:
            return [zero] * 4
        if (field, level) not in memo:
            memo[field, level] = field_at(field, level)
        return memo[field, level]

    def star(level):
        weight = inside([0.125 / jnp.maximum(m, 0.5) for m in get(MASS, level)])
        dz = lambda f: [u - d for u, d in zip(get(f, level + 1), get(f, level - 1))]
        forces = (
            (ext_x(get(XX, level)), ext_y(get(XY, level)), dz(ZX)),
            (ext_x(get(XY, level)), ext_y(get(YY, level)), dz(YZ)),
            (ext_x(get(ZX, level)), ext_y(get(YZ, level)), dz(ZZ)),
        )
        found = []
        for field, (fx, fy, fz) in zip((MX, MY, MZ), forces):
            found.append(
                [
                    (8.0 * m + (fx[n] + fy[n] + fz[n])) * weight[n]
                    for n, m in enumerate(get(field, level))
                ]
            )
        return found, weight

    def level_perm(level):
        own, x, y, _ = get(PERM, level)
        return [own] + [jnp.where(t > 0.0, t, 1.0) for t in (x, y)]

    def faces(level):
        pairs = zip(level_perm(level), level_perm(level + 1))
        return [0.5 * a * b / (a + b) for a, b in pairs]

    zero3 = [zero] * 3
    stars, weights = {}, {}
    stars[0], weights[0] = star(0)
    first_star = stars[0][2]
    wide = {0: [weights[0], get(ZX, 0), get(YZ, 0)]}
    stress = {0: get(ZZ, 0)}
    down = zero3
    kept, terms, sources, links = [], {}, {}, {}
    for level in range(LEVELS):
        if level + 1 < LEVELS:
            stars[level + 1], weights[level + 1] = star(level + 1)
        vx, vy, vz = stars[level]
        for n, part in enumerate((vx, vy, vz)):
            vel[n, pl.ds(level * ROWS, ROWS), :] = part[0]
        z_up = stars[level + 1][2] if level + 1 < LEVELS else zero3
        z_down = stars[level - 1][2] if level > 0 else zero3
        if level == LEVELS - 1:
            wide[1] = [weights[level], get(ZX, level), get(YZ, level)]
            stress[1] = get(ZZ, level)
        dx, dy = ext_x(vx), ext_y(vy)
        porosity = get(POR, level)[:3]
        up = faces(level) if level + 1 < LEVELS else zero3
        now = []
        for n in range(3):
            source = -0.0015 * (1.0 - porosity[n])
            right = source * (dx[n] + dy[n] + (z_up[n] - z_down[n]))
            main = 0.002 * porosity[n] + (down[n] + up[n])
            now.append((-down[n], main, -up[n], right, source))
        sources[level], links[level] = [t[4] for t in now], up
        down = up
        if level in (0, LEVELS - 1):
            terms[level] = now
        elif level == 1:
            kept.append([(lo, 1.0 / mid, hi, r) for lo, mid, hi, r, _ in now])
        else:
            rows = []
            for (lo, mid, hi, r, _), (f, inv, u, pr) in zip(now, kept[-1]):
                w = lo * inv
                rows.append((-w * f, 1.0 / (mid - w * u), hi, r - w * pr))
            kept.append(rows)
        for key in [k for k in memo if k[1] < level]:
            del memo[key]
    after = last_inner = None
    for n_row in range(len(kept) - 1, -1, -1):
        rows = []
        for t in range(3):
            f, inv, u, r = kept[n_row][t]
            if after is None:
                rows.append((r * inv, -f * inv, -u * inv))
            else:
                b2, f2, g2 = after[t]
                rows.append(((r - u * b2) * inv, -(f + u * f2) * inv, -u * g2 * inv))
            for m in range(3):
                inner[t, m, n_row] = rows[t][m]
        last_inner = last_inner or rows
        after = rows
    first_inner = after
    top = LEVELS - 1
    narrow = []
    for t in range(3):
        _, mid, hi, r, source = terms[0][t]
        b, f, g = first_inner[t]
        echo = sources[1][t] * weights[0][t] / links[0][t]
        face = level_perm(0)[t]
        mine = [face, mid + hi * f, hi * f, hi * g, r - hi * b, source, echo, first_star[t], stress[0][t]]
        lo, mid, _, r, source = terms[top][t]
        b, f, g = last_inner[t]
        echo = sources[top - 1][t] * weights[top][t] / links[top - 1][t]
        face = level_perm(top)[t]
        mine += [face, mid + lo * g, lo * g, lo * f, r - lo * b, source, echo, stars[top][2][t], stress[1][t]]
        narrow.append(mine)
    row, lane = tile_iota(0), tile_iota(1)
    x_parts = [zero] * -(-NARROW // 4)
    x_wide = [zero] * -(-WIDE // 2)
    y_part = zero

    def between(index, at, count):
        return (index >= at) & (index < at + count)

    for q in range(NARROW):
        own, x, y = (narrow[t][q] for t in range(3))
        out[8 * q : 8 * q + 8, :] = own
        at = 2 * q % 8
        x_parts[q // 4] = jnp.where(between(row, at, 2), turn(x, at + 1, 0), x_parts[q // 4])
        y_part = jnp.where(between(lane, 2 * q, 2), turn(y, 2 * q + 1, 1), y_part)
    for m, (own, x, y, xy) in enumerate(wide[0] + wide[1]):
        at = 8 * (NARROW + m)
        out[at : at + 8, :] = own
        at = 4 * (m % 2)
        x_wide[m // 2] = jnp.where(between(row, at, 4), turn(x, at + 2, 0), x_wide[m // 2])
        at = LANE_WIDE + 4 * m
        y_part = jnp.where(between(lane, at, 4), turn(y, at + 2, 1), y_part)
        at = LANE_CORNER + 2 * m
        y_part = jnp.where(between(lane, at, 2), turn(xy, at + 1, 1), y_part)
    for n, part in enumerate(x_parts):
        out[MSG_X + 8 * n : MSG_X + 8 * n + 8, :] = part
    for n, part in enumerate(x_wide):
        out[MSG_X_WIDE + 8 * n : MSG_X_WIDE + 8 * n + 8, :] = part
    out[MSG_Y : MSG_Y + 8, :] = y_part


def local_solve(where, sums, por, perm, below, above, packs):
    smem = pl.BlockSpec(memory_space=pltpu.SMEM)
    vmem = pl.BlockSpec(memory_space=pltpu.VMEM)
    return pl.pallas_call(
        local_kernel,
        in_specs=[smem] + [vmem] * 6,
        out_shape=[
            jax.ShapeDtypeStruct((3, CELLS, COLS), f32),
            jax.ShapeDtypeStruct((3, 3, LEVELS - 2, ROWS, COLS), f32),
            jax.ShapeDtypeStruct((MSG_ROWS, COLS), f32),
        ],
        scratch_shapes=[pltpu.VMEM((FIELDS, CELLS, COLS), f32), pltpu.VMEM((CELLS, COLS), f32)],
        compiler_params=pltpu.CompilerParams(vmem_limit_bytes=16 << 20),
        name="local_solve",
    )(where, sums, por, perm, below, above, packs)


def final_kernel(layers, where, vel, inner, told, out, pressure):
    me = where[LAYER]
    zero = jnp.zeros((ROWS, COLS), f32)

    def narrow(k, side, what):
        q = 9 * side + what
        at = MSG_X + 8 * (q // 4)
        return [
            told[k, 8 * q : 8 * q + 8, :],
            turn(told[k, at : at + 8, :], -(2 * q % 8 + 1), 0),
            turn(told[k, MSG_Y : MSG_Y + 8, :], -(2 * q + 1), 1),
        ]

    def wide(k, side, what):
        m = 3 * side + what
        own = 8 * (NARROW + m)
        at = MSG_X_WIDE + 8 * (m // 2)
        lanes = told[k, MSG_Y : MSG_Y + 8, :]
        return [
            told[k, own : own + 8, :],
            turn(told[k, at : at + 8, :], -(4 * (m % 2) + 2), 0),
            turn(lanes, -(LANE_WIDE + 4 * m + 2), 1),
            turn(lanes, -(LANE_CORNER + 2 * m + 1), 1),
        ]

    def times(*factors):
        product = factors[0]
        for factor in factors[1:]:
            product = [a * b for a, b in zip(product, factor)]
        return product

    def plus(*terms):
        total = terms[0]
        for term in terms[1:]:
            total = [a + b for a, b in zip(total, term)]
        return total

    def minus(a, b):
        return [x - y for x, y in zip(a, b)]

    def half_face(a, b):
        return [0.5 * x * y / (x + y) for x, y in zip(a, b)]

    rows, gains, echoes = [], [], []
    for k in range(layers):
        gain, echo = [], []
        sides = []
        for side, other in ((0, k - 1), (1, k + 1)):
            right = narrow(k, side, RIGHT)
            main = narrow(k, side, MAIN)
            if 0 <= other < layers:
                weight = wide(k, side, WEIGHT)
                sign = -1.0 if side == 0 else 1.0
                weight = [sign * w for w in weight]
                stress = narrow(other, 1 - side, STRESSZ)
                vx = times(weight, wide(other, 1 - side, SHEARX))
                vy = times(weight, wide(other, 1 - side, SHEARY))
                vz = times(weight, stress)
                change = times(wide(other, 1 - side, WEIGHT), narrow(k, side, STRESSZ))
                beyond = minus(narrow(other, 1 - side, VELZ), [sign * c for c in change])
                spread = plus(ext_x(vx)[:3], ext_y(vy)[:3], [sign * v for v in beyond])
                right = plus(right, times(narrow(k, side, SOURCE), spread))
                link = half_face(narrow(k, side, FACE), narrow(other, 1 - side, FACE))
                main = plus(main, link)
                echo.append(times(narrow(k, side, ECHO), stress))
                gain.append((vx[0], vy[0], vz[0]))
            else:
                link = [zero] * 3
                if side == 1:
                    main = plus(main, [0.25 * v for v in narrow(k, side, FACE)])
                echo.append([zero] * 3)
                gain.append((zero, zero, zero))
            sides.append((link, main, right))
        for side, (link, main, right) in enumerate(sides):
            near, far = narrow(k, side, NEAR), narrow(k, side, FAR)
            right = minus(right, plus(times(near, echo[side]), times(far, echo[1 - side])))
            inv = [1.0 / m for m in main]
            link = [-v * i for v, i in zip(link, inv)]
            far, right = times(far, inv), times(right, inv)
            rows.append((link, far, right) if side == 0 else (far, link, right))
        gains.append(gain)
        echoes.append(echo)
    done = []
    for n, (lo, hi, r) in enumerate(rows):
        if n == 0:
            done.append((hi, r))
            continue
        hs, rs = done[-1]
        inv = [1.0 / (1.0 - l * h) for l, h in zip(lo, hs)]
        done.append((times(hi, inv), times(minus(r, times(lo, rs)), inv)))
    ends = [None] * len(rows)
    ends[-1] = done[-1][1]
    for n in range(len(rows) - 2, -1, -1):
        hs, rs = done[n]
        ends[n] = minus(rs, times(hs, ends[n + 1]))

    def mine(values):
        chosen = values[0]
        for k in range(1, layers):
            chosen = [jnp.where(me == k, v, c) for v, c in zip(values[k], chosen)]
        return chosen

    first, last = mine(ends[0::2]), mine(ends[1::2])
    under = mine([[zero]] + [e[:1] for e in ends[1:-1:2]])[0]
    over = mine([e[:1] for e in ends[2::2]] + [[zero]])[0]
    first_seen = plus(first, mine([e[0] for e in echoes]))
    last_seen = plus(last, mine([e[1] for e in echoes]))
    gain = {0: mine([g[0] for g in gains]), LEVELS - 1: mine([g[1] for g in gains])}
    in_x, in_y, _ = rim_masks(where)

    def press(level):
        if level < 0:
            return [under]
        if level >= LEVELS:
            return [over]
        if level == 0:
            parts = first
        elif level == LEVELS - 1:
            parts = last
        else:
            parts = [
                inner[t, 0, level - 1]
                + inner[t, 1, level - 1] * first_seen[t]
                + inner[t, 2, level - 1] * last_seen[t]
                for t in range(3)
            ]
        return [parts[0], jnp.where(in_x, parts[1], 0.0), jnp.where(in_y, parts[2], 0.0)]

    before, now = press(-1), press(0)
    for level in range(LEVELS):
        after = press(level + 1)
        rows_at = pl.ds(level * ROWS, ROWS)
        pressure[rows_at, :] = now[0]
        grads = (
            diff_x(now[0], now[1])[0],
            diff_y(now[0], now[2])[0],
            after[0] - before[0],
        )
        for n in range(3):
            value = vel[n, rows_at, :] - 0.125 * grads[n]
            out[n, rows_at, :] = value + gain[level][n] if level in gain else value
        before, now = now, after


def final(where, vel, inner, told):
    smem = pl.BlockSpec(memory_space=pltpu.SMEM)
    vmem = pl.BlockSpec(memory_space=pltpu.VMEM)
    return pl.pallas_call(
        functools.partial(final_kernel, told.shape[0]),
        in_specs=[smem] + [vmem] * 3,
        out_shape=[
            jax.ShapeDtypeStruct((3, CELLS, COLS), f32),
            jax.ShapeDtypeStruct((CELLS, COLS), f32),
        ],
        compiler_params=pltpu.CompilerParams(vmem_limit_bytes=16 << 20),
        name="final",
    )(where, vel, inner, told)


def shift_up(block, axis):
    count = lax.axis_size(axis)
    return lax.ppermute(block, axis, [(i, i + 1) for i in range(count - 1)])


def shift_down(block, axis):
    count = lax.axis_size(axis)
    return lax.ppermute(block, axis, [(i + 1, i) for i in range(count - 1)])


def neighbours(block, axis):
    count, me = lax.axis_size(axis), lax.axis_index(axis)
    if count > 4:
        return jnp.stack([shift_up(block, axis), shift_down(block, axis)]), 0, 1
    stacked = lax.all_gather(block, axis, axis=0)
    return stacked, jnp.maximum(me - 1, 0), jnp.minimum(me + 1, count - 1)


def shards(trial, mean, cons, vel, wt, cell, flag, count, por, perm):
    por = por.reshape(CELLS, COLS)
    perm = perm.reshape(CELLS, COLS)
    points = point_args(trial, mean, cons, vel, wt, cell, flag, count)
    near, low, high = near_sums(points, por, perm)
    above = shift_down(low, "gx")
    below = shift_up(high, "gx")

    def ends(axis):
        me = lax.axis_index(axis)
        return [(me > 0).astype(i32), (me < lax.axis_size(axis) - 1).astype(i32)]

    has = ends("gx") + ends("gy")
    sums, own = assemble(near, far_sums(points), por, perm)
    packs, y_low, y_high = neighbours(with_rims(own, below, above), "gy")
    where = jnp.stack(
        [jnp.asarray(v, i32) for v in [y_low, y_high] + has + [lax.axis_index("gz")]]
    )
    star, inner, told = local_solve(where, sums, por, perm, below, above, packs)
    velocity, pressure = final(where, star, inner, lax.all_gather(told, "gz", axis=0))
    return (
        velocity.reshape(3, LEVELS, ROWS, COLS),
        pressure.reshape(LEVELS, ROWS, COLS),
    )


def solution(mesh):
    points = ("gx", "gy", "gz")
    cells = P("gz", "gx", "gy")
    placed = (
        P(None, points), P(points), P(points), P(None, points), P(points), P(points), P(points),
        P(*points), cells, cells,
    )
    return jax.shard_map(
        shards,
        mesh=mesh,
        in_specs=placed,
        out_specs=(P(None, *cells), cells),
        check_vma=False,
    )
```

```python
import functools

import jax
import jax.numpy as jnp
from jax import lax
from jax.experimental import pallas as pl
from jax.experimental.pallas import tpu as pltpu
from jax.sharding import PartitionSpec as P

bf = jnp.bfloat16
f8 = jnp.float8_e4m3fn
f32 = jnp.float32
i32 = jnp.int32

LEVELS, ROWS, COLS = 16, 8, 128
CELLS = LEVELS * ROWS

ZX, YZ, ZZ, XX, YY, XY, MX, MY, MZ, MASS, POR, PERM = range(12)
FIELDS = 12
STRESS_ORDER = (5, 4, 2, 0, 1, 3)

X_ROWS = (
    (ZX, 0), (ZX, 1), (YZ, 0), (ZZ, 0), (PERM, 0), (POR, 0),
    (XX, 0), (XX, 1), (XX, 2), (XY, 0), (XY, 1), (YY, 0),
    (MX, 0), (MX, 1), (MY, 0), (MZ, 0), (MASS, 0), (MASS, 1),
)
X_DEEP = 3
X_SENT = len(X_ROWS) + X_DEEP
Y_DEPTH = {ZX: 1, YZ: 2, ZZ: 1, XX: 1, YY: 3, XY: 2, MX: 1, MY: 2, MZ: 1, MASS: 2, POR: 1, PERM: 1}
Y_PLACE = {}
_at = 0
for _f in range(FIELDS):
    Y_PLACE[_f] = _at + Y_DEPTH[_f]
    _at += 2 * Y_DEPTH[_f]
HALF = 64
FACE, MAIN, NEAR, FAR, RIGHT, SOURCE, ECHO, VELZ, STRESSZ = range(9)
WEIGHT, SHEARX, SHEARY = range(3)
NARROW, WIDE = 18, 6
MSG_X = 8 * (NARROW + WIDE)
MSG_X_WIDE = MSG_X + 8 * -(-NARROW // 4)
MSG_Y = MSG_X_WIDE + 8 * -(-WIDE // 2)
MSG_ROWS = MSG_Y + 8
LANE_WIDE = 2 * NARROW
LANE_CORNER = LANE_WIDE + 4 * WIDE


def tile_iota(dim):
    return lax.broadcasted_iota(i32, (ROWS, COLS), dim)


def turn(tile, shift, axis):
    shift %= tile.shape[axis]
    return tile if shift == 0 else pltpu.roll(tile, shift, axis)


def row_stress(trial, mean, cons, flag):
    part = lax.broadcasted_iota(i32, trial.shape, 0)
    size = jnp.sqrt(
        jnp.sum(trial * trial * jnp.where(part < 3, 1.5, 3.0), axis=0, keepdims=True)
    )
    yield_size = 1.2 * jnp.sqrt(mean * (cons - mean))
    factor = jnp.where(flag == 1, yield_size / jnp.maximum(size, 1.0), 1.0)
    return trial * factor - jnp.where(part < 3, mean, 0.0)


def point_rows(trial, mean, cons, vel, wt, flag, live):
    weight = jnp.where(live, wt, 0.0)
    stress = row_stress(trial, mean, cons, flag) * weight
    momentum = vel * weight
    rows = [stress[i : i + 1] for i in STRESS_ORDER]
    return rows + [momentum[i : i + 1] for i in range(3)] + [weight]


def cell_products(rows, place, groups):
    chunk = place.shape[1]
    row = (place >> 7) & (ROWS - 1)
    deep = jnp.where(row < ROWS // 2, row, ROWS - 1 - row)
    hi = deep * 16 + (row >> 2) * 8 + ((place >> 10) & 7)
    lo = ((place >> 13) << 7) | (place & (COLS - 1))

    def spread(row):
        return jnp.broadcast_to(row, (16, chunk)).astype(bf)

    one, zero = jnp.array(1, bf), jnp.array(0, bf)
    base = lax.broadcasted_iota(i32, (16, chunk), 0)

    def equal(index, count):
        index = spread(index.astype(f32))
        return [(base + b * 16).astype(f32).astype(bf) == index for b in range(count // 16)]

    mask = equal(hi, 64)
    right = jnp.concatenate([jnp.where(m, one, zero) for m in equal(lo, 256)], axis=0)
    tops = [row.astype(bf).astype(f32) for row in rows]
    parts = [spread(top) for top in tops]
    rests = [spread((row - top) * 256.0) for row, top in zip(rows, tops)]
    left = jnp.concatenate([jnp.where(mask[d], parts[f], zero) for f, d in groups], axis=0)
    left8 = jnp.concatenate([jnp.where(mask[d], rests[f], zero) for f, d in groups], axis=0)
    dims = (((1,), (1,)), ((), ()))
    prod = lax.dot_general(left, right, dims, preferred_element_type=f32)
    prod8 = lax.dot_general(
        left8.astype(f8), right.astype(f8), dims, preferred_element_type=f32
    )
    return prod + prod8 * (1 / 256.0)


POINT_ARGS = 8


def group_sums(chunk, groups, args, acc, arrived=lambda c: None):
    trial, mean, cons, vel, wt, cell, flag, count = args[:POINT_ARGS]

    def step(c, carry):
        arrived(c)
        at = pl.ds(pl.multiple_of(c * chunk, chunk), chunk)
        slot = c * chunk + lax.broadcasted_iota(i32, (1, chunk), 1)
        live = slot < count[0]
        rows = point_rows(
            trial[:, at], mean[:, at], cons[:, at], vel[:, at], wt[:, at], flag[:, at], live
        )
        prod = cell_products(rows, cell[:, at], groups)

        @pl.when(c == 0)
        def _():
            acc[...] = prod

        @pl.when(c > 0)
        def _():
            acc[...] += prod

        return carry

    lax.fori_loop(0, cell.shape[1] // chunk, step, 0)


def copied_sums(chunk, groups, sources, scratch, acc, sems):
    chunks = sources[1].shape[1] // chunk
    points = range(POINT_ARGS - 1)

    def copy(n, c):
        if n in points:
            at = pl.ds(pl.multiple_of(c * chunk, chunk), chunk)
            return pltpu.make_async_copy(sources[n].at[:, at], scratch[n].at[:, at], sems.at[n, c])
        return pltpu.make_async_copy(sources[n], scratch[n], sems.at[n, 0])

    others = range(POINT_ARGS, len(sources))
    copy(7, 0).start()
    for c in range(chunks):
        for n in points:
            copy(n, c).start()
    for n in others:
        copy(n, 0).start()
    copy(7, 0).wait()

    def arrived(c):
        for n in points:
            copy(n, c).wait()

    group_sums(chunk, groups, scratch, acc, arrived)
    for n in others:
        copy(n, 0).wait()


NEAR_GROUPS = tuple(x for x in X_ROWS if x[0] < 10)
FAR_GROUPS = tuple(
    (f, d) for f in range(10) for d in range(ROWS // 2) if (f, d) not in NEAR_GROUPS
)
HALVES = ((0, 0), (1, COLS))


def near_kernel(chunk, *refs):
    sources, (acc, low, high), scratch, sems = refs[:10], refs[10:13], refs[13:23], refs[23]
    copied_sums(chunk, NEAR_GROUPS, sources, scratch, acc, sems)
    por, perm = scratch[POINT_ARGS:]
    lane = lax.broadcasted_iota(i32, (LEVELS, COLS), 1)
    packed = [[jnp.zeros((LEVELS, COLS), f32)] * X_DEEP for _ in range(2)]
    for q, (field, deep) in enumerate(X_ROWS):
        at, depth = Y_PLACE[field] + HALF, Y_DEPTH[field]
        mask = (lane >= at - depth) & (lane < at + depth)
        for side, row in ((0, deep), (1, ROWS - 1 - deep)):
            face = (low, high)[side]
            if field < 10:
                first = NEAR_GROUPS.index((field, deep)) * 16 + side * 8
                for half, col in HALVES:
                    face[q, 8 * half : 8 * half + 8, :] = acc[first : first + 8, col : col + COLS]
            else:
                face[q] = (por if field == POR else perm)[pl.ds(row, LEVELS, stride=ROWS), :]
            packed[side][deep] = jnp.where(mask, turn(face[q], at, 1), packed[side][deep])
    for deep in range(X_DEEP):
        low[len(X_ROWS) + deep] = packed[0][deep]
        high[len(X_ROWS) + X_DEEP - 1 - deep] = packed[1][deep]


def far_kernel(chunk, *refs):
    args, acc = refs[:POINT_ARGS], refs[POINT_ARGS]
    group_sums(chunk, FAR_GROUPS, args, acc)


def assemble_kernel(near, far, por, perm, out, own):
    for groups, values in ((NEAR_GROUPS, near), (FAR_GROUPS, far)):
        for n, (field, deep) in enumerate(groups):
            for side, row in ((0, deep), (1, ROWS - 1 - deep)):
                first = n * 16 + side * 8
                for half, col in HALVES:
                    rows = pl.ds(half * (CELLS // 2) + row, LEVELS // 2, stride=ROWS)
                    out[field, rows, :] = values[first : first + 8, col : col + COLS]
    lane = lax.broadcasted_iota(i32, (CELLS, COLS), 1)
    packed = jnp.zeros((CELLS, COLS), f32)
    for field in range(FIELDS):
        at, depth = Y_PLACE[field], Y_DEPTH[field]
        values = out[field] if field < 10 else (por if field == POR else perm)[...]
        mask = (lane >= at - depth) & (lane < at + depth)
        packed = jnp.where(mask, turn(values, at, 1), packed)
    own[...] = packed


def assemble(near, far, por, perm):
    return pl.pallas_call(
        assemble_kernel,
        out_shape=[
            jax.ShapeDtypeStruct((10, CELLS, COLS), f32),
            jax.ShapeDtypeStruct((CELLS, COLS), f32),
        ],
        compiler_params=pltpu.CompilerParams(vmem_limit_bytes=8 << 20),
        cost_estimate=pl.CostEstimate(flops=4000000, bytes_accessed=1500000, transcendentals=0),
        name="assemble",
    )(near, far, por, perm)


def group_call(kernel, groups, args, outs, copied, scratch, grant, name):
    points = args[1].shape[1]
    chunk = points // 2 if points % 256 == 0 else points
    if copied:
        scratch = [pltpu.VMEM(v.shape, v.dtype) for v in args] + scratch
        scratch = scratch + [pltpu.SemaphoreType.DMA((len(args), points // chunk))]
    space = pltpu.HBM if copied else pltpu.VMEM
    return pl.pallas_call(
        functools.partial(kernel, chunk),
        in_specs=[pl.BlockSpec(memory_space=space)] * len(args),
        out_shape=[jax.ShapeDtypeStruct(shape, f32) for shape in outs],
        scratch_shapes=scratch,
        compiler_params=pltpu.CompilerParams(vmem_limit_bytes=grant << 20),
        cost_estimate=pl.CostEstimate(
            flops=2 * 24 * len(groups) * 256 * points, bytes_accessed=64 * points, transcendentals=0
        ),
        name=name,
    )(*args)


def point_args(trial, mean, cons, vel, wt, cell, flag, count):
    row = lambda v: v.reshape(1, -1)
    return (trial, row(mean), row(cons), vel, row(wt), row(cell), row(flag), count)


def near_sums(points, por, perm):
    acc = (16 * len(NEAR_GROUPS), 2 * COLS)
    faces = (X_SENT, LEVELS, COLS)
    outs = [acc, faces, faces]
    args = (*points, por, perm)
    return group_call(near_kernel, NEAR_GROUPS, args, outs, True, [], 56, "near_sums")


def far_sums(points):
    outs = [(16 * len(FAR_GROUPS), 2 * COLS)]
    return group_call(far_kernel, FAR_GROUPS, points, outs, False, [], 44, "far_sums")[0]


def with_rims(own, below, above):
    rows = X_DEEP * LEVELS
    first = above[len(X_ROWS) :].reshape(rows, COLS)
    last = below[len(X_ROWS) :].reshape(rows, COLS)
    return own + jnp.concatenate([first, jnp.zeros((CELLS - 2 * rows, COLS), f32), last])


def y_from_above(shape):
    lane = lax.broadcasted_iota(i32, shape, 1) & (HALF - 1)
    mask = lane < 0
    for field in range(FIELDS):
        at = Y_PLACE[field]
        mask |= (lane >= at) & (lane < at + Y_DEPTH[field])
    return mask


Y_LOW, Y_HIGH, X_HAS_LOW, X_HAS_HIGH, Y_HAS_LOW, Y_HAS_HIGH, LAYER = range(7)


def met(where, packs, from_above, rows):
    low = packs[where[Y_LOW], rows, :] * where[Y_HAS_LOW].astype(f32)
    high = packs[where[Y_HIGH], rows, :] * where[Y_HAS_HIGH].astype(f32)
    return jnp.where(from_above, high, low)


def diff_x(own, rim):
    row = tile_iota(0)
    own_up, rim_up = turn(own, -1, 0), turn(rim, -1, 0)
    own_down, rim_down = turn(own, 1, 0), turn(rim, 1, 0)
    top, bottom = row == ROWS - 1, row == 0
    return (
        jnp.where(top, rim_up, own_up) - jnp.where(bottom, rim_down, own_down),
        jnp.where(top, own_up, rim_up) - jnp.where(bottom, own_down, rim_down),
    )


def diff_y(own, rim):
    lane = tile_iota(1)
    own_up, rim_up = turn(own, -1, 1), turn(rim, -1, 1)
    own_down, rim_down = turn(own, 1, 1), turn(rim, 1, 1)
    top, bottom = lane == COLS - 1, lane == 0
    return (
        jnp.where(top, rim_up, own_up) - jnp.where(bottom, rim_down, own_down),
        jnp.where(top, own_up, rim_up) - jnp.where(bottom, own_down, rim_down),
    )


def ext_x(t):
    a0, a1 = diff_x(t[0], t[1])
    b0, b1 = diff_x(t[2], t[3])
    return [a0, a1, b0, b1]


def ext_y(t):
    a0, a2 = diff_y(t[0], t[2])
    b1, b3 = diff_y(t[1], t[3])
    return [a0, b1, a2, b3]


def rim_masks(where):
    row, lane = tile_iota(0), tile_iota(1)
    has = lambda low, high, test: jnp.where(test, where[high], where[low]) == 1
    in_x = has(X_HAS_LOW, X_HAS_HIGH, row < 4)
    in_y = has(Y_HAS_LOW, Y_HAS_HIGH, lane < HALF)
    return in_x, in_y, in_x & in_y


def local_kernel(where, sums, por, perm, below, above, packs, vel, inner, out, rim, corner):
    rim[...] = jnp.zeros_like(rim)
    for q, (field, deep) in enumerate(X_ROWS):
        rim[field, pl.ds(deep, LEVELS, stride=ROWS), :] = above[q]
        rim[field, pl.ds(ROWS - 1 - deep, LEVELS, stride=ROWS), :] = below[q]
    from_above = y_from_above((LEVELS, COLS))
    for slot in range(ROWS):
        rows = pl.ds(slot * LEVELS, LEVELS)
        corner[pl.ds(slot, LEVELS, stride=ROWS), :] = met(where, packs, from_above, rows)
    from_above = y_from_above((ROWS, COLS))
    in_x, in_y, in_xy = rim_masks(where)
    in_rims = (in_x, in_y, in_xy)
    inside = lambda t: t[:1] + [jnp.where(m, v, 0.0) for m, v in zip(in_rims, t[1:])]
    zero = jnp.zeros((ROWS, COLS), f32)

    def field_at(field, level):
        rows = pl.ds(level * ROWS, ROWS)
        at = Y_PLACE[field]
        own = sums[field, rows, :] if field < 10 else (por if field == POR else perm)[rows, :]
        if level not in merged:
            merged[level] = met(where, packs, from_above, rows)
        lanes = merged[level]
        return [
            own,
            rim[field, rows, :],
            turn(lanes, -at, 1),
            turn(corner[rows, :], -at - HALF, 1),
        ]

    memo, merged = {}, {}

    def get(field, level):
        if not 0 <= level < LEVELS:
            return [zero] * 4
        if (field, level) not in memo:
            memo[field, level] = field_at(field, level)
        return memo[field, level]

    def star(level):
        weight = inside([0.125 / jnp.maximum(m, 0.5) for m in get(MASS, level)])
        dz = lambda f: [u - d for u, d in zip(get(f, level + 1), get(f, level - 1))]
        forces = (
            (ext_x(get(XX, level)), ext_y(get(XY, level)), dz(ZX)),
            (ext_x(get(XY, level)), ext_y(get(YY, level)), dz(YZ)),
            (ext_x(get(ZX, level)), ext_y(get(YZ, level)), dz(ZZ)),
        )
        found = []
        for field, (fx, fy, fz) in zip((MX, MY, MZ), forces):
            found.append(
                [
                    (8.0 * m + (fx[n] + fy[n] + fz[n])) * weight[n]
                    for n, m in enumerate(get(field, level))
                ]
            )
        return found, weight

    def level_perm(level):
        own, x, y, _ = get(PERM, level)
        return [own] + [jnp.where(t > 0.0, t, 1.0) for t in (x, y)]

    def faces(level):
        pairs = zip(level_perm(level), level_perm(level + 1))
        return [0.5 * a * b / (a + b) for a, b in pairs]

    zero3 = [zero] * 3
    stars, weights = {}, {}
    stars[0], weights[0] = star(0)
    first_star = stars[0][2]
    wide = {0: [weights[0], get(ZX, 0), get(YZ, 0)]}
    stress = {0: get(ZZ, 0)}
    down = zero3
    kept, terms, sources, links = [], {}, {}, {}
    for level in range(LEVELS):
        if level + 1 < LEVELS:
            stars[level + 1], weights[level + 1] = star(level + 1)
        vx, vy, vz = stars[level]
        for n, part in enumerate((vx, vy, vz)):
            vel[n, pl.ds(level * ROWS, ROWS), :] = part[0]
        z_up = stars[level + 1][2] if level + 1 < LEVELS else zero3
        z_down = stars[level - 1][2] if level > 0 else zero3
        if level == LEVELS - 1:
            wide[1] = [weights[level], get(ZX, level), get(YZ, level)]
            stress[1] = get(ZZ, level)
        dx, dy = ext_x(vx), ext_y(vy)
        porosity = get(POR, level)[:3]
        up = faces(level) if level + 1 < LEVELS else zero3
        now = []
        for n in range(3):
            source = -0.0015 * (1.0 - porosity[n])
            right = source * (dx[n] + dy[n] + (z_up[n] - z_down[n]))
            main = 0.002 * porosity[n] + (down[n] + up[n])
            now.append((-down[n], main, -up[n], right, source))
        sources[level], links[level] = [t[4] for t in now], up
        down = up
        if level in (0, LEVELS - 1):
            terms[level] = now
        elif level == 1:
            kept.append([(lo, 1.0 / mid, hi, r) for lo, mid, hi, r, _ in now])
        else:
            rows = []
            for (lo, mid, hi, r, _), (f, inv, u, pr) in zip(now, kept[-1]):
                w = lo * inv
                rows.append((-w * f, 1.0 / (mid - w * u), hi, r - w * pr))
            kept.append(rows)
        for key in [k for k in memo if k[1] < level]:
            del memo[key]
    after = last_inner = None
    for n_row in range(len(kept) - 1, -1, -1):
        rows = []
        for t in range(3):
            f, inv, u, r = kept[n_row][t]
            if after is None:
                rows.append((r * inv, -f * inv, -u * inv))
            else:
                b2, f2, g2 = after[t]
                rows.append(((r - u * b2) * inv, -(f + u * f2) * inv, -u * g2 * inv))
            for m in range(3):
                inner[t, m, n_row] = rows[t][m]
        last_inner = last_inner or rows
        after = rows
    first_inner = after
    top = LEVELS - 1
    narrow = []
    for t in range(3):
        _, mid, hi, r, source = terms[0][t]
        b, f, g = first_inner[t]
        echo = sources[1][t] * weights[0][t] / links[0][t]
        face = level_perm(0)[t]
        mine = [face, mid + hi * f, hi * f, hi * g, r - hi * b, source, echo, first_star[t], stress[0][t]]
        lo, mid, _, r, source = terms[top][t]
        b, f, g = last_inner[t]
        echo = sources[top - 1][t] * weights[top][t] / links[top - 1][t]
        face = level_perm(top)[t]
        mine += [face, mid + lo * g, lo * g, lo * f, r - lo * b, source, echo, stars[top][2][t], stress[1][t]]
        narrow.append(mine)
    row, lane = tile_iota(0), tile_iota(1)
    x_parts = [zero] * -(-NARROW // 4)
    x_wide = [zero] * -(-WIDE // 2)
    y_part = zero

    def between(index, at, count):
        return (index >= at) & (index < at + count)

    for q in range(NARROW):
        own, x, y = (narrow[t][q] for t in range(3))
        out[8 * q : 8 * q + 8, :] = own
        at = 2 * q % 8
        x_parts[q // 4] = jnp.where(between(row, at, 2), turn(x, at + 1, 0), x_parts[q // 4])
        y_part = jnp.where(between(lane, 2 * q, 2), turn(y, 2 * q + 1, 1), y_part)
    for m, (own, x, y, xy) in enumerate(wide[0] + wide[1]):
        at = 8 * (NARROW + m)
        out[at : at + 8, :] = own
        at = 4 * (m % 2)
        x_wide[m // 2] = jnp.where(between(row, at, 4), turn(x, at + 2, 0), x_wide[m // 2])
        at = LANE_WIDE + 4 * m
        y_part = jnp.where(between(lane, at, 4), turn(y, at + 2, 1), y_part)
        at = LANE_CORNER + 2 * m
        y_part = jnp.where(between(lane, at, 2), turn(xy, at + 1, 1), y_part)
    for n, part in enumerate(x_parts):
        out[MSG_X + 8 * n : MSG_X + 8 * n + 8, :] = part
    for n, part in enumerate(x_wide):
        out[MSG_X_WIDE + 8 * n : MSG_X_WIDE + 8 * n + 8, :] = part
    out[MSG_Y : MSG_Y + 8, :] = y_part


def local_solve(where, sums, por, perm, below, above, packs):
    smem = pl.BlockSpec(memory_space=pltpu.SMEM)
    vmem = pl.BlockSpec(memory_space=pltpu.VMEM)
    return pl.pallas_call(
        local_kernel,
        in_specs=[smem] + [vmem] * 6,
        out_shape=[
            jax.ShapeDtypeStruct((3, CELLS, COLS), f32),
            jax.ShapeDtypeStruct((3, 3, LEVELS - 2, ROWS, COLS), f32),
            jax.ShapeDtypeStruct((MSG_ROWS, COLS), f32),
        ],
        scratch_shapes=[pltpu.VMEM((FIELDS, CELLS, COLS), f32), pltpu.VMEM((CELLS, COLS), f32)],
        compiler_params=pltpu.CompilerParams(vmem_limit_bytes=16 << 20),
        name="local_solve",
    )(where, sums, por, perm, below, above, packs)


def final_kernel(layers, where, vel, inner, told, out, pressure):
    me = where[LAYER]
    zero = jnp.zeros((ROWS, COLS), f32)

    def narrow(k, side, what):
        q = 9 * side + what
        at = MSG_X + 8 * (q // 4)
        return [
            told[k, 8 * q : 8 * q + 8, :],
            turn(told[k, at : at + 8, :], -(2 * q % 8 + 1), 0),
            turn(told[k, MSG_Y : MSG_Y + 8, :], -(2 * q + 1), 1),
        ]

    def wide(k, side, what):
        m = 3 * side + what
        own = 8 * (NARROW + m)
        at = MSG_X_WIDE + 8 * (m // 2)
        lanes = told[k, MSG_Y : MSG_Y + 8, :]
        return [
            told[k, own : own + 8, :],
            turn(told[k, at : at + 8, :], -(4 * (m % 2) + 2), 0),
            turn(lanes, -(LANE_WIDE + 4 * m + 2), 1),
            turn(lanes, -(LANE_CORNER + 2 * m + 1), 1),
        ]

    def times(*factors):
        product = factors[0]
        for factor in factors[1:]:
            product = [a * b for a, b in zip(product, factor)]
        return product

    def plus(*terms):
        total = terms[0]
        for term in terms[1:]:
            total = [a + b for a, b in zip(total, term)]
        return total

    def minus(a, b):
        return [x - y for x, y in zip(a, b)]

    def half_face(a, b):
        return [0.5 * x * y / (x + y) for x, y in zip(a, b)]

    rows, gains, echoes = [], [], []
    for k in range(layers):
        gain, echo = [], []
        sides = []
        for side, other in ((0, k - 1), (1, k + 1)):
            right = narrow(k, side, RIGHT)
            main = narrow(k, side, MAIN)
            if 0 <= other < layers:
                weight = wide(k, side, WEIGHT)
                sign = -1.0 if side == 0 else 1.0
                weight = [sign * w for w in weight]
                stress = narrow(other, 1 - side, STRESSZ)
                vx = times(weight, wide(other, 1 - side, SHEARX))
                vy = times(weight, wide(other, 1 - side, SHEARY))
                vz = times(weight, stress)
                change = times(wide(other, 1 - side, WEIGHT), narrow(k, side, STRESSZ))
                beyond = minus(narrow(other, 1 - side, VELZ), [sign * c for c in change])
                spread = plus(ext_x(vx)[:3], ext_y(vy)[:3], [sign * v for v in beyond])
                right = plus(right, times(narrow(k, side, SOURCE), spread))
                link = half_face(narrow(k, side, FACE), narrow(other, 1 - side, FACE))
                main = plus(main, link)
                echo.append(times(narrow(k, side, ECHO), stress))
                gain.append((vx[0], vy[0], vz[0]))
            else:
                link = [zero] * 3
                if side == 1:
                    main = plus(main, [0.25 * v for v in narrow(k, side, FACE)])
                echo.append([zero] * 3)
                gain.append((zero, zero, zero))
            sides.append((link, main, right))
        for side, (link, main, right) in enumerate(sides):
            near, far = narrow(k, side, NEAR), narrow(k, side, FAR)
            right = minus(right, plus(times(near, echo[side]), times(far, echo[1 - side])))
            inv = [1.0 / m for m in main]
            link = [-v * i for v, i in zip(link, inv)]
            far, right = times(far, inv), times(right, inv)
            rows.append((link, far, right) if side == 0 else (far, link, right))
        gains.append(gain)
        echoes.append(echo)
    done = []
    for n, (lo, hi, r) in enumerate(rows):
        if n == 0:
            done.append((hi, r))
            continue
        hs, rs = done[-1]
        inv = [1.0 / (1.0 - l * h) for l, h in zip(lo, hs)]
        done.append((times(hi, inv), times(minus(r, times(lo, rs)), inv)))
    ends = [None] * len(rows)
    ends[-1] = done[-1][1]
    for n in range(len(rows) - 2, -1, -1):
        hs, rs = done[n]
        ends[n] = minus(rs, times(hs, ends[n + 1]))

    def mine(values):
        chosen = values[0]
        for k in range(1, layers):
            chosen = [jnp.where(me == k, v, c) for v, c in zip(values[k], chosen)]
        return chosen

    first, last = mine(ends[0::2]), mine(ends[1::2])
    under = mine([[zero]] + [e[:1] for e in ends[1:-1:2]])[0]
    over = mine([e[:1] for e in ends[2::2]] + [[zero]])[0]
    first_seen = plus(first, mine([e[0] for e in echoes]))
    last_seen = plus(last, mine([e[1] for e in echoes]))
    gain = {0: mine([g[0] for g in gains]), LEVELS - 1: mine([g[1] for g in gains])}
    in_x, in_y, _ = rim_masks(where)

    def press(level):
        if level < 0:
            return [under]
        if level >= LEVELS:
            return [over]
        if level == 0:
            parts = first
        elif level == LEVELS - 1:
            parts = last
        else:
            parts = [
                inner[t, 0, level - 1]
                + inner[t, 1, level - 1] * first_seen[t]
                + inner[t, 2, level - 1] * last_seen[t]
                for t in range(3)
            ]
        return [parts[0], jnp.where(in_x, parts[1], 0.0), jnp.where(in_y, parts[2], 0.0)]

    before, now = press(-1), press(0)
    for level in range(LEVELS):
        after = press(level + 1)
        rows_at = pl.ds(level * ROWS, ROWS)
        pressure[rows_at, :] = now[0]
        grads = (
            diff_x(now[0], now[1])[0],
            diff_y(now[0], now[2])[0],
            after[0] - before[0],
        )
        for n in range(3):
            value = vel[n, rows_at, :] - 0.125 * grads[n]
            out[n, rows_at, :] = value + gain[level][n] if level in gain else value
        before, now = now, after


def final(where, vel, inner, told):
    smem = pl.BlockSpec(memory_space=pltpu.SMEM)
    vmem = pl.BlockSpec(memory_space=pltpu.VMEM)
    return pl.pallas_call(
        functools.partial(final_kernel, told.shape[0]),
        in_specs=[smem] + [vmem] * 3,
        out_shape=[
            jax.ShapeDtypeStruct((3, CELLS, COLS), f32),
            jax.ShapeDtypeStruct((CELLS, COLS), f32),
        ],
        compiler_params=pltpu.CompilerParams(vmem_limit_bytes=16 << 20),
        name="final",
    )(where, vel, inner, told)


def shift_up(block, axis):
    count = lax.axis_size(axis)
    return lax.ppermute(block, axis, [(i, i + 1) for i in range(count - 1)])


def shift_down(block, axis):
    count = lax.axis_size(axis)
    return lax.ppermute(block, axis, [(i + 1, i) for i in range(count - 1)])


def neighbours(block, axis):
    count, me = lax.axis_size(axis), lax.axis_index(axis)
    if count == 2:
        return lax.ppermute(block, axis, [(0, 1), (1, 0)])[None], 0, 0
    if count > 4:
        return jnp.stack([shift_up(block, axis), shift_down(block, axis)]), 0, 1
    stacked = lax.all_gather(block, axis, axis=0)
    return stacked, jnp.maximum(me - 1, 0), jnp.minimum(me + 1, count - 1)


def shards(trial, mean, cons, vel, wt, cell, flag, count, por, perm):
    por = por.reshape(CELLS, COLS)
    perm = perm.reshape(CELLS, COLS)
    points = point_args(trial, mean, cons, vel, wt, cell, flag, count)
    near, low, high = near_sums(points, por, perm)
    above = shift_down(low, "gx")
    below = shift_up(high, "gx")

    def ends(axis):
        me = lax.axis_index(axis)
        return [(me > 0).astype(i32), (me < lax.axis_size(axis) - 1).astype(i32)]

    has = ends("gx") + ends("gy")
    sums, own = assemble(near, far_sums(points), por, perm)
    packs, y_low, y_high = neighbours(with_rims(own, below, above), "gy")
    where = jnp.stack(
        [jnp.asarray(v, i32) for v in [y_low, y_high] + has + [lax.axis_index("gz")]]
    )
    star, inner, told = local_solve(where, sums, por, perm, below, above, packs)
    velocity, pressure = final(where, star, inner, lax.all_gather(told, "gz", axis=0))
    return (
        velocity.reshape(3, LEVELS, ROWS, COLS),
        pressure.reshape(LEVELS, ROWS, COLS),
    )


def solution(mesh):
    points = ("gx", "gy", "gz")
    cells = P("gz", "gx", "gy")
    placed = (
        P(None, points), P(points), P(points), P(None, points), P(points), P(points), P(points),
        P(*points), cells, cells,
    )
    return jax.shard_map(
        shards,
        mesh=mesh,
        in_specs=placed,
        out_specs=(P(None, *cells), cells),
        check_vma=False,
    )
```

```python
import functools

import jax
import jax.numpy as jnp
from jax import lax
from jax.experimental import pallas as pl
from jax.experimental.pallas import tpu as pltpu
from jax.sharding import PartitionSpec as P

bf = jnp.bfloat16
f8 = jnp.float8_e4m3fn
f32 = jnp.float32
i32 = jnp.int32

LEVELS, ROWS, COLS = 16, 8, 128
CELLS = LEVELS * ROWS

ZX, YZ, ZZ, XX, YY, XY, MX, MY, MZ, MASS, POR, PERM = range(12)
FIELDS = 12
STRESS_ORDER = (5, 4, 2, 0, 1, 3)

X_ROWS = (
    (ZX, 0), (ZX, 1), (YZ, 0), (ZZ, 0), (PERM, 0), (POR, 0),
    (XX, 0), (XX, 1), (XX, 2), (XY, 0), (XY, 1), (YY, 0),
    (MX, 0), (MX, 1), (MY, 0), (MZ, 0), (MASS, 0), (MASS, 1),
)
X_DEEP = 3
X_SENT = len(X_ROWS) + X_DEEP
Y_DEPTH = {ZX: 1, YZ: 2, ZZ: 1, XX: 1, YY: 3, XY: 2, MX: 1, MY: 2, MZ: 1, MASS: 2, POR: 1, PERM: 1}
Y_PLACE = {}
_at = 0
for _f in range(FIELDS):
    Y_PLACE[_f] = _at + Y_DEPTH[_f]
    _at += 2 * Y_DEPTH[_f]
HALF = 64
FACE, MAIN, NEAR, FAR, RIGHT, SOURCE, ECHO, VELZ, STRESSZ = range(9)
WEIGHT, SHEARX, SHEARY = range(3)
NARROW, WIDE = 18, 6
MSG_X = 8 * (NARROW + WIDE)
MSG_X_WIDE = MSG_X + 8 * -(-NARROW // 4)
MSG_Y = MSG_X_WIDE + 8 * -(-WIDE // 2)
MSG_ROWS = MSG_Y + 8
LANE_WIDE = 2 * NARROW
LANE_CORNER = LANE_WIDE + 4 * WIDE


def tile_iota(dim):
    return lax.broadcasted_iota(i32, (ROWS, COLS), dim)


def turn(tile, shift, axis):
    shift %= tile.shape[axis]
    return tile if shift == 0 else pltpu.roll(tile, shift, axis)


def row_stress(trial, mean, cons, flag):
    part = lax.broadcasted_iota(i32, trial.shape, 0)
    size = jnp.sqrt(
        jnp.sum(trial * trial * jnp.where(part < 3, 1.5, 3.0), axis=0, keepdims=True)
    )
    yield_size = 1.2 * jnp.sqrt(mean * (cons - mean))
    factor = jnp.where(flag == 1, yield_size / jnp.maximum(size, 1.0), 1.0)
    return trial * factor - jnp.where(part < 3, mean, 0.0)


def point_rows(trial, mean, cons, vel, wt, flag, live):
    weight = jnp.where(live, wt, 0.0)
    stress = row_stress(trial, mean, cons, flag) * weight
    momentum = vel * weight
    rows = [stress[i : i + 1] for i in STRESS_ORDER]
    return rows + [momentum[i : i + 1] for i in range(3)] + [weight]


def cell_products(rows, place, groups):
    chunk = place.shape[1]
    row = (place >> 7) & (ROWS - 1)
    deep = jnp.where(row < ROWS // 2, row, ROWS - 1 - row)
    hi = deep * 16 + (row >> 2) * 8 + ((place >> 10) & 7)
    lo = ((place >> 13) << 7) | (place & (COLS - 1))

    def spread(row):
        return jnp.broadcast_to(row, (16, chunk)).astype(bf)

    one, zero = jnp.array(1, bf), jnp.array(0, bf)
    base = lax.broadcasted_iota(i32, (16, chunk), 0)

    def equal(index, count):
        index = spread(index.astype(f32))
        return [(base + b * 16).astype(f32).astype(bf) == index for b in range(count // 16)]

    mask = equal(hi, 64)
    right = jnp.concatenate([jnp.where(m, one, zero) for m in equal(lo, 256)], axis=0)
    tops = [row.astype(bf).astype(f32) for row in rows]
    parts = [spread(top) for top in tops]
    rests = [spread((row - top) * 256.0) for row, top in zip(rows, tops)]
    left = jnp.concatenate([jnp.where(mask[d], parts[f], zero) for f, d in groups], axis=0)
    left8 = jnp.concatenate([jnp.where(mask[d], rests[f], zero) for f, d in groups], axis=0)
    dims = (((1,), (1,)), ((), ()))
    prod = lax.dot_general(left, right, dims, preferred_element_type=f32)
    prod8 = lax.dot_general(
        left8.astype(f8), right.astype(f8), dims, preferred_element_type=f32
    )
    return prod + prod8 * (1 / 256.0)


POINT_ARGS = 8


def group_sums(chunk, groups, args, acc, arrived=lambda c: None):
    trial, mean, cons, vel, wt, cell, flag, count = args[:POINT_ARGS]

    def step(c, carry):
        arrived(c)
        at = pl.ds(pl.multiple_of(c * chunk, chunk), chunk)
        slot = c * chunk + lax.broadcasted_iota(i32, (1, chunk), 1)
        live = slot < count[0]
        rows = point_rows(
            trial[:, at], mean[:, at], cons[:, at], vel[:, at], wt[:, at], flag[:, at], live
        )
        prod = cell_products(rows, cell[:, at], groups)

        @pl.when(c == 0)
        def _():
            acc[...] = prod

        @pl.when(c > 0)
        def _():
            acc[...] += prod

        return carry

    lax.fori_loop(0, cell.shape[1] // chunk, step, 0)


def copied_sums(chunk, groups, sources, scratch, acc, sems):
    chunks = sources[1].shape[1] // chunk
    points = range(POINT_ARGS - 1)

    def copy(n, c):
        if n in points:
            at = pl.ds(pl.multiple_of(c * chunk, chunk), chunk)
            return pltpu.make_async_copy(sources[n].at[:, at], scratch[n].at[:, at], sems.at[n, c])
        return pltpu.make_async_copy(sources[n], scratch[n], sems.at[n, 0])

    others = range(POINT_ARGS, len(sources))
    copy(7, 0).start()
    for c in range(chunks):
        for n in points:
            copy(n, c).start()
    for n in others:
        copy(n, 0).start()
    copy(7, 0).wait()

    def arrived(c):
        for n in points:
            copy(n, c).wait()

    group_sums(chunk, groups, scratch, acc, arrived)
    for n in others:
        copy(n, 0).wait()


NEAR_GROUPS = tuple(x for x in X_ROWS if x[0] < 10)
FAR_GROUPS = tuple(
    (f, d) for f in range(10) for d in range(ROWS // 2) if (f, d) not in NEAR_GROUPS
)
HALVES = ((0, 0), (1, COLS))


def near_kernel(chunk, *refs):
    sources, (acc, low, high), scratch, sems = refs[:10], refs[10:13], refs[13:23], refs[23]
    copied_sums(chunk, NEAR_GROUPS, sources, scratch, acc, sems)
    por, perm = scratch[POINT_ARGS:]
    lane = lax.broadcasted_iota(i32, (LEVELS, COLS), 1)
    packed = [[jnp.zeros((LEVELS, COLS), f32)] * X_DEEP for _ in range(2)]
    for q, (field, deep) in enumerate(X_ROWS):
        at, depth = Y_PLACE[field] + HALF, Y_DEPTH[field]
        mask = (lane >= at - depth) & (lane < at + depth)
        for side, row in ((0, deep), (1, ROWS - 1 - deep)):
            face = (low, high)[side]
            if field < 10:
                first = NEAR_GROUPS.index((field, deep)) * 16 + side * 8
                for half, col in HALVES:
                    face[q, 8 * half : 8 * half + 8, :] = acc[first : first + 8, col : col + COLS]
            else:
                face[q] = (por if field == POR else perm)[pl.ds(row, LEVELS, stride=ROWS), :]
            packed[side][deep] = jnp.where(mask, turn(face[q], at, 1), packed[side][deep])
    for deep in range(X_DEEP):
        low[len(X_ROWS) + deep] = packed[0][deep]
        high[len(X_ROWS) + X_DEEP - 1 - deep] = packed[1][deep]


def far_kernel(chunk, *refs):
    args, acc = refs[:POINT_ARGS], refs[POINT_ARGS]
    group_sums(chunk, FAR_GROUPS, args, acc)


def assemble_kernel(near, far, por, perm, out, own):
    for groups, values in ((NEAR_GROUPS, near), (FAR_GROUPS, far)):
        for n, (field, deep) in enumerate(groups):
            for side, row in ((0, deep), (1, ROWS - 1 - deep)):
                first = n * 16 + side * 8
                for half, col in HALVES:
                    rows = pl.ds(half * (CELLS // 2) + row, LEVELS // 2, stride=ROWS)
                    out[field, rows, :] = values[first : first + 8, col : col + COLS]
    lane = lax.broadcasted_iota(i32, (CELLS, COLS), 1)
    packed = jnp.zeros((CELLS, COLS), f32)
    for field in range(FIELDS):
        at, depth = Y_PLACE[field], Y_DEPTH[field]
        values = out[field] if field < 10 else (por if field == POR else perm)[...]
        mask = (lane >= at - depth) & (lane < at + depth)
        packed = jnp.where(mask, turn(values, at, 1), packed)
    own[...] = packed


def assemble(near, far, por, perm):
    return pl.pallas_call(
        assemble_kernel,
        out_shape=[
            jax.ShapeDtypeStruct((10, CELLS, COLS), f32),
            jax.ShapeDtypeStruct((CELLS, COLS), f32),
        ],
        compiler_params=pltpu.CompilerParams(vmem_limit_bytes=8 << 20),
        cost_estimate=pl.CostEstimate(flops=4000000, bytes_accessed=1500000, transcendentals=0),
        name="assemble",
    )(near, far, por, perm)


def group_call(kernel, groups, args, outs, copied, scratch, grant, name):
    points = args[1].shape[1]
    chunk = points // 2 if points % 256 == 0 else points
    if copied:
        scratch = [pltpu.VMEM(v.shape, v.dtype) for v in args] + scratch
        scratch = scratch + [pltpu.SemaphoreType.DMA((len(args), points // chunk))]
    space = pltpu.HBM if copied else pltpu.VMEM
    return pl.pallas_call(
        functools.partial(kernel, chunk),
        in_specs=[pl.BlockSpec(memory_space=space)] * len(args),
        out_shape=[jax.ShapeDtypeStruct(shape, f32) for shape in outs],
        scratch_shapes=scratch,
        compiler_params=pltpu.CompilerParams(vmem_limit_bytes=grant << 20),
        cost_estimate=pl.CostEstimate(
            flops=2 * 24 * len(groups) * 256 * points, bytes_accessed=64 * points, transcendentals=0
        ),
        name=name,
    )(*args)


def point_args(trial, mean, cons, vel, wt, cell, flag, count):
    row = lambda v: v.reshape(1, -1)
    return (trial, row(mean), row(cons), vel, row(wt), row(cell), row(flag), count)


def near_sums(points, por, perm):
    acc = (16 * len(NEAR_GROUPS), 2 * COLS)
    faces = (X_SENT, LEVELS, COLS)
    outs = [acc, faces, faces]
    args = (*points, por, perm)
    return group_call(near_kernel, NEAR_GROUPS, args, outs, True, [], 56, "near_sums")


def far_sums(points):
    outs = [(16 * len(FAR_GROUPS), 2 * COLS)]
    return group_call(far_kernel, FAR_GROUPS, points, outs, False, [], 44, "far_sums")[0]


def with_rims(own, below, above):
    rows = X_DEEP * LEVELS
    first = above[len(X_ROWS) :].reshape(rows, COLS)
    last = below[len(X_ROWS) :].reshape(rows, COLS)
    return own + jnp.concatenate([first, jnp.zeros((CELLS - 2 * rows, COLS), f32), last])


def y_from_above(shape):
    lane = lax.broadcasted_iota(i32, shape, 1) & (HALF - 1)
    mask = lane < 0
    for field in range(FIELDS):
        at = Y_PLACE[field]
        mask |= (lane >= at) & (lane < at + Y_DEPTH[field])
    return mask


Y_LOW, Y_HIGH, X_HAS_LOW, X_HAS_HIGH, Y_HAS_LOW, Y_HAS_HIGH, LAYER = range(7)


def met(where, packs, from_above, rows):
    low = packs[where[Y_LOW], rows, :] * where[Y_HAS_LOW].astype(f32)
    high = packs[where[Y_HIGH], rows, :] * where[Y_HAS_HIGH].astype(f32)
    return jnp.where(from_above, high, low)


def diff_x(own, rim):
    row = tile_iota(0)
    own_up, rim_up = turn(own, -1, 0), turn(rim, -1, 0)
    own_down, rim_down = turn(own, 1, 0), turn(rim, 1, 0)
    top, bottom = row == ROWS - 1, row == 0
    return (
        jnp.where(top, rim_up, own_up) - jnp.where(bottom, rim_down, own_down),
        jnp.where(top, own_up, rim_up) - jnp.where(bottom, own_down, rim_down),
    )


def diff_y(own, rim):
    lane = tile_iota(1)
    own_up, rim_up = turn(own, -1, 1), turn(rim, -1, 1)
    own_down, rim_down = turn(own, 1, 1), turn(rim, 1, 1)
    top, bottom = lane == COLS - 1, lane == 0
    return (
        jnp.where(top, rim_up, own_up) - jnp.where(bottom, rim_down, own_down),
        jnp.where(top, own_up, rim_up) - jnp.where(bottom, own_down, rim_down),
    )


def ext_x(t):
    a0, a1 = diff_x(t[0], t[1])
    b0, b1 = diff_x(t[2], t[3])
    return [a0, a1, b0, b1]


def ext_y(t):
    a0, a2 = diff_y(t[0], t[2])
    b1, b3 = diff_y(t[1], t[3])
    return [a0, b1, a2, b3]


def rim_masks(where):
    row, lane = tile_iota(0), tile_iota(1)
    has = lambda low, high, test: jnp.where(test, where[high], where[low]) == 1
    in_x = has(X_HAS_LOW, X_HAS_HIGH, row < 4)
    in_y = has(Y_HAS_LOW, Y_HAS_HIGH, lane < HALF)
    return in_x, in_y, in_x & in_y


def partial_kernel(where, sums, por, perm, below, above, rim, parts, edges):
    rim[...] = jnp.zeros_like(rim)
    for q, (field, deep) in enumerate(X_ROWS):
        rim[field, pl.ds(deep, LEVELS, stride=ROWS), :] = above[q]
        rim[field, pl.ds(ROWS - 1 - deep, LEVELS, stride=ROWS), :] = below[q]
    in_x = rim_masks(where)[0]
    lane = tile_iota(1)
    zero = jnp.zeros((ROWS, COLS), f32)

    def get(field, level):
        if not 0 <= level < LEVELS:
            return [zero] * 2
        rows = pl.ds(level * ROWS, ROWS)
        return [sums[field, rows, :], rim[field, rows, :]]

    for level in range(LEVELS):
        rows = pl.ds(level * ROWS, ROWS)
        mass = get(MASS, level)
        parts[3, 0, rows, :] = 0.125 / jnp.maximum(mass[0], 0.5)
        parts[3, 1, rows, :] = jnp.where(in_x, 0.125 / jnp.maximum(mass[1], 0.5), 0.0)
        for n, (field, fx, fy, fz) in enumerate(
            ((MX, XX, XY, ZX), (MY, XY, YY, YZ), (MZ, ZX, YZ, ZZ))
        ):
            in_rows = diff_x(*get(fx, level))
            higher, lower, momentum = get(fz, level + 1), get(fz, level - 1), get(field, level)
            for t, tile in enumerate(get(fy, level)):
                up, down = turn(tile, -1, 1), turn(tile, 1, 1)
                edges[n, t, rows, :] = jnp.where(lane == COLS - 1, up, down)
                in_lanes = jnp.where(lane == COLS - 1, 0.0, up) - jnp.where(lane == 0, 0.0, down)
                parts[n, t, rows, :] = (
                    8.0 * momentum[t] + in_rows[t] + in_lanes + (higher[t] - lower[t])
                )


def partial_sums(where, sums, por, perm, below, above):
    smem = pl.BlockSpec(memory_space=pltpu.SMEM)
    vmem = pl.BlockSpec(memory_space=pltpu.VMEM)
    return pl.pallas_call(
        partial_kernel,
        in_specs=[smem] + [vmem] * 5,
        out_shape=[
            jax.ShapeDtypeStruct((FIELDS, CELLS, COLS), f32),
            jax.ShapeDtypeStruct((4, 2, CELLS, COLS), f32),
            jax.ShapeDtypeStruct((3, 2, CELLS, COLS), f32),
        ],
        compiler_params=pltpu.CompilerParams(vmem_limit_bytes=16 << 20),
        cost_estimate=pl.CostEstimate(flops=8000000, bytes_accessed=3000000, transcendentals=0),
        name="partial_sums",
    )(where, sums, por, perm, below, above)


def local_kernel(where, sums, por, perm, rim, parts, edges, packs, vel, inner, out, corner):
    from_above = y_from_above((LEVELS, COLS))
    for slot in range(ROWS):
        rows = pl.ds(slot * LEVELS, LEVELS)
        corner[pl.ds(slot, LEVELS, stride=ROWS), :] = met(where, packs, from_above, rows)
    from_above = y_from_above((ROWS, COLS))
    in_x, in_y, in_xy = rim_masks(where)
    in_rims = (in_x, in_y, in_xy)
    zero = jnp.zeros((ROWS, COLS), f32)

    def field_at(field, level):
        rows = pl.ds(level * ROWS, ROWS)
        at = Y_PLACE[field]
        own = sums[field, rows, :] if field < 10 else (por if field == POR else perm)[rows, :]
        if level not in merged:
            merged[level] = met(where, packs, from_above, rows)
        lanes = merged[level]
        return [
            own,
            rim[field, rows, :],
            turn(lanes, -at, 1),
            turn(corner[rows, :], -at - HALF, 1),
        ]

    memo, merged = {}, {}

    def get(field, level):
        if not 0 <= level < LEVELS:
            return [zero] * 4
        if (field, level) not in memo:
            memo[field, level] = field_at(field, level)
        return memo[field, level]

    lanes = tile_iota(1)
    first_lane, last_lane = lanes == 0, lanes == COLS - 1

    def star(level):
        rows = pl.ds(level * ROWS, ROWS)
        weight = [0.125 / jnp.maximum(m, 0.5) for m in get(MASS, level)[2:]]
        weight = [jnp.where(m, w, 0.0) for m, w in zip(in_rims[1:], weight)]
        weight = [parts[3, 0, rows, :], parts[3, 1, rows, :]] + weight
        found = []
        for n, (field, fx, fy, fz) in enumerate(
            ((MX, XX, XY, ZX), (MY, XY, YY, YZ), (MZ, ZX, YZ, ZZ))
        ):
            in_rows = diff_x(*get(fx, level)[2:])
            higher, lower = get(fz, level + 1)[2:], get(fz, level - 1)[2:]
            momentum = get(field, level)[2:]
            own, outer = [], []
            for t, packed in enumerate((merged[level], corner[rows, :])):
                at = Y_PLACE[fy] + HALF * t
                up, down = turn(packed, -at - 1, 1), turn(packed, 1 - at, 1)
                beside = edges[n, t, rows, :]
                reach = jnp.where(last_lane, up, 0.0) - jnp.where(first_lane, down, 0.0)
                own.append((parts[n, t, rows, :] + reach) * weight[t])
                in_lanes = jnp.where(last_lane, beside, up) - jnp.where(first_lane, beside, down)
                total = 8.0 * momentum[t] + in_rows[t] + in_lanes + (higher[t] - lower[t])
                outer.append(total * weight[2 + t])
            found.append(own + outer)
        return found, weight

    def level_perm(level):
        own, x, y, _ = get(PERM, level)
        return [own] + [jnp.where(t > 0.0, t, 1.0) for t in (x, y)]

    def faces(level):
        pairs = zip(level_perm(level), level_perm(level + 1))
        return [0.5 * a * b / (a + b) for a, b in pairs]

    zero3 = [zero] * 3
    stars, weights = {}, {}
    stars[0], weights[0] = star(0)
    first_star = stars[0][2]
    wide = {0: [weights[0], get(ZX, 0), get(YZ, 0)]}
    stress = {0: get(ZZ, 0)}
    down = zero3
    kept, terms, sources, links = [], {}, {}, {}
    for level in range(LEVELS):
        if level + 1 < LEVELS:
            stars[level + 1], weights[level + 1] = star(level + 1)
        vx, vy, vz = stars[level]
        for n, part in enumerate((vx, vy, vz)):
            vel[n, pl.ds(level * ROWS, ROWS), :] = part[0]
        z_up = stars[level + 1][2] if level + 1 < LEVELS else zero3
        z_down = stars[level - 1][2] if level > 0 else zero3
        if level == LEVELS - 1:
            wide[1] = [weights[level], get(ZX, level), get(YZ, level)]
            stress[1] = get(ZZ, level)
        dx, dy = ext_x(vx), ext_y(vy)
        porosity = get(POR, level)[:3]
        up = faces(level) if level + 1 < LEVELS else zero3
        now = []
        for n in range(3):
            source = -0.0015 * (1.0 - porosity[n])
            right = source * (dx[n] + dy[n] + (z_up[n] - z_down[n]))
            main = 0.002 * porosity[n] + (down[n] + up[n])
            now.append((-down[n], main, -up[n], right, source))
        sources[level], links[level] = [t[4] for t in now], up
        down = up
        if level in (0, LEVELS - 1):
            terms[level] = now
        elif level == 1:
            kept.append([(lo, 1.0 / mid, hi, r) for lo, mid, hi, r, _ in now])
        else:
            rows = []
            for (lo, mid, hi, r, _), (f, inv, u, pr) in zip(now, kept[-1]):
                w = lo * inv
                rows.append((-w * f, 1.0 / (mid - w * u), hi, r - w * pr))
            kept.append(rows)
        for key in [k for k in memo if k[1] < level]:
            del memo[key]
    after = last_inner = None
    for n_row in range(len(kept) - 1, -1, -1):
        rows = []
        for t in range(3):
            f, inv, u, r = kept[n_row][t]
            if after is None:
                rows.append((r * inv, -f * inv, -u * inv))
            else:
                b2, f2, g2 = after[t]
                rows.append(((r - u * b2) * inv, -(f + u * f2) * inv, -u * g2 * inv))
            for m in range(3):
                inner[t, m, n_row] = rows[t][m]
        last_inner = last_inner or rows
        after = rows
    first_inner = after
    top = LEVELS - 1
    narrow = []
    for t in range(3):
        _, mid, hi, r, source = terms[0][t]
        b, f, g = first_inner[t]
        echo = sources[1][t] * weights[0][t] / links[0][t]
        face = level_perm(0)[t]
        mine = [face, mid + hi * f, hi * f, hi * g, r - hi * b, source, echo, first_star[t], stress[0][t]]
        lo, mid, _, r, source = terms[top][t]
        b, f, g = last_inner[t]
        echo = sources[top - 1][t] * weights[top][t] / links[top - 1][t]
        face = level_perm(top)[t]
        mine += [face, mid + lo * g, lo * g, lo * f, r - lo * b, source, echo, stars[top][2][t], stress[1][t]]
        narrow.append(mine)
    row, lane = tile_iota(0), tile_iota(1)
    x_parts = [zero] * -(-NARROW // 4)
    x_wide = [zero] * -(-WIDE // 2)
    y_part = zero

    def between(index, at, count):
        return (index >= at) & (index < at + count)

    for q in range(NARROW):
        own, x, y = (narrow[t][q] for t in range(3))
        out[8 * q : 8 * q + 8, :] = own
        at = 2 * q % 8
        x_parts[q // 4] = jnp.where(between(row, at, 2), turn(x, at + 1, 0), x_parts[q // 4])
        y_part = jnp.where(between(lane, 2 * q, 2), turn(y, 2 * q + 1, 1), y_part)
    for m, (own, x, y, xy) in enumerate(wide[0] + wide[1]):
        at = 8 * (NARROW + m)
        out[at : at + 8, :] = own
        at = 4 * (m % 2)
        x_wide[m // 2] = jnp.where(between(row, at, 4), turn(x, at + 2, 0), x_wide[m // 2])
        at = LANE_WIDE + 4 * m
        y_part = jnp.where(between(lane, at, 4), turn(y, at + 2, 1), y_part)
        at = LANE_CORNER + 2 * m
        y_part = jnp.where(between(lane, at, 2), turn(xy, at + 1, 1), y_part)
    for n, part in enumerate(x_parts):
        out[MSG_X + 8 * n : MSG_X + 8 * n + 8, :] = part
    for n, part in enumerate(x_wide):
        out[MSG_X_WIDE + 8 * n : MSG_X_WIDE + 8 * n + 8, :] = part
    out[MSG_Y : MSG_Y + 8, :] = y_part


def local_solve(where, sums, por, perm, rim, parts, edges, packs):
    smem = pl.BlockSpec(memory_space=pltpu.SMEM)
    vmem = pl.BlockSpec(memory_space=pltpu.VMEM)
    return pl.pallas_call(
        local_kernel,
        in_specs=[smem] + [vmem] * 7,
        out_shape=[
            jax.ShapeDtypeStruct((3, CELLS, COLS), f32),
            jax.ShapeDtypeStruct((3, 3, LEVELS - 2, ROWS, COLS), f32),
            jax.ShapeDtypeStruct((MSG_ROWS, COLS), f32),
        ],
        scratch_shapes=[pltpu.VMEM((CELLS, COLS), f32)],
        compiler_params=pltpu.CompilerParams(vmem_limit_bytes=16 << 20),
        name="local_solve",
    )(where, sums, por, perm, rim, parts, edges, packs)


def final_kernel(layers, where, vel, inner, told, out, pressure):
    me = where[LAYER]
    zero = jnp.zeros((ROWS, COLS), f32)

    def narrow(k, side, what):
        q = 9 * side + what
        at = MSG_X + 8 * (q // 4)
        return [
            told[k, 8 * q : 8 * q + 8, :],
            turn(told[k, at : at + 8, :], -(2 * q % 8 + 1), 0),
            turn(told[k, MSG_Y : MSG_Y + 8, :], -(2 * q + 1), 1),
        ]

    def wide(k, side, what):
        m = 3 * side + what
        own = 8 * (NARROW + m)
        at = MSG_X_WIDE + 8 * (m // 2)
        lanes = told[k, MSG_Y : MSG_Y + 8, :]
        return [
            told[k, own : own + 8, :],
            turn(told[k, at : at + 8, :], -(4 * (m % 2) + 2), 0),
            turn(lanes, -(LANE_WIDE + 4 * m + 2), 1),
            turn(lanes, -(LANE_CORNER + 2 * m + 1), 1),
        ]

    def times(*factors):
        product = factors[0]
        for factor in factors[1:]:
            product = [a * b for a, b in zip(product, factor)]
        return product

    def plus(*terms):
        total = terms[0]
        for term in terms[1:]:
            total = [a + b for a, b in zip(total, term)]
        return total

    def minus(a, b):
        return [x - y for x, y in zip(a, b)]

    def half_face(a, b):
        return [0.5 * x * y / (x + y) for x, y in zip(a, b)]

    rows, gains, echoes = [], [], []
    for k in range(layers):
        gain, echo = [], []
        sides = []
        for side, other in ((0, k - 1), (1, k + 1)):
            right = narrow(k, side, RIGHT)
            main = narrow(k, side, MAIN)
            if 0 <= other < layers:
                weight = wide(k, side, WEIGHT)
                sign = -1.0 if side == 0 else 1.0
                weight = [sign * w for w in weight]
                stress = narrow(other, 1 - side, STRESSZ)
                vx = times(weight, wide(other, 1 - side, SHEARX))
                vy = times(weight, wide(other, 1 - side, SHEARY))
                vz = times(weight, stress)
                change = times(wide(other, 1 - side, WEIGHT), narrow(k, side, STRESSZ))
                beyond = minus(narrow(other, 1 - side, VELZ), [sign * c for c in change])
                spread = plus(ext_x(vx)[:3], ext_y(vy)[:3], [sign * v for v in beyond])
                right = plus(right, times(narrow(k, side, SOURCE), spread))
                link = half_face(narrow(k, side, FACE), narrow(other, 1 - side, FACE))
                main = plus(main, link)
                echo.append(times(narrow(k, side, ECHO), stress))
                gain.append((vx[0], vy[0], vz[0]))
            else:
                link = [zero] * 3
                if side == 1:
                    main = plus(main, [0.25 * v for v in narrow(k, side, FACE)])
                echo.append([zero] * 3)
                gain.append((zero, zero, zero))
            sides.append((link, main, right))
        for side, (link, main, right) in enumerate(sides):
            near, far = narrow(k, side, NEAR), narrow(k, side, FAR)
            right = minus(right, plus(times(near, echo[side]), times(far, echo[1 - side])))
            inv = [1.0 / m for m in main]
            link = [-v * i for v, i in zip(link, inv)]
            far, right = times(far, inv), times(right, inv)
            rows.append((link, far, right) if side == 0 else (far, link, right))
        gains.append(gain)
        echoes.append(echo)
    done = []
    for n, (lo, hi, r) in enumerate(rows):
        if n == 0:
            done.append((hi, r))
            continue
        hs, rs = done[-1]
        inv = [1.0 / (1.0 - l * h) for l, h in zip(lo, hs)]
        done.append((times(hi, inv), times(minus(r, times(lo, rs)), inv)))
    ends = [None] * len(rows)
    ends[-1] = done[-1][1]
    for n in range(len(rows) - 2, -1, -1):
        hs, rs = done[n]
        ends[n] = minus(rs, times(hs, ends[n + 1]))

    def mine(values):
        chosen = values[0]
        for k in range(1, layers):
            chosen = [jnp.where(me == k, v, c) for v, c in zip(values[k], chosen)]
        return chosen

    first, last = mine(ends[0::2]), mine(ends[1::2])
    under = mine([[zero]] + [e[:1] for e in ends[1:-1:2]])[0]
    over = mine([e[:1] for e in ends[2::2]] + [[zero]])[0]
    first_seen = plus(first, mine([e[0] for e in echoes]))
    last_seen = plus(last, mine([e[1] for e in echoes]))
    gain = {0: mine([g[0] for g in gains]), LEVELS - 1: mine([g[1] for g in gains])}
    in_x, in_y, _ = rim_masks(where)

    def press(level):
        if level < 0:
            return [under]
        if level >= LEVELS:
            return [over]
        if level == 0:
            parts = first
        elif level == LEVELS - 1:
            parts = last
        else:
            parts = [
                inner[t, 0, level - 1]
                + inner[t, 1, level - 1] * first_seen[t]
                + inner[t, 2, level - 1] * last_seen[t]
                for t in range(3)
            ]
        return [parts[0], jnp.where(in_x, parts[1], 0.0), jnp.where(in_y, parts[2], 0.0)]

    before, now = press(-1), press(0)
    for level in range(LEVELS):
        after = press(level + 1)
        rows_at = pl.ds(level * ROWS, ROWS)
        pressure[rows_at, :] = now[0]
        grads = (
            diff_x(now[0], now[1])[0],
            diff_y(now[0], now[2])[0],
            after[0] - before[0],
        )
        for n in range(3):
            value = vel[n, rows_at, :] - 0.125 * grads[n]
            out[n, rows_at, :] = value + gain[level][n] if level in gain else value
        before, now = now, after


def final(where, vel, inner, told):
    smem = pl.BlockSpec(memory_space=pltpu.SMEM)
    vmem = pl.BlockSpec(memory_space=pltpu.VMEM)
    return pl.pallas_call(
        functools.partial(final_kernel, told.shape[0]),
        in_specs=[smem] + [vmem] * 3,
        out_shape=[
            jax.ShapeDtypeStruct((3, CELLS, COLS), f32),
            jax.ShapeDtypeStruct((CELLS, COLS), f32),
        ],
        compiler_params=pltpu.CompilerParams(vmem_limit_bytes=16 << 20),
        name="final",
    )(where, vel, inner, told)


def shift_up(block, axis):
    count = lax.axis_size(axis)
    return lax.ppermute(block, axis, [(i, i + 1) for i in range(count - 1)])


def shift_down(block, axis):
    count = lax.axis_size(axis)
    return lax.ppermute(block, axis, [(i + 1, i) for i in range(count - 1)])


def neighbours(block, axis):
    count, me = lax.axis_size(axis), lax.axis_index(axis)
    if count == 2:
        return lax.ppermute(block, axis, [(0, 1), (1, 0)])[None], 0, 0
    if count > 4:
        return jnp.stack([shift_up(block, axis), shift_down(block, axis)]), 0, 1
    stacked = lax.all_gather(block, axis, axis=0)
    return stacked, jnp.maximum(me - 1, 0), jnp.minimum(me + 1, count - 1)


def shards(trial, mean, cons, vel, wt, cell, flag, count, por, perm):
    por = por.reshape(CELLS, COLS)
    perm = perm.reshape(CELLS, COLS)
    points = point_args(trial, mean, cons, vel, wt, cell, flag, count)
    near, low, high = near_sums(points, por, perm)
    above = shift_down(low, "gx")
    below = shift_up(high, "gx")

    def ends(axis):
        me = lax.axis_index(axis)
        return [(me > 0).astype(i32), (me < lax.axis_size(axis) - 1).astype(i32)]

    has = ends("gx") + ends("gy")
    sums, own = assemble(near, far_sums(points), por, perm)
    packs, y_low, y_high = neighbours(with_rims(own, below, above), "gy")
    where = jnp.stack(
        [jnp.asarray(v, i32) for v in [y_low, y_high] + has + [lax.axis_index("gz")]]
    )
    rim, parts, edges = partial_sums(where, sums, por, perm, below, above)
    star, inner, told = local_solve(where, sums, por, perm, rim, parts, edges, packs)
    velocity, pressure = final(where, star, inner, lax.all_gather(told, "gz", axis=0))
    return (
        velocity.reshape(3, LEVELS, ROWS, COLS),
        pressure.reshape(LEVELS, ROWS, COLS),
    )


def solution(mesh):
    points = ("gx", "gy", "gz")
    cells = P("gz", "gx", "gy")
    placed = (
        P(None, points), P(points), P(points), P(None, points), P(points), P(points), P(points),
        P(*points), cells, cells,
    )
    return jax.shard_map(
        shards,
        mesh=mesh,
        in_specs=placed,
        out_specs=(P(None, *cells), cells),
        check_vma=False,
    )
```

```python
import functools

import jax
import jax.numpy as jnp
from jax import lax
from jax.experimental import pallas as pl
from jax.experimental.pallas import tpu as pltpu
from jax.sharding import PartitionSpec as P

bf = jnp.bfloat16
f8 = jnp.float8_e4m3fn
f32 = jnp.float32
i32 = jnp.int32

LEVELS, ROWS, COLS = 16, 8, 128
CELLS = LEVELS * ROWS

ZX, YZ, ZZ, XX, YY, XY, MX, MY, MZ, MASS, POR, PERM = range(12)
FIELDS = 12
STRESS_ORDER = (5, 4, 2, 0, 1, 3)

X_ROWS = (
    (ZX, 0), (ZX, 1), (YZ, 0), (ZZ, 0), (PERM, 0), (POR, 0),
    (XX, 0), (XX, 1), (XX, 2), (XY, 0), (XY, 1), (YY, 0),
    (MX, 0), (MX, 1), (MY, 0), (MZ, 0), (MASS, 0), (MASS, 1),
)
X_DEEP = 3
X_SENT = len(X_ROWS) + X_DEEP
Y_DEPTH = {ZX: 1, YZ: 2, ZZ: 1, XX: 1, YY: 3, XY: 2, MX: 1, MY: 2, MZ: 1, MASS: 2, POR: 1, PERM: 1}
Y_PLACE = {}
_at = 0
for _f in range(FIELDS):
    Y_PLACE[_f] = _at + Y_DEPTH[_f]
    _at += 2 * Y_DEPTH[_f]
HALF = 64
FACE, MAIN, NEAR, RIGHT, SOURCE, ECHO, VELZ, STRESSZ, FAR = range(9)
WEIGHT, SHEARX, SHEARY = range(3)
NARROW, WIDE = 17, 6
MSG_X = 8 * (NARROW + WIDE)
MSG_X_WIDE = MSG_X + 8 * -(-NARROW // 4)
MSG_Y = MSG_X_WIDE + 8 * -(-WIDE // 2)
MSG_ROWS = MSG_Y + 8
LANE_WIDE = 2 * NARROW
LANE_CORNER = LANE_WIDE + 4 * WIDE


def tile_iota(dim):
    return lax.broadcasted_iota(i32, (ROWS, COLS), dim)


def turn(tile, shift, axis):
    shift %= tile.shape[axis]
    return tile if shift == 0 else pltpu.roll(tile, shift, axis)


def row_stress(trial, mean, cons, flag):
    part = lax.broadcasted_iota(i32, trial.shape, 0)
    size = jnp.sqrt(
        jnp.sum(trial * trial * jnp.where(part < 3, 1.5, 3.0), axis=0, keepdims=True)
    )
    yield_size = 1.2 * jnp.sqrt(mean * (cons - mean))
    factor = jnp.where(flag == 1, yield_size / jnp.maximum(size, 1.0), 1.0)
    return trial * factor - jnp.where(part < 3, mean, 0.0)


def point_rows(trial, mean, cons, vel, wt, flag, live):
    weight = jnp.where(live, wt, 0.0)
    stress = row_stress(trial, mean, cons, flag) * weight
    momentum = vel * weight
    rows = [stress[i : i + 1] for i in STRESS_ORDER]
    return rows + [momentum[i : i + 1] for i in range(3)] + [weight]


def cell_products(rows, place, groups):
    chunk = place.shape[1]
    row = (place >> 7) & (ROWS - 1)
    deep = jnp.where(row < ROWS // 2, row, ROWS - 1 - row)
    hi = deep * 16 + (row >> 2) * 8 + ((place >> 10) & 7)
    lo = ((place >> 13) << 7) | (place & (COLS - 1))

    def spread(row):
        return jnp.broadcast_to(row, (16, chunk)).astype(bf)

    one, zero = jnp.array(1, bf), jnp.array(0, bf)
    base = lax.broadcasted_iota(i32, (16, chunk), 0)

    def equal(index, count):
        index = spread(index.astype(f32))
        return [(base + b * 16).astype(f32).astype(bf) == index for b in range(count // 16)]

    mask = equal(hi, 64)
    right = jnp.concatenate([jnp.where(m, one, zero) for m in equal(lo, 256)], axis=0)
    tops = [row.astype(bf).astype(f32) for row in rows]
    parts = [spread(top) for top in tops]
    rests = [spread((row - top) * 256.0) for row, top in zip(rows, tops)]
    left = jnp.concatenate([jnp.where(mask[d], parts[f], zero) for f, d in groups], axis=0)
    left8 = jnp.concatenate([jnp.where(mask[d], rests[f], zero) for f, d in groups], axis=0)
    dims = (((1,), (1,)), ((), ()))
    prod = lax.dot_general(left, right, dims, preferred_element_type=f32)
    prod8 = lax.dot_general(
        left8.astype(f8), right.astype(f8), dims, preferred_element_type=f32
    )
    return prod + prod8 * (1 / 256.0)


POINT_ARGS = 8


def group_sums(chunk, groups, args, acc, arrived=lambda c: None):
    trial, mean, cons, vel, wt, cell, flag, count = args[:POINT_ARGS]

    def step(c, carry):
        arrived(c)
        at = pl.ds(pl.multiple_of(c * chunk, chunk), chunk)
        slot = c * chunk + lax.broadcasted_iota(i32, (1, chunk), 1)
        live = slot < count[0]
        rows = point_rows(
            trial[:, at], mean[:, at], cons[:, at], vel[:, at], wt[:, at], flag[:, at], live
        )
        prod = cell_products(rows, cell[:, at], groups)

        @pl.when(c == 0)
        def _():
            acc[...] = prod

        @pl.when(c > 0)
        def _():
            acc[...] += prod

        return carry

    lax.fori_loop(0, cell.shape[1] // chunk, step, 0)


def copied_sums(chunk, groups, sources, scratch, acc, sems):
    chunks = sources[1].shape[1] // chunk
    points = range(POINT_ARGS - 1)

    def copy(n, c):
        if n in points:
            at = pl.ds(pl.multiple_of(c * chunk, chunk), chunk)
            return pltpu.make_async_copy(sources[n].at[:, at], scratch[n].at[:, at], sems.at[n, c])
        return pltpu.make_async_copy(sources[n], scratch[n], sems.at[n, 0])

    others = range(POINT_ARGS, len(sources))
    copy(7, 0).start()
    for c in range(chunks):
        for n in points:
            copy(n, c).start()
    for n in others:
        copy(n, 0).start()
    copy(7, 0).wait()

    def arrived(c):
        for n in points:
            copy(n, c).wait()

    group_sums(chunk, groups, scratch, acc, arrived)
    for n in others:
        copy(n, 0).wait()


NEAR_GROUPS = tuple(x for x in X_ROWS if x[0] < 10)
FAR_GROUPS = tuple(
    (f, d) for f in range(10) for d in range(ROWS // 2) if (f, d) not in NEAR_GROUPS
)
HALVES = ((0, 0), (1, COLS))


def near_kernel(chunk, *refs):
    sources, (acc, low, high), scratch, sems = refs[:10], refs[10:13], refs[13:23], refs[23]
    copied_sums(chunk, NEAR_GROUPS, sources, scratch, acc, sems)
    por, perm = scratch[POINT_ARGS:]
    lane = lax.broadcasted_iota(i32, (LEVELS, COLS), 1)
    packed = [[jnp.zeros((LEVELS, COLS), f32)] * X_DEEP for _ in range(2)]
    for q, (field, deep) in enumerate(X_ROWS):
        at, depth = Y_PLACE[field] + HALF, Y_DEPTH[field]
        mask = (lane >= at - depth) & (lane < at + depth)
        for side, row in ((0, deep), (1, ROWS - 1 - deep)):
            face = (low, high)[side]
            if field < 10:
                first = NEAR_GROUPS.index((field, deep)) * 16 + side * 8
                for half, col in HALVES:
                    face[q, 8 * half : 8 * half + 8, :] = acc[first : first + 8, col : col + COLS]
            else:
                face[q] = (por if field == POR else perm)[pl.ds(row, LEVELS, stride=ROWS), :]
            packed[side][deep] = jnp.where(mask, turn(face[q], at, 1), packed[side][deep])
    for deep in range(X_DEEP):
        low[len(X_ROWS) + deep] = packed[0][deep]
        high[len(X_ROWS) + X_DEEP - 1 - deep] = packed[1][deep]


def far_kernel(chunk, *refs):
    args, acc = refs[:POINT_ARGS], refs[POINT_ARGS]
    group_sums(chunk, FAR_GROUPS, args, acc)


def assemble_kernel(near, far, por, perm, out, own):
    for groups, values in ((NEAR_GROUPS, near), (FAR_GROUPS, far)):
        for n, (field, deep) in enumerate(groups):
            for side, row in ((0, deep), (1, ROWS - 1 - deep)):
                first = n * 16 + side * 8
                for half, col in HALVES:
                    rows = pl.ds(half * (CELLS // 2) + row, LEVELS // 2, stride=ROWS)
                    out[field, rows, :] = values[first : first + 8, col : col + COLS]
    lane = lax.broadcasted_iota(i32, (CELLS, COLS), 1)
    packed = jnp.zeros((CELLS, COLS), f32)
    for field in range(FIELDS):
        at, depth = Y_PLACE[field], Y_DEPTH[field]
        values = out[field] if field < 10 else (por if field == POR else perm)[...]
        mask = (lane >= at - depth) & (lane < at + depth)
        packed = jnp.where(mask, turn(values, at, 1), packed)
    own[...] = packed


def assemble(near, far, por, perm):
    return pl.pallas_call(
        assemble_kernel,
        out_shape=[
            jax.ShapeDtypeStruct((10, CELLS, COLS), f32),
            jax.ShapeDtypeStruct((CELLS, COLS), f32),
        ],
        compiler_params=pltpu.CompilerParams(vmem_limit_bytes=8 << 20),
        cost_estimate=pl.CostEstimate(flops=4000000, bytes_accessed=1500000, transcendentals=0),
        name="assemble",
    )(near, far, por, perm)


def group_call(kernel, groups, args, outs, copied, scratch, grant, name):
    points = args[1].shape[1]
    chunk = points // 2 if points % 256 == 0 else points
    if copied:
        scratch = [pltpu.VMEM(v.shape, v.dtype) for v in args] + scratch
        scratch = scratch + [pltpu.SemaphoreType.DMA((len(args), points // chunk))]
    space = pltpu.HBM if copied else pltpu.VMEM
    return pl.pallas_call(
        functools.partial(kernel, chunk),
        in_specs=[pl.BlockSpec(memory_space=space)] * len(args),
        out_shape=[jax.ShapeDtypeStruct(shape, f32) for shape in outs],
        scratch_shapes=scratch,
        compiler_params=pltpu.CompilerParams(vmem_limit_bytes=grant << 20),
        cost_estimate=pl.CostEstimate(
            flops=2 * 24 * len(groups) * 256 * points, bytes_accessed=64 * points, transcendentals=0
        ),
        name=name,
    )(*args)


def point_args(trial, mean, cons, vel, wt, cell, flag, count):
    row = lambda v: v.reshape(1, -1)
    return (trial, row(mean), row(cons), vel, row(wt), row(cell), row(flag), count)


def near_sums(points, por, perm):
    acc = (16 * len(NEAR_GROUPS), 2 * COLS)
    faces = (X_SENT, LEVELS, COLS)
    outs = [acc, faces, faces]
    args = (*points, por, perm)
    return group_call(near_kernel, NEAR_GROUPS, args, outs, True, [], 56, "near_sums")


def far_sums(points):
    outs = [(16 * len(FAR_GROUPS), 2 * COLS)]
    return group_call(far_kernel, FAR_GROUPS, points, outs, False, [], 44, "far_sums")[0]


def with_rims(own, below, above):
    rows = X_DEEP * LEVELS
    first = above[len(X_ROWS) :].reshape(rows, COLS)
    last = below[len(X_ROWS) :].reshape(rows, COLS)
    return own + jnp.concatenate([first, jnp.zeros((CELLS - 2 * rows, COLS), f32), last])


def y_from_above(shape):
    lane = lax.broadcasted_iota(i32, shape, 1) & (HALF - 1)
    mask = lane < 0
    for field in range(FIELDS):
        at = Y_PLACE[field]
        mask |= (lane >= at) & (lane < at + Y_DEPTH[field])
    return mask


Y_LOW, Y_HIGH, X_HAS_LOW, X_HAS_HIGH, Y_HAS_LOW, Y_HAS_HIGH, LAYER = range(7)


def met(where, packs, from_above, rows):
    low = packs[where[Y_LOW], rows, :] * where[Y_HAS_LOW].astype(f32)
    high = packs[where[Y_HIGH], rows, :] * where[Y_HAS_HIGH].astype(f32)
    return jnp.where(from_above, high, low)


def diff_x(own, rim):
    row = tile_iota(0)
    own_up, rim_up = turn(own, -1, 0), turn(rim, -1, 0)
    own_down, rim_down = turn(own, 1, 0), turn(rim, 1, 0)
    top, bottom = row == ROWS - 1, row == 0
    return (
        jnp.where(top, rim_up, own_up) - jnp.where(bottom, rim_down, own_down),
        jnp.where(top, own_up, rim_up) - jnp.where(bottom, own_down, rim_down),
    )


def diff_y(own, rim):
    lane = tile_iota(1)
    own_up, rim_up = turn(own, -1, 1), turn(rim, -1, 1)
    own_down, rim_down = turn(own, 1, 1), turn(rim, 1, 1)
    top, bottom = lane == COLS - 1, lane == 0
    return (
        jnp.where(top, rim_up, own_up) - jnp.where(bottom, rim_down, own_down),
        jnp.where(top, own_up, rim_up) - jnp.where(bottom, own_down, rim_down),
    )


def ext_x(t):
    a0, a1 = diff_x(t[0], t[1])
    b0, b1 = diff_x(t[2], t[3])
    return [a0, a1, b0, b1]


def ext_y(t):
    a0, a2 = diff_y(t[0], t[2])
    b1, b3 = diff_y(t[1], t[3])
    return [a0, b1, a2, b3]


def rim_masks(where):
    row, lane = tile_iota(0), tile_iota(1)
    has = lambda low, high, test: jnp.where(test, where[high], where[low]) == 1
    in_x = has(X_HAS_LOW, X_HAS_HIGH, row < 4)
    in_y = has(Y_HAS_LOW, Y_HAS_HIGH, lane < HALF)
    return in_x, in_y, in_x & in_y


def partial_kernel(where, sums, por, perm, below, above, rim, parts, edges):
    rim[...] = jnp.zeros_like(rim)
    for q, (field, deep) in enumerate(X_ROWS):
        rim[field, pl.ds(deep, LEVELS, stride=ROWS), :] = above[q]
        rim[field, pl.ds(ROWS - 1 - deep, LEVELS, stride=ROWS), :] = below[q]
    in_x = rim_masks(where)[0]
    lane = tile_iota(1)
    zero = jnp.zeros((ROWS, COLS), f32)

    def get(field, level):
        if not 0 <= level < LEVELS:
            return [zero] * 2
        rows = pl.ds(level * ROWS, ROWS)
        return [sums[field, rows, :], rim[field, rows, :]]

    for level in range(LEVELS):
        rows = pl.ds(level * ROWS, ROWS)
        mass = get(MASS, level)
        parts[3, 0, rows, :] = 0.125 / jnp.maximum(mass[0], 0.5)
        parts[3, 1, rows, :] = jnp.where(in_x, 0.125 / jnp.maximum(mass[1], 0.5), 0.0)
        for n, (field, fx, fy, fz) in enumerate(
            ((MX, XX, XY, ZX), (MY, XY, YY, YZ), (MZ, ZX, YZ, ZZ))
        ):
            in_rows = diff_x(*get(fx, level))
            higher, lower, momentum = get(fz, level + 1), get(fz, level - 1), get(field, level)
            for t, tile in enumerate(get(fy, level)):
                up, down = turn(tile, -1, 1), turn(tile, 1, 1)
                edges[n, t, rows, :] = jnp.where(lane == COLS - 1, up, down)
                in_lanes = jnp.where(lane == COLS - 1, 0.0, up) - jnp.where(lane == 0, 0.0, down)
                parts[n, t, rows, :] = (
                    8.0 * momentum[t] + in_rows[t] + in_lanes + (higher[t] - lower[t])
                )


def partial_sums(where, sums, por, perm, below, above):
    smem = pl.BlockSpec(memory_space=pltpu.SMEM)
    vmem = pl.BlockSpec(memory_space=pltpu.VMEM)
    return pl.pallas_call(
        partial_kernel,
        in_specs=[smem] + [vmem] * 5,
        out_shape=[
            jax.ShapeDtypeStruct((FIELDS, CELLS, COLS), f32),
            jax.ShapeDtypeStruct((4, 2, CELLS, COLS), f32),
            jax.ShapeDtypeStruct((3, 2, CELLS, COLS), f32),
        ],
        compiler_params=pltpu.CompilerParams(vmem_limit_bytes=16 << 20),
        cost_estimate=pl.CostEstimate(flops=8000000, bytes_accessed=3000000, transcendentals=0),
        name="partial_sums",
    )(where, sums, por, perm, below, above)


def local_kernel(where, sums, por, perm, rim, parts, edges, packs, vel, inner, out, corner):
    from_above = y_from_above((LEVELS, COLS))
    for slot in range(ROWS):
        rows = pl.ds(slot * LEVELS, LEVELS)
        corner[pl.ds(slot, LEVELS, stride=ROWS), :] = met(where, packs, from_above, rows)
    from_above = y_from_above((ROWS, COLS))
    in_x, in_y, in_xy = rim_masks(where)
    in_rims = (in_x, in_y, in_xy)
    zero = jnp.zeros((ROWS, COLS), f32)

    def field_at(field, level):
        rows = pl.ds(level * ROWS, ROWS)
        at = Y_PLACE[field]
        own = sums[field, rows, :] if field < 10 else (por if field == POR else perm)[rows, :]
        if level not in merged:
            merged[level] = met(where, packs, from_above, rows)
        lanes = merged[level]
        return [
            own,
            rim[field, rows, :],
            turn(lanes, -at, 1),
            turn(corner[rows, :], -at - HALF, 1),
        ]

    memo, merged = {}, {}

    def get(field, level):
        if not 0 <= level < LEVELS:
            return [zero] * 4
        if (field, level) not in memo:
            memo[field, level] = field_at(field, level)
        return memo[field, level]

    lanes = tile_iota(1)
    first_lane, last_lane = lanes == 0, lanes == COLS - 1

    def star(level):
        rows = pl.ds(level * ROWS, ROWS)
        weight = [0.125 / jnp.maximum(m, 0.5) for m in get(MASS, level)[2:]]
        weight = [jnp.where(m, w, 0.0) for m, w in zip(in_rims[1:], weight)]
        weight = [parts[3, 0, rows, :], parts[3, 1, rows, :]] + weight
        found = []
        for n, (field, fx, fy, fz) in enumerate(
            ((MX, XX, XY, ZX), (MY, XY, YY, YZ), (MZ, ZX, YZ, ZZ))
        ):
            in_rows = diff_x(*get(fx, level)[2:])
            higher, lower = get(fz, level + 1)[2:], get(fz, level - 1)[2:]
            momentum = get(field, level)[2:]
            own, outer = [], []
            for t, packed in enumerate((merged[level], corner[rows, :])):
                at = Y_PLACE[fy] + HALF * t
                up, down = turn(packed, -at - 1, 1), turn(packed, 1 - at, 1)
                beside = edges[n, t, rows, :]
                reach = jnp.where(last_lane, up, 0.0) - jnp.where(first_lane, down, 0.0)
                own.append((parts[n, t, rows, :] + reach) * weight[t])
                in_lanes = jnp.where(last_lane, beside, up) - jnp.where(first_lane, beside, down)
                total = 8.0 * momentum[t] + in_rows[t] + in_lanes + (higher[t] - lower[t])
                outer.append(total * weight[2 + t])
            found.append(own + outer)
        return found, weight

    def level_perm(level):
        own, x, y, _ = get(PERM, level)
        return [own] + [jnp.where(t > 0.0, t, 1.0) for t in (x, y)]

    def faces(level):
        pairs = zip(level_perm(level), level_perm(level + 1))
        return [0.5 * a * b / (a + b) for a, b in pairs]

    zero3 = [zero] * 3
    stars, weights = {}, {}
    stars[0], weights[0] = star(0)
    first_star = stars[0][2]
    wide = {0: [weights[0], get(ZX, 0), get(YZ, 0)]}
    stress = {0: get(ZZ, 0)}
    down = zero3
    kept, terms, sources, links = [], {}, {}, {}
    for level in range(LEVELS):
        if level + 1 < LEVELS:
            stars[level + 1], weights[level + 1] = star(level + 1)
        vx, vy, vz = stars[level]
        for n, part in enumerate((vx, vy, vz)):
            vel[n, pl.ds(level * ROWS, ROWS), :] = part[0]
        z_up = stars[level + 1][2] if level + 1 < LEVELS else zero3
        z_down = stars[level - 1][2] if level > 0 else zero3
        if level == LEVELS - 1:
            wide[1] = [weights[level], get(ZX, level), get(YZ, level)]
            stress[1] = get(ZZ, level)
        dx, dy = ext_x(vx), ext_y(vy)
        porosity = get(POR, level)[:3]
        up = faces(level) if level + 1 < LEVELS else zero3
        now = []
        for n in range(3):
            source = -0.0015 * (1.0 - porosity[n])
            right = source * (dx[n] + dy[n] + (z_up[n] - z_down[n]))
            main = 0.002 * porosity[n] + (down[n] + up[n])
            now.append((-down[n], main, -up[n], right, source))
        sources[level], links[level] = [t[4] for t in now], up
        down = up
        if level in (0, LEVELS - 1):
            terms[level] = now
        elif level == 1:
            kept.append([(lo, 1.0 / mid, hi, r) for lo, mid, hi, r, _ in now])
        else:
            rows = []
            for (lo, mid, hi, r, _), (f, inv, u, pr) in zip(now, kept[-1]):
                w = lo * inv
                rows.append((-w * f, 1.0 / (mid - w * u), hi, r - w * pr))
            kept.append(rows)
        for key in [k for k in memo if k[1] < level]:
            del memo[key]
    after = last_inner = None
    for n_row in range(len(kept) - 1, -1, -1):
        rows = []
        for t in range(3):
            f, inv, u, r = kept[n_row][t]
            if after is None:
                rows.append((r * inv, -f * inv, -u * inv))
            else:
                b2, f2, g2 = after[t]
                rows.append(((r - u * b2) * inv, -(f + u * f2) * inv, -u * g2 * inv))
            for m in range(3):
                inner[t, m, n_row] = rows[t][m]
        last_inner = last_inner or rows
        after = rows
    first_inner = after
    top = LEVELS - 1
    narrow = []
    for t in range(3):
        _, mid, hi, r, source = terms[0][t]
        b, f, g = first_inner[t]
        echo = sources[1][t] * weights[0][t] / links[0][t]
        face = level_perm(0)[t]
        mine = [face, mid + hi * f, hi * f, r - hi * b, source, echo, first_star[t], stress[0][t], hi * g]
        lo, mid, _, r, source = terms[top][t]
        b, f, g = last_inner[t]
        echo = sources[top - 1][t] * weights[top][t] / links[top - 1][t]
        face = level_perm(top)[t]
        mine += [face, mid + lo * g, lo * g, r - lo * b, source, echo, stars[top][2][t], stress[1][t]]
        narrow.append(mine)
    row, lane = tile_iota(0), tile_iota(1)
    x_parts = [zero] * -(-NARROW // 4)
    x_wide = [zero] * -(-WIDE // 2)
    y_part = zero

    def between(index, at, count):
        return (index >= at) & (index < at + count)

    for q in range(NARROW):
        own, x, y = (narrow[t][q] for t in range(3))
        out[8 * q : 8 * q + 8, :] = own
        at = 2 * q % 8
        x_parts[q // 4] = jnp.where(between(row, at, 2), turn(x, at + 1, 0), x_parts[q // 4])
        y_part = jnp.where(between(lane, 2 * q, 2), turn(y, 2 * q + 1, 1), y_part)
    for m, (own, x, y, xy) in enumerate(wide[0] + wide[1]):
        at = 8 * (NARROW + m)
        out[at : at + 8, :] = own
        at = 4 * (m % 2)
        x_wide[m // 2] = jnp.where(between(row, at, 4), turn(x, at + 2, 0), x_wide[m // 2])
        at = LANE_WIDE + 4 * m
        y_part = jnp.where(between(lane, at, 4), turn(y, at + 2, 1), y_part)
        at = LANE_CORNER + 2 * m
        y_part = jnp.where(between(lane, at, 2), turn(xy, at + 1, 1), y_part)
    for n, part in enumerate(x_parts):
        out[MSG_X + 8 * n : MSG_X + 8 * n + 8, :] = part
    for n, part in enumerate(x_wide):
        out[MSG_X_WIDE + 8 * n : MSG_X_WIDE + 8 * n + 8, :] = part
    out[MSG_Y : MSG_Y + 8, :] = y_part


def local_solve(where, sums, por, perm, rim, parts, edges, packs):
    smem = pl.BlockSpec(memory_space=pltpu.SMEM)
    vmem = pl.BlockSpec(memory_space=pltpu.VMEM)
    return pl.pallas_call(
        local_kernel,
        in_specs=[smem] + [vmem] * 7,
        out_shape=[
            jax.ShapeDtypeStruct((3, CELLS, COLS), f32),
            jax.ShapeDtypeStruct((3, 3, LEVELS - 2, ROWS, COLS), f32),
            jax.ShapeDtypeStruct((MSG_ROWS, COLS), f32),
        ],
        scratch_shapes=[pltpu.VMEM((CELLS, COLS), f32)],
        compiler_params=pltpu.CompilerParams(vmem_limit_bytes=16 << 20),
        name="local_solve",
    )(where, sums, por, perm, rim, parts, edges, packs)


def final_kernel(layers, where, vel, inner, told, out, pressure):
    me = where[LAYER]
    zero = jnp.zeros((ROWS, COLS), f32)

    def narrow(k, side, what):
        q = 9 * side + what
        at = MSG_X + 8 * (q // 4)
        return [
            told[k, 8 * q : 8 * q + 8, :],
            turn(told[k, at : at + 8, :], -(2 * q % 8 + 1), 0),
            turn(told[k, MSG_Y : MSG_Y + 8, :], -(2 * q + 1), 1),
        ]

    def wide(k, side, what):
        m = 3 * side + what
        own = 8 * (NARROW + m)
        at = MSG_X_WIDE + 8 * (m // 2)
        lanes = told[k, MSG_Y : MSG_Y + 8, :]
        return [
            told[k, own : own + 8, :],
            turn(told[k, at : at + 8, :], -(4 * (m % 2) + 2), 0),
            turn(lanes, -(LANE_WIDE + 4 * m + 2), 1),
            turn(lanes, -(LANE_CORNER + 2 * m + 1), 1),
        ]

    def times(*factors):
        product = factors[0]
        for factor in factors[1:]:
            product = [a * b for a, b in zip(product, factor)]
        return product

    def plus(*terms):
        total = terms[0]
        for term in terms[1:]:
            total = [a + b for a, b in zip(total, term)]
        return total

    def minus(a, b):
        return [x - y for x, y in zip(a, b)]

    def half_face(a, b):
        return [0.5 * x * y / (x + y) for x, y in zip(a, b)]

    rows, gains, echoes = [], [], []
    for k in range(layers):
        gain, echo = [], []
        sides = []
        for side, other in ((0, k - 1), (1, k + 1)):
            right = narrow(k, side, RIGHT)
            main = narrow(k, side, MAIN)
            if 0 <= other < layers:
                weight = wide(k, side, WEIGHT)
                sign = -1.0 if side == 0 else 1.0
                weight = [sign * w for w in weight]
                stress = narrow(other, 1 - side, STRESSZ)
                vx = times(weight, wide(other, 1 - side, SHEARX))
                vy = times(weight, wide(other, 1 - side, SHEARY))
                vz = times(weight, stress)
                change = times(wide(other, 1 - side, WEIGHT), narrow(k, side, STRESSZ))
                beyond = minus(narrow(other, 1 - side, VELZ), [sign * c for c in change])
                spread = plus(ext_x(vx)[:3], ext_y(vy)[:3], [sign * v for v in beyond])
                right = plus(right, times(narrow(k, side, SOURCE), spread))
                link = half_face(narrow(k, side, FACE), narrow(other, 1 - side, FACE))
                main = plus(main, link)
                echo.append(times(narrow(k, side, ECHO), stress))
                gain.append((vx[0], vy[0], vz[0]))
            else:
                link = [zero] * 3
                if side == 1:
                    main = plus(main, [0.25 * v for v in narrow(k, side, FACE)])
                echo.append([zero] * 3)
                gain.append((zero, zero, zero))
            sides.append((link, main, right))
        for side, (link, main, right) in enumerate(sides):
            near, far = narrow(k, side, NEAR), narrow(k, 0, FAR)
            right = minus(right, plus(times(near, echo[side]), times(far, echo[1 - side])))
            inv = [1.0 / m for m in main]
            link = [-v * i for v, i in zip(link, inv)]
            far, right = times(far, inv), times(right, inv)
            rows.append((link, far, right) if side == 0 else (far, link, right))
        gains.append(gain)
        echoes.append(echo)
    done = []
    for n, (lo, hi, r) in enumerate(rows):
        if n == 0:
            done.append((hi, r))
            continue
        hs, rs = done[-1]
        inv = [1.0 / (1.0 - l * h) for l, h in zip(lo, hs)]
        done.append((times(hi, inv), times(minus(r, times(lo, rs)), inv)))
    ends = [None] * len(rows)
    ends[-1] = done[-1][1]
    for n in range(len(rows) - 2, -1, -1):
        hs, rs = done[n]
        ends[n] = minus(rs, times(hs, ends[n + 1]))

    def mine(values):
        chosen = values[0]
        for k in range(1, layers):
            chosen = [jnp.where(me == k, v, c) for v, c in zip(values[k], chosen)]
        return chosen

    first, last = mine(ends[0::2]), mine(ends[1::2])
    under = mine([[zero]] + [e[:1] for e in ends[1:-1:2]])[0]
    over = mine([e[:1] for e in ends[2::2]] + [[zero]])[0]
    first_seen = plus(first, mine([e[0] for e in echoes]))
    last_seen = plus(last, mine([e[1] for e in echoes]))
    gain = {0: mine([g[0] for g in gains]), LEVELS - 1: mine([g[1] for g in gains])}
    in_x, in_y, _ = rim_masks(where)

    def press(level):
        if level < 0:
            return [under]
        if level >= LEVELS:
            return [over]
        if level == 0:
            parts = first
        elif level == LEVELS - 1:
            parts = last
        else:
            parts = [
                inner[t, 0, level - 1]
                + inner[t, 1, level - 1] * first_seen[t]
                + inner[t, 2, level - 1] * last_seen[t]
                for t in range(3)
            ]
        return [parts[0], jnp.where(in_x, parts[1], 0.0), jnp.where(in_y, parts[2], 0.0)]

    before, now = press(-1), press(0)
    for level in range(LEVELS):
        after = press(level + 1)
        rows_at = pl.ds(level * ROWS, ROWS)
        pressure[rows_at, :] = now[0]
        grads = (
            diff_x(now[0], now[1])[0],
            diff_y(now[0], now[2])[0],
            after[0] - before[0],
        )
        for n in range(3):
            value = vel[n, rows_at, :] - 0.125 * grads[n]
            out[n, rows_at, :] = value + gain[level][n] if level in gain else value
        before, now = now, after


def final(where, vel, inner, told):
    smem = pl.BlockSpec(memory_space=pltpu.SMEM)
    vmem = pl.BlockSpec(memory_space=pltpu.VMEM)
    return pl.pallas_call(
        functools.partial(final_kernel, told.shape[0]),
        in_specs=[smem] + [vmem] * 3,
        out_shape=[
            jax.ShapeDtypeStruct((3, CELLS, COLS), f32),
            jax.ShapeDtypeStruct((CELLS, COLS), f32),
        ],
        compiler_params=pltpu.CompilerParams(vmem_limit_bytes=16 << 20),
        name="final",
    )(where, vel, inner, told)


def shift_up(block, axis):
    count = lax.axis_size(axis)
    return lax.ppermute(block, axis, [(i, i + 1) for i in range(count - 1)])


def shift_down(block, axis):
    count = lax.axis_size(axis)
    return lax.ppermute(block, axis, [(i + 1, i) for i in range(count - 1)])


def neighbours(block, axis):
    count, me = lax.axis_size(axis), lax.axis_index(axis)
    if count == 2:
        return lax.ppermute(block, axis, [(0, 1), (1, 0)])[None], 0, 0
    if count > 4:
        return jnp.stack([shift_up(block, axis), shift_down(block, axis)]), 0, 1
    stacked = lax.all_gather(block, axis, axis=0)
    return stacked, jnp.maximum(me - 1, 0), jnp.minimum(me + 1, count - 1)


def shards(trial, mean, cons, vel, wt, cell, flag, count, por, perm):
    por = por.reshape(CELLS, COLS)
    perm = perm.reshape(CELLS, COLS)
    points = point_args(trial, mean, cons, vel, wt, cell, flag, count)
    near, low, high = near_sums(points, por, perm)
    above = shift_down(low, "gx")
    below = shift_up(high, "gx")

    def ends(axis):
        me = lax.axis_index(axis)
        return [(me > 0).astype(i32), (me < lax.axis_size(axis) - 1).astype(i32)]

    has = ends("gx") + ends("gy")
    sums, own = assemble(near, far_sums(points), por, perm)
    packs, y_low, y_high = neighbours(with_rims(own, below, above), "gy")
    where = jnp.stack(
        [jnp.asarray(v, i32) for v in [y_low, y_high] + has + [lax.axis_index("gz")]]
    )
    rim, parts, edges = partial_sums(where, sums, por, perm, below, above)
    star, inner, told = local_solve(where, sums, por, perm, rim, parts, edges, packs)
    velocity, pressure = final(where, star, inner, lax.all_gather(told, "gz", axis=0))
    return (
        velocity.reshape(3, LEVELS, ROWS, COLS),
        pressure.reshape(LEVELS, ROWS, COLS),
    )


def solution(mesh):
    points = ("gx", "gy", "gz")
    cells = P("gz", "gx", "gy")
    placed = (
        P(None, points), P(points), P(points), P(None, points), P(points), P(points), P(points),
        P(*points), cells, cells,
    )
    return jax.shard_map(
        shards,
        mesh=mesh,
        in_specs=placed,
        out_specs=(P(None, *cells), cells),
        check_vma=False,
    )
```
